32 devices in a mesh: grid: 8 (over z, y), blk: 4 (over x, core).
Axes of the slice: x: 2, y: 2, z: 4, core: 2. Of those that a mesh axis runs over, the one named last changes fastest.
Arguments:
- a_slots: bfloat16 [8, 4, 8, 2, 128, 128], P('grid', 'blk'), may hold values from -6 to 6
- a_rows: int32 [8, 4, 8, 2], P('grid', 'blk'), may hold values from 0 to 63, as said below
- a_cols: int32 [8, 4, 8, 2], P('grid', 'blk'), may hold values from 0 to 31
- a_count: int32 [8, 4, 8], P('grid', 'blk'), may hold values from 0 to 2, as said below
- owned_rows: int32 [8, 8], P('grid'), may hold values from 0 to 63, as said below
- b_matrix: bfloat16 [4096, 4096], P('grid', 'blk'), may hold values from -0.1875 to 0.1875
Outputs:
- product: bfloat16 [8192, 4096], P('grid', 'blk')
The draws below stay inside these ranges and needn't reach their ends.
Inputs may be any that keep to these rules, and one draw needn't show every extreme that they name: `a_rows`: every slot sent to product owner g, live or padded, names one of the block rows owned_rows[g, 0 .. 7]; no two slots of the whole draw name the same block row and block column. `a_count`: some product owner receives 2 live slots from every atom owner and atom column. `owned_rows`: A permutation of the 64 block rows.
All inputs are finite; a program needn't handle non-finite values.
Results may differ from the reference program's by a relative error of at most 0.001.
Values may be sent and summed in bfloat16 or wider, within the bound.
No kernel may reach another device: no remote copies, remote signals or barrier semaphores. Data moves between devices by JAX's collectives and lax.ppermute only.
A program may use at most 128 MiB of HBM per device.

```python
import jax
import jax.numpy as jnp
from jax import lax

BS = 128
CAP = 2
RB = 8
KB = 4
NK = 32
NC = 32
N_GRID = 8
N_BLK = 4


def layout_tables(key):
    order = jax.random.permutation(jax.random.fold_in(key, 11), RB * N_GRID).astype(jnp.int32)
    owned = order.reshape(N_GRID, RB)
    place_keys = jax.random.split(jax.random.fold_in(key, 12), N_GRID)
    spots = jax.vmap(lambda one_key: jax.random.permutation(one_key, RB * KB * N_GRID))(place_keys)
    used = spots[:, :N_GRID * N_BLK * CAP].astype(jnp.int32)
    local_row = used // (KB * N_GRID)
    block_col = used % (KB * N_GRID)
    row_ids = jnp.take_along_axis(owned, local_row, axis=1)
    row_ids = row_ids.reshape(N_GRID, N_GRID, N_BLK, CAP).transpose(1, 2, 0, 3)
    col_ids = block_col.reshape(N_GRID, N_GRID, N_BLK, CAP).transpose(1, 2, 0, 3)
    counts = jax.random.randint(jax.random.fold_in(key, 13), (N_GRID, N_BLK, N_GRID), 0, CAP + 1)
    full_owner = jax.random.randint(jax.random.fold_in(key, 14), (), 0, N_GRID)
    owner_ids = jnp.arange(N_GRID)[None, None, :]
    counts = jnp.where(owner_ids == full_owner, CAP, counts)
    return (owned.astype(jnp.int32), row_ids.astype(jnp.int32), col_ids.astype(jnp.int32), counts.astype(jnp.int32))


def draw_a_rows(key, part):
    return layout_tables(key)[1]


def draw_a_cols(key, part):
    return layout_tables(key)[2]


def draw_a_count(key, part):
    return layout_tables(key)[3]


def draw_owned_rows(key, part):
    return layout_tables(key)[0]


def block_levels(own_key, shape, shards, least, top_value):
    def one(axis_at, shards_of):
        heights = jax.random.uniform(jax.random.fold_in(jax.random.fold_in(own_key, 6), axis_at), (shards_of,), jnp.float32, least / len(shards), top_value / len(shards))
        return jnp.repeat(jnp.exp(heights), shape[axis_at] // shards_of).reshape((-1,) + (1,) * (len(shape) - axis_at - 1))

    level = one(*shards[0])
    for cut in shards[1:]:
        level = level * one(*cut)
    return level


def centred(stream_key, dims, scale, bound, shards=(), kind=jnp.bfloat16):
    values = scale * jax.random.normal(stream_key, dims, jnp.float32)
    if shards:
        values = values * block_levels(stream_key, dims, shards, -0.22, 0.18)
    return jnp.clip(values, -bound, bound).astype(kind)


def setup_inputs(seed: int = 0) -> dict:
    seeds = jax.random.split(jax.random.key(seed), 7)
    a_slots = centred(seeds[0], (N_GRID, N_BLK, N_GRID, CAP, BS, BS), 1.0, 6.0, ((0, 8), (1, 4)))
    a_rows = draw_a_rows(jax.random.fold_in(seeds[6], 71), 0)
    a_cols = draw_a_cols(jax.random.fold_in(seeds[6], 71), 0)
    a_count = draw_a_count(jax.random.fold_in(seeds[6], 71), 0)
    owned_rows = draw_owned_rows(jax.random.fold_in(seeds[6], 71), 0)
    b_matrix = centred(seeds[5], (NK * BS, NC * BS), (KB * N_GRID * BS // 4) ** -0.5, 0.1875, ((0, 8), (1, 4)))
    return {"a_slots": a_slots, "a_rows": a_rows, "a_cols": a_cols, "a_count": a_count, "owned_rows": owned_rows, "b_matrix": b_matrix}


def reference(a_slots, a_rows, a_cols, a_count, owned_rows, b_matrix):
    k_blocks = KB * N_GRID
    live = jnp.arange(CAP, dtype=jnp.int32)[None, None, None, :] < a_count[..., None]

    def one_owner(owner):
        data = jnp.take(a_slots, owner, axis=2).reshape(-1, BS, BS)
        slot_rows = jnp.take(a_rows, owner, axis=2).reshape(-1)
        slot_cols = jnp.take(a_cols, owner, axis=2).reshape(-1)
        alive = jnp.take(live, owner, axis=2).reshape(-1)
        owned = jnp.take(owned_rows, owner, axis=0)
        match = slot_rows[:, None] == owned[None, :]
        local_row = jnp.argmax(match, axis=1).astype(jnp.int32)
        keep = alive & jnp.any(match, axis=1)
        values = jnp.where(keep[:, None, None], data.astype(jnp.float32), jnp.float32(0.0))
        tile = jnp.zeros((RB, k_blocks, BS, BS), jnp.float32).at[local_row, slot_cols].add(values)
        tile = tile.astype(jnp.bfloat16).transpose(0, 2, 1, 3).reshape(RB * BS, k_blocks * BS)
        return jnp.dot(tile, b_matrix, preferred_element_type=jnp.float32).astype(jnp.bfloat16)

    blocks = lax.map(one_owner, jnp.arange(N_GRID, dtype=jnp.int32))
    return blocks.reshape(N_GRID * RB * BS, NC * BS)
```

```python
import functools

import jax
import jax.numpy as jnp
import numpy as np
from jax import lax
from jax.experimental import pallas as pl
from jax.experimental.pallas import tpu as pltpu
from jax.sharding import PartitionSpec as P

META = 16


def ring_order(n):
    return list(range(0, n, 2)) + list(range(n - 1, 0, -2))


def build_kernel(n_parts, per_part, cap, bs, dest_ref, *refs):
    parts, tile_ref = refs[:n_parts], refs[n_parts]
    tile_ref[...] = jnp.zeros_like(tile_ref)
    k_blocks = tile_ref.shape[0] * 2
    for q in range(n_parts):
        part = parts[q]

        def place(i, carry):
            for c in range(cap):
                dest = dest_ref[q, i, c]

                @pl.when(dest >= 0)
                def _():
                    row = dest // k_blocks
                    col = dest % k_blocks
                    tile_ref[
                        col // 2,
                        pl.ds(pl.multiple_of(row * bs, bs), bs),
                        pl.ds(pl.multiple_of((col % 2) * bs, bs), bs),
                    ] = part[i, pl.ds(c * bs, bs), :]

            return carry

        lax.fori_loop(0, per_part, place, 0)


def build_tile(dest, parts, rows, k_blocks, bs, cap):
    n_parts, per_part = len(parts), parts[0].shape[0]
    return pl.pallas_call(
        functools.partial(build_kernel, n_parts, per_part, cap, bs),
        out_shape=jax.ShapeDtypeStruct((k_blocks // 2, rows, 2 * bs), jnp.bfloat16),
        in_specs=[pl.BlockSpec(memory_space=pltpu.SMEM)]
        + [pl.BlockSpec(memory_space=pltpu.VMEM)] * n_parts,
        out_specs=pl.BlockSpec(memory_space=pltpu.VMEM),
        compiler_params=pltpu.CompilerParams(vmem_limit_bytes=48 << 20),
        cost_estimate=pl.CostEstimate(
            flops=0, bytes_accessed=rows * k_blocks * bs * 4, transcendentals=0
        ),
    )(dest, *parts)


def mul_kernel(n_pieces, has_acc, idx_ref, *refs):
    tiles = refs[:n_pieces]
    pieces = refs[n_pieces : 2 * n_pieces]
    out_ref = refs[-1]
    total = refs[2 * n_pieces][...] if has_acc else None
    for tile, piece in zip(tiles, pieces):
        term = jnp.dot(tile[0], piece[...], preferred_element_type=jnp.float32)
        total = term if total is None else total + term
    out_ref[...] = total.astype(out_ref.dtype)


def mul(idx, tile, pieces, acc, out_dtype):
    n = len(pieces)
    rows = tile.shape[1]
    depth, cols = pieces[0].shape
    bm = 256
    in_specs = [
        pl.BlockSpec((1, bm, depth), functools.partial(lambda i, m, idx: (idx[i], m, 0), i))
        for i in range(n)
    ]
    in_specs += [pl.BlockSpec((depth, cols), lambda m, idx: (0, 0)) for _ in range(n)]
    args = [tile] * n + list(pieces)
    if acc is not None:
        in_specs.append(pl.BlockSpec((bm, cols), lambda m, idx: (m, 0)))
        args.append(acc)
    return pl.pallas_call(
        functools.partial(mul_kernel, n, acc is not None),
        out_shape=jax.ShapeDtypeStruct((rows, cols), out_dtype),
        grid_spec=pltpu.PrefetchScalarGridSpec(
            num_scalar_prefetch=1,
            grid=(rows // bm,),
            in_specs=in_specs,
            out_specs=pl.BlockSpec((bm, cols), lambda m, idx: (m, 0)),
        ),
        compiler_params=pltpu.CompilerParams(vmem_limit_bytes=56 << 20),
        cost_estimate=pl.CostEstimate(
            flops=2 * n * rows * depth * cols,
            bytes_accessed=n * (rows + cols) * depth * 2 + rows * cols * 8,
            transcendentals=0,
        ),
    )(idx, *args)


def body(a_slots, a_rows, a_cols, a_count, owned_rows, b_matrix):
    groups = lax.axis_size("grid")
    columns = lax.axis_size("blk")
    bs = a_slots.shape[-1]
    cap = a_slots.shape[3]
    rb = owned_rows.shape[-1]
    k_local = b_matrix.shape[0]
    k_blocks = k_local * groups // bs
    depth = 2 * bs
    me = lax.axis_index("grid")

    order = ring_order(groups)
    table = jnp.asarray(np.array(order, np.int32))
    place_of = jnp.asarray(np.argsort(np.array(order)).astype(np.int32))
    pos = place_of[me]
    to_right = [(order[i], order[(i + 1) % groups]) for i in range(groups)]
    to_left = [(order[(i + 1) % groups], order[i]) for i in range(groups)]

    per = k_local // depth
    own = [b_matrix[h * depth : (h + 1) * depth] for h in range(per)]
    events = [[(me * per + h, own[h]) for h in range(per)]]
    from_left, from_right = list(own), list(own)
    half = groups // 2
    for s in range(1, half + 1):
        low = range(per) if s < half else range(per // 2)
        high = range(per) if s < half else range(per // 2, per)
        from_left = {h: lax.ppermute(from_left[h], "grid", to_right) for h in low}
        from_right = {h: lax.ppermute(from_right[h], "grid", to_left) for h in high}
        left_owner = table[(pos - s + groups) % groups]
        right_owner = table[(pos + s) % groups]
        events.append(
            [(left_owner * per + h, from_left[h]) for h in low]
            + [(right_owner * per + h, from_right[h]) for h in high]
        )

    live = jnp.arange(cap, dtype=jnp.int32)[None, :] < a_count.reshape(groups, 1)
    row_code = jnp.where(live, a_rows.reshape(groups, cap) + 1, 0)
    meta = jnp.concatenate([row_code, a_cols.reshape(groups, cap)], axis=1)
    meta = jnp.pad(meta.astype(jnp.bfloat16)[:, None, :], ((0, 0), (0, META - 1), (0, bs - 2 * cap)))
    message = jnp.concatenate([a_slots.reshape(groups, cap * bs, bs), meta], axis=1)
    landed = lax.all_to_all(message, "grid", split_axis=0, concat_axis=0, tiled=True)
    if columns == 4:
        swap_core = [(j, j ^ 1) for j in range(columns)]
        swap_chip = [(j, j ^ 2) for j in range(columns)]
        across = lax.ppermute(landed, "blk", swap_chip)
        parts = [
            landed,
            across,
            lax.ppermute(landed, "blk", swap_core),
            lax.ppermute(across, "blk", swap_core),
        ]
    else:
        gathered = lax.all_gather(landed, "blk", axis=0)
        parts = [gathered[j] for j in range(columns)]
    metas = jnp.stack([p[:, cap * bs, : 2 * cap] for p in parts]).astype(jnp.int32)
    owned = owned_rows.reshape(rb)
    hit = metas[..., :cap, None] == owned + 1
    local_row = jnp.sum(jnp.where(hit, jnp.arange(rb, dtype=jnp.int32), 0), axis=-1)
    dest = jnp.where(jnp.any(hit, axis=-1), local_row * k_blocks + metas[..., cap:], -1)
    tile = build_tile(dest, parts, rb * bs, k_blocks, bs, cap)

    acc = None
    early = sum(events[: half - 1], [])
    stages = [early] + events[half - 1 :]
    for t, stage in enumerate(stages):
        idx = jnp.stack([k for k, _ in stage]).astype(jnp.int32)
        last = t == len(stages) - 1
        acc = mul(idx, tile, [p for _, p in stage], acc, jnp.bfloat16 if last else jnp.float32)
    return acc


def solution(mesh):
    in_specs = (
        P("grid", "blk", None, None, None, None),
        P("grid", "blk", None, None),
        P("grid", "blk", None, None),
        P("grid", "blk", None),
        P("grid", None),
        P("grid", "blk"),
    )
    out_specs = P("grid", "blk")
    return jax.shard_map(body, mesh=mesh, in_specs=in_specs, out_specs=out_specs, check_vma=False)
```

```python
import functools

import jax
import jax.numpy as jnp
from jax import lax
from jax.experimental import pallas as pl
from jax.experimental.pallas import tpu as pltpu
from jax.sharding import PartitionSpec as P

META = 16


def ring_order(n):
    return list(range(0, n, 2)) + list(range(n - 1, 0, -2))


def ring_place(g, n):
    return jnp.where(g % 2 == 0, g // 2, n - 1 - g // 2)


def build_kernel(dims, bounds, pos_ref, owned_ref, *refs):
    n_parts, per_part, cap, bs, groups, blocks = dims
    metas, parts = refs[:n_parts], refs[n_parts : 2 * n_parts]
    tiles = refs[2 * n_parts :]
    for tile in tiles:
        tile[...] = jnp.zeros_like(tile)
    half, per = groups // 2, blocks // 2
    for meta, part in zip(metas, parts):

        def place(i, carry):
            for c in range(cap):
                code, col = meta[i, c], meta[i, cap + c]
                row, found = jnp.int32(0), jnp.int32(0)
                for r in range(owned_ref.shape[0]):
                    hit = owned_ref[r] + 1 == code
                    row = jnp.where(hit, r, row)
                    found = jnp.where(hit, 1, found)
                owner, local = col // blocks, col % blocks
                ahead = lax.rem(ring_place(owner, groups) - pos_ref[0] + groups, groups)
                hops = jnp.minimum(ahead, groups - ahead)
                first = jnp.where(hops == 0, 0, per * (2 * hops - 1))
                first += jnp.where((ahead > 0) & (ahead < half), per, 0)
                piece = first + local // 2
                for (low, high), tile in zip(bounds, tiles):

                    @pl.when((found == 1) & (piece >= low) & (piece < high))
                    def _():
                        at = ((piece - low) * 2 + local % 2) * bs
                        tile[
                            pl.ds(pl.multiple_of(row * bs, bs), bs),
                            pl.ds(pl.multiple_of(at, bs), bs),
                        ] = part[i, pl.ds(c * bs, bs), :]

            return carry

        lax.fori_loop(0, per_part, place, 0)


def build_tiles(pos, owned, metas, parts, dims, bounds, rows):
    n_parts, _, _, bs, groups, blocks = dims
    smem = pl.BlockSpec(memory_space=pltpu.SMEM)
    vmem = pl.BlockSpec(memory_space=pltpu.VMEM)
    return pl.pallas_call(
        functools.partial(build_kernel, dims, bounds),
        out_shape=[
            jax.ShapeDtypeStruct((rows, (high - low) * 2 * bs), jnp.bfloat16)
            for low, high in bounds
        ],
        in_specs=[smem] * (2 + n_parts) + [vmem] * n_parts,
        out_specs=[vmem] * len(bounds),
        compiler_params=pltpu.CompilerParams(vmem_limit_bytes=48 << 20),
        cost_estimate=pl.CostEstimate(
            flops=0, bytes_accessed=rows * groups * blocks * bs * 4, transcendentals=0
        ),
    )(pos, owned, *metas, *parts)


def mul_kernel(n_pieces, tile_ref, *refs):
    right = jnp.concatenate([piece[...] for piece in refs[:n_pieces]], axis=0)
    total = jnp.dot(tile_ref[...], right, preferred_element_type=jnp.float32)
    if len(refs) == n_pieces + 2:
        total += refs[n_pieces][...]
    refs[-1][...] = total.astype(refs[-1].dtype)


def mul(tile, pieces, acc, out_dtype):
    n = len(pieces)
    rows, inner = tile.shape
    depth, cols = pieces[0].shape
    bn = 256
    in_specs = [pl.BlockSpec((rows, inner), lambda j: (0, 0))]
    in_specs += [pl.BlockSpec((depth, bn), lambda j: (0, j)) for _ in range(n)]
    args = [tile, *pieces]
    if acc is not None:
        in_specs.append(pl.BlockSpec((rows, bn), lambda j: (0, j)))
        args.append(acc)
    return pl.pallas_call(
        functools.partial(mul_kernel, n),
        out_shape=jax.ShapeDtypeStruct((rows, cols), out_dtype),
        grid=(cols // bn,),
        in_specs=in_specs,
        out_specs=pl.BlockSpec((rows, bn), lambda j: (0, j)),
        compiler_params=pltpu.CompilerParams(vmem_limit_bytes=56 << 20),
        cost_estimate=pl.CostEstimate(
            flops=2 * rows * inner * cols,
            bytes_accessed=(rows + cols) * inner * 2 + rows * cols * 8,
            transcendentals=0,
        ),
    )(*args)


def body(a_slots, a_rows, a_cols, a_count, owned_rows, b_matrix):
    groups = lax.axis_size("grid")
    columns = lax.axis_size("blk")
    bs = a_slots.shape[-1]
    cap = a_slots.shape[3]
    rb = owned_rows.shape[-1]
    blocks = b_matrix.shape[0] // bs
    depth = 2 * bs
    per = blocks // 2
    half = groups // 2
    pos = ring_place(lax.axis_index("grid"), groups).reshape(1)

    order = ring_order(groups)
    to_right = [(order[i], order[(i + 1) % groups]) for i in range(groups)]
    to_left = [(order[(i + 1) % groups], order[i]) for i in range(groups)]

    own = [b_matrix[h * depth : (h + 1) * depth] for h in range(per)]
    events = [own]
    from_left, from_right = list(own), list(own)
    for s in range(1, half + 1):
        low = range(per) if s < half else range(per // 2)
        high = range(per) if s < half else range(per // 2, per)
        from_left = {h: lax.ppermute(from_left[h], "grid", to_right) for h in low}
        from_right = {h: lax.ppermute(from_right[h], "grid", to_left) for h in high}
        events.append([from_left[h] for h in low] + [from_right[h] for h in high])

    live = jnp.arange(cap, dtype=jnp.int32)[None, :] < a_count.reshape(groups, 1)
    row_code = jnp.where(live, a_rows.reshape(groups, cap) + 1, 0)
    meta = jnp.concatenate([row_code, a_cols.reshape(groups, cap)], axis=1)
    meta = jnp.pad(meta.astype(jnp.bfloat16)[:, None, :], ((0, 0), (0, META - 1), (0, bs - 2 * cap)))
    message = jnp.concatenate([a_slots.reshape(groups, cap * bs, bs), meta], axis=1)
    landed = lax.all_to_all(message, "grid", split_axis=0, concat_axis=0, tiled=True)
    if columns == 4:
        swap_core = [(j, j ^ 1) for j in range(columns)]
        swap_chip = [(j, j ^ 2) for j in range(columns)]
        across = lax.ppermute(landed, "blk", swap_chip)
        parts = [
            landed,
            across,
            lax.ppermute(landed, "blk", swap_core),
            lax.ppermute(across, "blk", swap_core),
        ]
    else:
        gathered = lax.all_gather(landed, "blk", axis=0)
        parts = [gathered[j] for j in range(columns)]
    metas = [p[:, cap * bs, : 2 * cap].astype(jnp.int32) for p in parts]

    stages = [sum(events[: half - 1], []), events[half - 1], events[half]]
    bounds, start = [], 0
    for stage in stages:
        bounds.append((start, start + len(stage)))
        start += len(stage)
    dims = (columns, groups, cap, bs, groups, blocks)
    tiles = build_tiles(pos, owned_rows.reshape(rb), metas, parts, dims, bounds, rb * bs)

    acc = None
    for t, (tile, stage) in enumerate(zip(tiles, stages)):
        acc = mul(tile, stage, acc, jnp.bfloat16 if t == len(stages) - 1 else jnp.float32)
    return acc


def solution(mesh):
    in_specs = (
        P("grid", "blk", None, None, None, None),
        P("grid", "blk", None, None),
        P("grid", "blk", None, None),
        P("grid", "blk", None),
        P("grid", None),
        P("grid", "blk"),
    )
    out_specs = P("grid", "blk")
    return jax.shard_map(body, mesh=mesh, in_specs=in_specs, out_specs=out_specs, check_vma=False)
```

```python
import functools

import jax
import jax.numpy as jnp
from jax import lax
from jax.experimental import pallas as pl
from jax.experimental.pallas import tpu as pltpu
from jax.sharding import PartitionSpec as P

META = 16


def ring_order(n):
    return list(range(0, n, 2)) + list(range(n - 1, 0, -2))


def ring_place(g, n):
    return jnp.where(g % 2 == 0, g // 2, n - 1 - g // 2)


def build_kernel(dims, bounds, pos_ref, owned_ref, *refs):
    n_parts, per_part, cap, bs, groups, blocks = dims
    metas, parts = refs[:n_parts], refs[n_parts : 2 * n_parts]
    tiles = refs[2 * n_parts :]
    for tile in tiles:
        tile[...] = jnp.zeros_like(tile)
    half, per = groups // 2, blocks // 2
    for meta, part in zip(metas, parts):

        def place(i, carry):
            for c in range(cap):
                code, col = meta[i, c], meta[i, cap + c]
                row, found = jnp.int32(0), jnp.int32(0)
                for r in range(owned_ref.shape[0]):
                    hit = owned_ref[r] + 1 == code
                    row = jnp.where(hit, r, row)
                    found = jnp.where(hit, 1, found)
                owner, local = col // blocks, col % blocks
                ahead = lax.rem(ring_place(owner, groups) - pos_ref[0] + groups, groups)
                hops = jnp.minimum(ahead, groups - ahead)
                first = jnp.where(hops == 0, 0, per * (2 * hops - 1))
                first += jnp.where((ahead > 0) & (ahead < half), per, 0)
                piece = first + local // 2
                for (low, high), tile in zip(bounds, tiles):

                    @pl.when((found == 1) & (piece >= low) & (piece < high))
                    def _():
                        at = ((piece - low) * 2 + local % 2) * bs
                        tile[
                            pl.ds(pl.multiple_of(row * bs, bs), bs),
                            pl.ds(pl.multiple_of(at, bs), bs),
                        ] = part[i, pl.ds(c * bs, bs), :]

            return carry

        lax.fori_loop(0, per_part, place, 0)


def build_tiles(pos, owned, metas, parts, dims, bounds, rows):
    n_parts, _, _, bs, groups, blocks = dims
    smem = pl.BlockSpec(memory_space=pltpu.SMEM)
    vmem = pl.BlockSpec(memory_space=pltpu.VMEM)
    return pl.pallas_call(
        functools.partial(build_kernel, dims, bounds),
        out_shape=[
            jax.ShapeDtypeStruct((rows, (high - low) * 2 * bs), jnp.bfloat16)
            for low, high in bounds
        ],
        in_specs=[smem] * (2 + n_parts) + [vmem] * n_parts,
        out_specs=[vmem] * len(bounds),
        compiler_params=pltpu.CompilerParams(vmem_limit_bytes=48 << 20),
        cost_estimate=pl.CostEstimate(
            flops=0, bytes_accessed=rows * groups * blocks * bs * 4, transcendentals=0
        ),
    )(pos, owned, *metas, *parts)


def after_kernel(*refs):
    pass


def after(values, others):
    anywhere = pl.BlockSpec(memory_space=pl.ANY)
    return pl.pallas_call(
        after_kernel,
        out_shape=[jax.ShapeDtypeStruct(v.shape, v.dtype) for v in values],
        in_specs=[anywhere] * (len(values) + len(others)),
        out_specs=[anywhere] * len(values),
        input_output_aliases={i: i for i in range(len(values))},
        cost_estimate=pl.CostEstimate(flops=0, bytes_accessed=0, transcendentals=0),
    )(*values, *others)


def mul_kernel(n_pieces, tile_ref, *refs):
    right = jnp.concatenate([piece[...] for piece in refs[:n_pieces]], axis=0)
    total = jnp.dot(tile_ref[...], right, preferred_element_type=jnp.float32)
    if len(refs) == n_pieces + 2:
        total += refs[n_pieces][...]
    refs[-1][...] = total.astype(refs[-1].dtype)


def mul(tile, pieces, acc, out_dtype):
    n = len(pieces)
    rows, inner = tile.shape
    depth, cols = pieces[0].shape
    bn = 256
    in_specs = [pl.BlockSpec((rows, inner), lambda j: (0, 0))]
    in_specs += [pl.BlockSpec((depth, bn), lambda j: (0, j)) for _ in range(n)]
    args = [tile, *pieces]
    if acc is not None:
        in_specs.append(pl.BlockSpec((rows, bn), lambda j: (0, j)))
        args.append(acc)
    return pl.pallas_call(
        functools.partial(mul_kernel, n),
        out_shape=jax.ShapeDtypeStruct((rows, cols), out_dtype),
        grid=(cols // bn,),
        in_specs=in_specs,
        out_specs=pl.BlockSpec((rows, bn), lambda j: (0, j)),
        compiler_params=pltpu.CompilerParams(vmem_limit_bytes=56 << 20),
        cost_estimate=pl.CostEstimate(
            flops=2 * rows * inner * cols,
            bytes_accessed=(rows + cols) * inner * 2 + rows * cols * 8,
            transcendentals=0,
        ),
    )(*args)


def across_row(landed, columns):
    if columns != 4:
        gathered = lax.all_gather(landed, "blk", axis=0)
        return [gathered[j] for j in range(columns)]
    swap_core = [(j, j ^ 1) for j in range(columns)]
    swap_chip = [(j, j ^ 2) for j in range(columns)]
    across = lax.ppermute(landed, "blk", swap_chip)
    near = lax.ppermute(landed, "blk", swap_core)
    return [landed, across, near, lax.ppermute(across, "blk", swap_core)]


def body(a_slots, a_rows, a_cols, a_count, owned_rows, b_matrix):
    groups = lax.axis_size("grid")
    columns = lax.axis_size("blk")
    bs = a_slots.shape[-1]
    cap = a_slots.shape[3]
    rb = owned_rows.shape[-1]
    blocks = b_matrix.shape[0] // bs
    depth = 2 * bs
    per = blocks // 2
    half = groups // 2
    pos = ring_place(lax.axis_index("grid"), groups).reshape(1)

    order = ring_order(groups)
    to_right = [(order[i], order[(i + 1) % groups]) for i in range(groups)]
    to_left = [(order[(i + 1) % groups], order[i]) for i in range(groups)]

    live = jnp.arange(cap, dtype=jnp.int32)[None, :] < a_count.reshape(groups, 1)
    row_code = jnp.where(live, a_rows.reshape(groups, cap) + 1, 0)
    meta = jnp.concatenate([row_code, a_cols.reshape(groups, cap)], axis=1)
    meta = jnp.pad(meta.astype(jnp.bfloat16)[:, None, :], ((0, 0), (0, META - 1), (0, bs - 2 * cap)))
    message = jnp.concatenate([a_slots.reshape(groups, cap * bs, bs), meta], axis=1)

    own = [b_matrix[h * depth : (h + 1) * depth] for h in range(per)]
    events = [own]
    from_left, from_right = list(own), list(own)
    for s in range(1, half + 1):
        low = range(per) if s < half else range(per // 2)
        high = range(per) if s < half else range(per // 2, per)
        from_left = {h: lax.ppermute(from_left[h], "grid", to_right) for h in low}
        from_right = {h: lax.ppermute(from_right[h], "grid", to_left) for h in high}
        if s == 1:
            (message,) = after([message], [from_left[0], from_right[0]])
            landed = lax.all_to_all(message, "grid", split_axis=0, concat_axis=0, tiled=True)
        if s == 2:
            from_left[0], from_right[0] = after([from_left[0], from_right[0]], [landed])
            parts = across_row(landed, columns)
        if s == half - 1:
            from_left[0], from_right[per - 1] = after(
                [from_left[0], from_right[per - 1]], parts[1:]
            )
        events.append([from_left[h] for h in low] + [from_right[h] for h in high])
    metas = [p[:, cap * bs, : 2 * cap].astype(jnp.int32) for p in parts]

    stages = [sum(events[: half - 1], []), events[half - 1], events[half]]
    bounds, start = [], 0
    for stage in stages:
        bounds.append((start, start + len(stage)))
        start += len(stage)
    dims = (columns, groups, cap, bs, groups, blocks)
    tiles = build_tiles(pos, owned_rows.reshape(rb), metas, parts, dims, bounds, rb * bs)

    acc = None
    for t, (tile, stage) in enumerate(zip(tiles, stages)):
        acc = mul(tile, stage, acc, jnp.bfloat16 if t == len(stages) - 1 else jnp.float32)
    return acc


def solution(mesh):
    in_specs = (
        P("grid", "blk", None, None, None, None),
        P("grid", "blk", None, None),
        P("grid", "blk", None, None),
        P("grid", "blk", None),
        P("grid", None),
        P("grid", "blk"),
    )
    out_specs = P("grid", "blk")
    return jax.shard_map(body, mesh=mesh, in_specs=in_specs, out_specs=out_specs, check_vma=False)
```

```python
import functools

import jax
import jax.numpy as jnp
from jax import lax
from jax.experimental import pallas as pl
from jax.experimental.pallas import tpu as pltpu
from jax.sharding import PartitionSpec as P

META = 16
VMEM_BYTES = 62 << 20


def ring_order(n):
    return list(range(0, n, 2)) + list(range(n - 1, 0, -2))


def ring_place(g, n):
    return jnp.where(g % 2 == 0, g // 2, n - 1 - g // 2)


def build_kernel(dims, bounds, pos_ref, owned_ref, *refs):
    n_parts, per_part, cap, bs, groups, blocks = dims
    metas, parts = refs[:n_parts], refs[n_parts : 2 * n_parts]
    tiles = refs[2 * n_parts :]
    for tile in tiles:
        tile[...] = jnp.zeros_like(tile)
    half, per = groups // 2, blocks // 2
    for meta, part in zip(metas, parts):

        def place(i, carry):
            for c in range(cap):
                code, col = meta[i, c], meta[i, cap + c]
                row, found = jnp.int32(0), jnp.int32(0)
                for r in range(owned_ref.shape[0]):
                    hit = owned_ref[r] + 1 == code
                    row = jnp.where(hit, r, row)
                    found = jnp.where(hit, 1, found)
                owner, local = col // blocks, col % blocks
                ahead = lax.rem(ring_place(owner, groups) - pos_ref[0] + groups, groups)
                hops = jnp.minimum(ahead, groups - ahead)
                first = jnp.where(hops == 0, 0, per * (2 * hops - 1))
                first += jnp.where((ahead > 0) & (ahead < half), per, 0)
                piece = first + local // 2
                for (low, high), tile in zip(bounds, tiles):

                    @pl.when((found == 1) & (piece >= low) & (piece < high))
                    def _():
                        at = ((piece - low) * 2 + local % 2) * bs
                        tile[
                            pl.ds(pl.multiple_of(row * bs, bs), bs),
                            pl.ds(pl.multiple_of(at, bs), bs),
                        ] = part[i, pl.ds(c * bs, bs), :]

            return carry

        lax.fori_loop(0, per_part, place, 0)


def build_tiles(pos, owned, metas, parts, dims, bounds, rows):
    n_parts, _, _, bs, groups, blocks = dims
    smem = pl.BlockSpec(memory_space=pltpu.SMEM)
    vmem = pl.BlockSpec(memory_space=pltpu.VMEM)
    return pl.pallas_call(
        functools.partial(build_kernel, dims, bounds),
        out_shape=[
            jax.ShapeDtypeStruct((rows, (high - low) * 2 * bs), jnp.bfloat16)
            for low, high in bounds
        ],
        in_specs=[smem] * (2 + n_parts) + [vmem] * n_parts,
        out_specs=[vmem] * len(bounds),
        compiler_params=pltpu.CompilerParams(vmem_limit_bytes=VMEM_BYTES),
        cost_estimate=pl.CostEstimate(
            flops=0, bytes_accessed=rows * groups * blocks * bs * 4, transcendentals=0
        ),
    )(pos, owned, *metas, *parts)


def after_kernel(*refs):
    pass


def after(values, others):
    anywhere = pl.BlockSpec(memory_space=pl.ANY)
    return pl.pallas_call(
        after_kernel,
        out_shape=[jax.ShapeDtypeStruct(v.shape, v.dtype) for v in values],
        in_specs=[anywhere] * (len(values) + len(others)),
        out_specs=[anywhere] * len(values),
        input_output_aliases={i: i for i in range(len(values))},
        cost_estimate=pl.CostEstimate(flops=0, bytes_accessed=0, transcendentals=0),
    )(*values, *others)


def mul_kernel(n_pieces, tile_ref, *refs):
    right = jnp.concatenate([piece[...] for piece in refs[:n_pieces]], axis=0)
    total = jnp.dot(tile_ref[...], right, preferred_element_type=jnp.float32)
    if len(refs) == n_pieces + 2:
        total += refs[n_pieces][...]
    refs[-1][...] = total.astype(refs[-1].dtype)


def mul(tile, pieces, acc, out_dtype):
    n = len(pieces)
    rows, inner = tile.shape
    depth, cols = pieces[0].shape
    bn = 256
    in_specs = [pl.BlockSpec((rows, inner), lambda j: (0, 0))]
    in_specs += [pl.BlockSpec((depth, bn), lambda j: (0, j)) for _ in range(n)]
    args = [tile, *pieces]
    if acc is not None:
        in_specs.append(pl.BlockSpec((rows, bn), lambda j: (0, j)))
        args.append(acc)
    return pl.pallas_call(
        functools.partial(mul_kernel, n),
        out_shape=jax.ShapeDtypeStruct((rows, cols), out_dtype),
        grid=(cols // bn,),
        in_specs=in_specs,
        out_specs=pl.BlockSpec((rows, bn), lambda j: (0, j)),
        compiler_params=pltpu.CompilerParams(vmem_limit_bytes=VMEM_BYTES),
        cost_estimate=pl.CostEstimate(
            flops=2 * rows * inner * cols,
            bytes_accessed=(rows + cols) * inner * 2 + rows * cols * 8,
            transcendentals=0,
        ),
    )(*args)


def across_row(landed, columns):
    if columns != 4:
        gathered = lax.all_gather(landed, "blk", axis=0)
        return [gathered[j] for j in range(columns)]
    swap_core = [(j, j ^ 1) for j in range(columns)]
    swap_chip = [(j, j ^ 2) for j in range(columns)]
    across = lax.ppermute(landed, "blk", swap_chip)
    near = lax.ppermute(landed, "blk", swap_core)
    return [landed, across, near, lax.ppermute(across, "blk", swap_core)]


def body(a_slots, a_rows, a_cols, a_count, owned_rows, b_matrix):
    groups = lax.axis_size("grid")
    columns = lax.axis_size("blk")
    bs = a_slots.shape[-1]
    cap = a_slots.shape[3]
    rb = owned_rows.shape[-1]
    blocks = b_matrix.shape[0] // bs
    depth = 2 * bs
    per = blocks // 2
    half = groups // 2
    pos = ring_place(lax.axis_index("grid"), groups).reshape(1)

    order = ring_order(groups)
    to_right = [(order[i], order[(i + 1) % groups]) for i in range(groups)]
    to_left = [(order[(i + 1) % groups], order[i]) for i in range(groups)]

    live = jnp.arange(cap, dtype=jnp.int32)[None, :] < a_count.reshape(groups, 1)
    row_code = jnp.where(live, a_rows.reshape(groups, cap) + 1, 0)
    meta = jnp.concatenate([row_code, a_cols.reshape(groups, cap)], axis=1)
    meta = jnp.pad(meta.astype(jnp.bfloat16)[:, None, :], ((0, 0), (0, META - 1), (0, bs - 2 * cap)))
    message = jnp.concatenate([a_slots.reshape(groups, cap * bs, bs), meta], axis=1)

    own = [b_matrix[h * depth : (h + 1) * depth] for h in range(per)]
    events = [own]
    from_left, from_right = list(own), list(own)
    for s in range(1, half + 1):
        low = range(per) if s < half else range(per // 2)
        high = range(per) if s < half else range(per // 2, per)
        from_left = {h: lax.ppermute(from_left[h], "grid", to_right) for h in low}
        from_right = {h: lax.ppermute(from_right[h], "grid", to_left) for h in high}
        if s == 1:
            first = list(from_left.values()) + list(from_right.values())
            (message,) = after([message], first)
            landed = lax.all_to_all(message, "grid", split_axis=0, concat_axis=0, tiled=True)
        if s == 2:
            from_left[per - 1], from_right[0] = after([from_left[per - 1], from_right[0]], [landed])
            parts = across_row(landed, columns)
        if s == half - 1:
            (from_left[0],) = after([from_left[0]], parts[1:2])
            (from_right[per - 1],) = after([from_right[per - 1]], parts[2:])
        events.append([from_left[h] for h in low] + [from_right[h] for h in high])
    metas = [p[:, cap * bs, : 2 * cap].astype(jnp.int32) for p in parts]

    stages = [sum(events[: half - 1], []), events[half - 1], events[half]]
    bounds, start = [], 0
    for stage in stages:
        bounds.append((start, start + len(stage)))
        start += len(stage)
    dims = (columns, groups, cap, bs, groups, blocks)
    tiles = build_tiles(pos, owned_rows.reshape(rb), metas, parts, dims, bounds, rb * bs)

    acc = None
    for t, (tile, stage) in enumerate(zip(tiles, stages)):
        acc = mul(tile, stage, acc, jnp.bfloat16 if t == len(stages) - 1 else jnp.float32)
    return acc


def solution(mesh):
    in_specs = (
        P("grid", "blk", None, None, None, None),
        P("grid", "blk", None, None),
        P("grid", "blk", None, None),
        P("grid", "blk", None),
        P("grid", None),
        P("grid", "blk"),
    )
    out_specs = P("grid", "blk")
    return jax.shard_map(body, mesh=mesh, in_specs=in_specs, out_specs=out_specs, check_vma=False)
```

```python
import functools

import jax
import jax.numpy as jnp
from jax import lax
from jax.experimental import pallas as pl
from jax.experimental.pallas import tpu as pltpu
from jax.sharding import PartitionSpec as P

META = 16
VMEM_BYTES = 62 << 20


def ring_order(n):
    return list(range(0, n, 2)) + list(range(n - 1, 0, -2))


def ring_place(g, n):
    return jnp.where(g % 2 == 0, g // 2, n - 1 - g // 2)


def build_kernel(dims, bounds, pos_ref, owned_ref, *refs):
    n_parts, per_part, cap, bs, groups, blocks = dims
    metas, parts = refs[:n_parts], refs[n_parts : 2 * n_parts]
    tiles = refs[2 * n_parts :]
    for tile in tiles:
        tile[...] = jnp.zeros_like(tile)
    half, per = groups // 2, blocks // 2
    for meta, part in zip(metas, parts):

        def place(i, carry):
            for c in range(cap):
                code, col = meta[i, c], meta[i, cap + c]
                row, found = jnp.int32(0), jnp.int32(0)
                for r in range(owned_ref.shape[0]):
                    hit = owned_ref[r] + 1 == code
                    row = jnp.where(hit, r, row)
                    found = jnp.where(hit, 1, found)
                owner, local = col // blocks, col % blocks
                ahead = lax.rem(ring_place(owner, groups) - pos_ref[0] + groups, groups)
                hops = jnp.minimum(ahead, groups - ahead)
                first = jnp.where(hops == 0, 0, per * (2 * hops - 1))
                first += jnp.where((ahead > 0) & (ahead < half), per, 0)
                piece = first + local // 2
                for (low, high), tile in zip(bounds, tiles):

                    @pl.when((found == 1) & (piece >= low) & (piece < high))
                    def _():
                        at = ((piece - low) * 2 + local % 2) * bs
                        tile[
                            pl.ds(pl.multiple_of(row * bs, bs), bs),
                            pl.ds(pl.multiple_of(at, bs), bs),
                        ] = part[i, pl.ds(c * bs, bs), :]

            return carry

        lax.fori_loop(0, per_part, place, 0)


def build_tiles(pos, owned, metas, parts, dims, bounds, rows):
    n_parts, _, _, bs, groups, blocks = dims
    smem = pl.BlockSpec(memory_space=pltpu.SMEM)
    vmem = pl.BlockSpec(memory_space=pltpu.VMEM)
    return pl.pallas_call(
        functools.partial(build_kernel, dims, bounds),
        out_shape=[
            jax.ShapeDtypeStruct((rows, (high - low) * 2 * bs), jnp.bfloat16)
            for low, high in bounds
        ],
        in_specs=[smem] * (2 + n_parts) + [vmem] * n_parts,
        out_specs=[vmem] * len(bounds),
        compiler_params=pltpu.CompilerParams(vmem_limit_bytes=VMEM_BYTES),
        cost_estimate=pl.CostEstimate(
            flops=0, bytes_accessed=rows * groups * blocks * bs * 4, transcendentals=0
        ),
    )(pos, owned, *metas, *parts)


def after_kernel(*refs):
    pass


def after(values, others):
    anywhere = pl.BlockSpec(memory_space=pl.ANY)
    return pl.pallas_call(
        after_kernel,
        out_shape=[jax.ShapeDtypeStruct(v.shape, v.dtype) for v in values],
        in_specs=[anywhere] * (len(values) + len(others)),
        out_specs=[anywhere] * len(values),
        input_output_aliases={i: i for i in range(len(values))},
        compiler_params=pltpu.CompilerParams(vmem_limit_bytes=VMEM_BYTES),
        cost_estimate=pl.CostEstimate(flops=0, bytes_accessed=0, transcendentals=0),
    )(*values, *others)


def mul_kernel(n_pieces, tile_ref, *refs):
    right = jnp.concatenate([piece[...] for piece in refs[:n_pieces]], axis=0)
    total = jnp.dot(tile_ref[...], right, preferred_element_type=jnp.float32)
    if len(refs) == n_pieces + 2:
        total += refs[n_pieces][...]
    refs[-1][...] = total.astype(refs[-1].dtype)


def mul(tile, pieces, acc, out_dtype):
    n = len(pieces)
    rows, inner = tile.shape
    depth, cols = pieces[0].shape
    bn = 256
    in_specs = [pl.BlockSpec((rows, inner), lambda j: (0, 0))]
    in_specs += [pl.BlockSpec((depth, bn), lambda j: (0, j)) for _ in range(n)]
    args = [tile, *pieces]
    if acc is not None:
        in_specs.append(pl.BlockSpec((rows, bn), lambda j: (0, j)))
        args.append(acc)
    return pl.pallas_call(
        functools.partial(mul_kernel, n),
        out_shape=jax.ShapeDtypeStruct((rows, cols), out_dtype),
        grid=(cols // bn,),
        in_specs=in_specs,
        out_specs=pl.BlockSpec((rows, bn), lambda j: (0, j)),
        compiler_params=pltpu.CompilerParams(vmem_limit_bytes=VMEM_BYTES),
        cost_estimate=pl.CostEstimate(
            flops=2 * rows * inner * cols,
            bytes_accessed=(rows + cols) * inner * 2 + rows * cols * 8,
            transcendentals=0,
        ),
    )(*args)


def across_row(landed, columns):
    if columns != 4:
        gathered = lax.all_gather(landed, "blk", axis=0)
        return [gathered[j] for j in range(columns)]
    swap_core = [(j, j ^ 1) for j in range(columns)]
    swap_chip = [(j, j ^ 2) for j in range(columns)]
    across = lax.ppermute(landed, "blk", swap_chip)
    near = lax.ppermute(landed, "blk", swap_core)
    return [landed, across, near, lax.ppermute(across, "blk", swap_core)]


def body(a_slots, a_rows, a_cols, a_count, owned_rows, b_matrix):
    groups = lax.axis_size("grid")
    columns = lax.axis_size("blk")
    bs = a_slots.shape[-1]
    cap = a_slots.shape[3]
    rb = owned_rows.shape[-1]
    blocks = b_matrix.shape[0] // bs
    depth = 2 * bs
    per = blocks // 2
    half = groups // 2
    pos = ring_place(lax.axis_index("grid"), groups).reshape(1)

    order = ring_order(groups)
    to_right = [(order[i], order[(i + 1) % groups]) for i in range(groups)]
    to_left = [(order[(i + 1) % groups], order[i]) for i in range(groups)]

    live = jnp.arange(cap, dtype=jnp.int32)[None, :] < a_count.reshape(groups, 1)
    row_code = jnp.where(live, a_rows.reshape(groups, cap) + 1, 0)
    meta = jnp.concatenate([row_code, a_cols.reshape(groups, cap)], axis=1)
    meta = jnp.pad(meta.astype(jnp.bfloat16)[:, None, :], ((0, 0), (0, META - 1), (0, bs - 2 * cap)))
    message = jnp.concatenate([a_slots.reshape(groups, cap * bs, bs), meta], axis=1)

    landed = lax.all_to_all(message, "grid", split_axis=0, concat_axis=0, tiled=True)
    parts = across_row(landed, columns)
    metas = [p[:, cap * bs, : 2 * cap].astype(jnp.int32) for p in parts]
    bounds, start = [], 0
    for count in (per * (half - 1) * 2 - per, per * 2, per):
        bounds.append((start, start + count))
        start += count
    dims = (columns, groups, cap, bs, groups, blocks)
    tiles = build_tiles(pos, owned_rows.reshape(rb), metas, parts, dims, bounds, rb * bs)

    own = [b_matrix[h * depth : (h + 1) * depth] for h in range(per)]
    events = [own]
    from_left, from_right = dict(enumerate(own)), dict(enumerate(own))
    for s in range(1, half + 1):
        low = range(per) if s < half else range(per // 2)
        high = range(per) if s < half else range(per // 2, per)
        from_left = {h: lax.ppermute(from_left[h], "grid", to_right) for h in low}
        from_right = {h: lax.ppermute(from_right[h], "grid", to_left) for h in high}
        if s == half - 2:
            from_left[0], from_right[0] = after([from_left[0], from_right[0]], parts[1:2])
            from_left[per - 1], from_right[per - 1] = after(
                [from_left[per - 1], from_right[per - 1]], parts[2:]
            )
        if s == half - 1:
            from_left[0], from_right[0] = after([from_left[0], from_right[0]], tiles)
        events.append([from_left[h] for h in low] + [from_right[h] for h in high])
    stages = [sum(events[: half - 1], []), events[half - 1], events[half]]

    acc = None
    for t, (tile, stage) in enumerate(zip(tiles, stages)):
        acc = mul(tile, stage, acc, jnp.bfloat16 if t == len(stages) - 1 else jnp.float32)
    return acc


def solution(mesh):
    in_specs = (
        P("grid", "blk", None, None, None, None),
        P("grid", "blk", None, None),
        P("grid", "blk", None, None),
        P("grid", "blk", None),
        P("grid", None),
        P("grid", "blk"),
    )
    out_specs = P("grid", "blk")
    return jax.shard_map(body, mesh=mesh, in_specs=in_specs, out_specs=out_specs, check_vma=False)
```

```python
import functools

import jax
import jax.numpy as jnp
from jax import lax
from jax.experimental import pallas as pl
from jax.experimental.pallas import tpu as pltpu
from jax.sharding import PartitionSpec as P

META = 16
VMEM_BYTES = 62 << 20


def ring_order(n):
    return list(range(0, n, 2)) + list(range(n - 1, 0, -2))


def ring_place(g, n):
    return jnp.where(g % 2 == 0, g // 2, n - 1 - g // 2)


def first_kernel(dims, dest_ref, *refs):
    n_parts, n_right, per_part, cap, bs, blocks = dims
    parts = refs[:n_parts]
    rights = refs[n_parts : n_parts + n_right]
    acc_hbm, late_hbm, left, right, acc, right_sem, acc_sem, late_sem = refs[n_parts + n_right :]
    depth = blocks * bs
    inner = n_right * depth
    bn = acc.shape[-1]
    fetches = [
        pltpu.make_async_copy(source, right.at[pl.ds(i * depth, depth)], right_sem.at[i])
        for i, source in enumerate(rights)
    ]
    for fetch in fetches:
        fetch.start()
    left[...] = jnp.zeros_like(left)
    k_blocks = left.shape[1] // bs
    for q, part in enumerate(parts):

        def place(i, carry):
            for c in range(cap):
                dest = dest_ref[q, i, c]

                @pl.when(dest >= 0)
                def _():
                    row, col = dest // k_blocks, dest % k_blocks
                    left[
                        pl.ds(pl.multiple_of(row * bs, bs), bs),
                        pl.ds(pl.multiple_of(col * bs, bs), bs),
                    ] = part[i, pl.ds(c * bs, bs), :]

            return carry

        lax.fori_loop(0, per_part, place, 0)
    late = pltpu.make_async_copy(left.at[:, pl.ds(inner, depth)], late_hbm, late_sem)
    late.start()
    for fetch in fetches:
        fetch.wait()
    stores = []
    for j in range(acc.shape[0]):
        acc[j] = jnp.dot(
            left[:, :inner],
            right[:, j * bn : (j + 1) * bn],
            preferred_element_type=jnp.float32,
        )
        store = pltpu.make_async_copy(acc.at[j], acc_hbm.at[j], acc_sem.at[j])
        store.start()
        stores.append(store)
    late.wait()
    for store in stores:
        store.wait()


def first_product(dest, parts, rights, rows, bs, cap, bn):
    n_parts, n_right = len(parts), len(rights)
    depth, cols = rights[0].shape
    inner = n_right * depth
    anywhere = pl.BlockSpec(memory_space=pl.ANY)
    dims = (n_parts, n_right, parts[0].shape[0], cap, bs, depth // bs)
    return pl.pallas_call(
        functools.partial(first_kernel, dims),
        out_shape=[
            jax.ShapeDtypeStruct((cols // bn, rows, bn), jnp.float32),
            jax.ShapeDtypeStruct((rows, depth), jnp.bfloat16),
        ],
        in_specs=[pl.BlockSpec(memory_space=pltpu.SMEM)]
        + [pl.BlockSpec(memory_space=pltpu.VMEM)] * n_parts
        + [anywhere] * n_right,
        out_specs=[anywhere] * 2,
        scratch_shapes=[
            pltpu.VMEM((rows, inner + depth), jnp.bfloat16),
            pltpu.VMEM((inner, cols), jnp.bfloat16),
            pltpu.VMEM((cols // bn, rows, bn), jnp.float32),
            pltpu.SemaphoreType.DMA((n_right,)),
            pltpu.SemaphoreType.DMA((cols // bn,)),
            pltpu.SemaphoreType.DMA,
        ],
        compiler_params=pltpu.CompilerParams(vmem_limit_bytes=VMEM_BYTES),
        cost_estimate=pl.CostEstimate(
            flops=2 * rows * inner * cols,
            bytes_accessed=inner * cols * 2 + rows * cols * 4,
            transcendentals=0,
        ),
    )(dest, *parts, *rights)


def last_kernel(left_ref, low_ref, high_ref, acc_ref, out_ref):
    right = jnp.concatenate([low_ref[...], high_ref[...]], axis=0)
    total = jnp.dot(left_ref[...], right, preferred_element_type=jnp.float32)
    out_ref[...] = (acc_ref[0] + total).astype(out_ref.dtype)


def last_product(left, low, high, acc):
    rows, inner = left.shape
    steps, _, bn = acc.shape
    return pl.pallas_call(
        last_kernel,
        out_shape=jax.ShapeDtypeStruct((rows, steps * bn), jnp.bfloat16),
        grid=(steps,),
        in_specs=[
            pl.BlockSpec((rows, inner), lambda j: (0, 0)),
            pl.BlockSpec((low.shape[0], bn), lambda j: (0, j)),
            pl.BlockSpec((high.shape[0], bn), lambda j: (0, j)),
            pl.BlockSpec((1, rows, bn), lambda j: (j, 0, 0)),
        ],
        out_specs=pl.BlockSpec((rows, bn), lambda j: (0, j)),
        compiler_params=pltpu.CompilerParams(vmem_limit_bytes=VMEM_BYTES),
        cost_estimate=pl.CostEstimate(
            flops=2 * rows * inner * steps * bn,
            bytes_accessed=(rows + steps * bn) * inner * 2 + rows * steps * bn * 6,
            transcendentals=0,
        ),
    )(left, low, high, acc)


def across_row(landed, columns):
    if columns != 4:
        gathered = lax.all_gather(landed, "blk", axis=0)
        return [gathered[j] for j in range(columns)]
    swap_core = [(j, j ^ 1) for j in range(columns)]
    swap_chip = [(j, j ^ 2) for j in range(columns)]
    across = lax.ppermute(landed, "blk", swap_chip)
    near = lax.ppermute(landed, "blk", swap_core)
    return [landed, across, near, lax.ppermute(across, "blk", swap_core)]


def body(a_slots, a_rows, a_cols, a_count, owned_rows, b_matrix):
    groups = lax.axis_size("grid")
    columns = lax.axis_size("blk")
    bs = a_slots.shape[-1]
    cap = a_slots.shape[3]
    rb = owned_rows.shape[-1]
    k_local, n_local = b_matrix.shape
    blocks = k_local // bs
    half = groups // 2

    order = ring_order(groups)
    to_right = [(order[i], order[(i + 1) % groups]) for i in range(groups)]
    to_left = [(order[(i + 1) % groups], order[i]) for i in range(groups)]
    from_left, from_right, rights = b_matrix, b_matrix, [b_matrix]
    for s in range(1, half):
        from_left = lax.ppermute(from_left, "grid", to_right)
        from_right = lax.ppermute(from_right, "grid", to_left)
        rights += [from_left, from_right]
    low = lax.ppermute(from_left[: k_local // 2], "grid", to_right)
    high = lax.ppermute(from_right[k_local // 2 :], "grid", to_left)

    live = jnp.arange(cap, dtype=jnp.int32)[None, :] < a_count.reshape(groups, 1)
    row_code = jnp.where(live, a_rows.reshape(groups, cap) + 1, 0)
    meta = jnp.concatenate([row_code, a_cols.reshape(groups, cap)], axis=1)
    meta = jnp.pad(meta.astype(jnp.bfloat16)[:, None, :], ((0, 0), (0, META - 1), (0, bs - 2 * cap)))
    message = jnp.concatenate([a_slots.reshape(groups, cap * bs, bs), meta], axis=1)
    landed = lax.all_to_all(message, "grid", split_axis=0, concat_axis=0, tiled=True)
    parts = across_row(landed, columns)

    metas = jnp.stack([p[:, cap * bs, : 2 * cap] for p in parts]).astype(jnp.int32)
    code, col = metas[..., :cap], metas[..., cap:]
    hit = code[..., None] == owned_rows.reshape(rb) + 1
    row = jnp.sum(jnp.where(hit, jnp.arange(rb, dtype=jnp.int32), 0), axis=-1)
    pos = ring_place(lax.axis_index("grid"), groups)
    ahead = (ring_place(col // blocks, groups) - pos + groups) % groups
    hops = jnp.minimum(ahead, groups - ahead)
    first = jnp.where(hops == 0, 0, 2 * hops - 1) + jnp.where((ahead > 0) & (ahead < half), 1, 0)
    dest = row * (blocks * groups) + first * blocks + col % blocks
    dest = jnp.where(jnp.any(hit, axis=-1), dest, -1)

    acc, late = first_product(dest, parts, rights, rb * bs, bs, cap, n_local // 4)
    return last_product(late, low, high, acc)


def solution(mesh):
    in_specs = (
        P("grid", "blk", None, None, None, None),
        P("grid", "blk", None, None),
        P("grid", "blk", None, None),
        P("grid", "blk", None),
        P("grid", None),
        P("grid", "blk"),
    )
    out_specs = P("grid", "blk")
    return jax.shard_map(body, mesh=mesh, in_specs=in_specs, out_specs=out_specs, check_vma=False)
```

```python
import functools

import jax
import jax.numpy as jnp
from jax import lax
from jax.experimental import pallas as pl
from jax.experimental.pallas import tpu as pltpu
from jax.sharding import PartitionSpec as P

META = 16
VMEM_BYTES = 62 << 20


def ring_order(n):
    return list(range(0, n, 2)) + list(range(n - 1, 0, -2))


def ring_place(g, n):
    return jnp.where(g % 2 == 0, g // 2, n - 1 - g // 2)


def first_kernel(dims, dest_ref, *refs):
    n_parts, n_right, per_part, cap, bs, blocks = dims
    parts = refs[:n_parts]
    rights = refs[n_parts : n_parts + n_right]
    acc_hbm, late_hbm, left, right, acc, right_sem, acc_sem, late_sem = refs[n_parts + n_right :]
    depth = blocks * bs
    inner = n_right * depth
    bn = acc.shape[-1]
    fetches = [
        pltpu.make_async_copy(source, right.at[pl.ds(i * depth, depth)], right_sem.at[i])
        for i, source in enumerate(rights)
    ]
    for fetch in fetches:
        fetch.start()
    left[...] = jnp.zeros_like(left)
    k_blocks = left.shape[1] // bs
    for q, part in enumerate(parts):

        def place(i, carry):
            for c in range(cap):
                dest = dest_ref[q, i, c]

                @pl.when(dest >= 0)
                def _():
                    row, col = dest // k_blocks, dest % k_blocks
                    left[
                        pl.ds(pl.multiple_of(row * bs, bs), bs),
                        pl.ds(pl.multiple_of(col * bs, bs), bs),
                    ] = part[i, pl.ds(c * bs, bs), :]

            return carry

        lax.fori_loop(0, per_part, place, 0)
    late = pltpu.make_async_copy(
        left.at[:, pl.ds(inner, late_hbm.shape[1])], late_hbm, late_sem
    )
    late.start()
    for fetch in fetches:
        fetch.wait()
    stores = []
    for j in range(acc.shape[0]):
        acc[j] = jnp.dot(
            left[:, :inner],
            right[:, j * bn : (j + 1) * bn],
            preferred_element_type=jnp.float32,
        )
        store = pltpu.make_async_copy(acc.at[j], acc_hbm.at[j], acc_sem.at[j])
        store.start()
        stores.append(store)
    late.wait()
    for store in stores:
        store.wait()


def first_product(dest, parts, rights, rows, late_width, bs, cap, bn):
    n_parts, n_right = len(parts), len(rights)
    depth, cols = rights[0].shape
    inner = n_right * depth
    anywhere = pl.BlockSpec(memory_space=pl.ANY)
    dims = (n_parts, n_right, parts[0].shape[0], cap, bs, depth // bs)
    return pl.pallas_call(
        functools.partial(first_kernel, dims),
        out_shape=[
            jax.ShapeDtypeStruct((cols // bn, rows, bn), jnp.float32),
            jax.ShapeDtypeStruct((rows, late_width), jnp.bfloat16),
        ],
        in_specs=[pl.BlockSpec(memory_space=pltpu.SMEM)]
        + [pl.BlockSpec(memory_space=pltpu.VMEM)] * n_parts
        + [anywhere] * n_right,
        out_specs=[anywhere] * 2,
        scratch_shapes=[
            pltpu.VMEM((rows, inner + late_width), jnp.bfloat16),
            pltpu.VMEM((inner, cols), jnp.bfloat16),
            pltpu.VMEM((cols // bn, rows, bn), jnp.float32),
            pltpu.SemaphoreType.DMA((n_right,)),
            pltpu.SemaphoreType.DMA((cols // bn,)),
            pltpu.SemaphoreType.DMA,
        ],
        compiler_params=pltpu.CompilerParams(vmem_limit_bytes=VMEM_BYTES),
        cost_estimate=pl.CostEstimate(
            flops=2 * rows * inner * cols,
            bytes_accessed=inner * cols * 2 + rows * cols * 4,
            transcendentals=0,
        ),
    )(dest, *parts, *rights)


def add_kernel(left_ref, *refs):
    right = jnp.concatenate([piece[...] for piece in refs[:-2]], axis=0)
    total = jnp.dot(left_ref[...], right, preferred_element_type=jnp.float32)
    out_ref = refs[-1]
    out_ref[...] = (refs[-2][0] + total).astype(out_ref.dtype).reshape(out_ref.shape)


def add_product(left, place, pieces, acc, last):
    steps, rows, bn = acc.shape
    inner = sum(piece.shape[0] for piece in pieces)
    acc_spec = pl.BlockSpec((1, rows, bn), lambda j: (j, 0, 0))
    out_spec = pl.BlockSpec((rows, bn), lambda j: (0, j))
    out_shape = jax.ShapeDtypeStruct((rows, steps * bn), jnp.bfloat16)
    return pl.pallas_call(
        add_kernel,
        out_shape=out_shape if last else jax.ShapeDtypeStruct(acc.shape, acc.dtype),
        grid=(steps,),
        in_specs=[pl.BlockSpec((rows, inner), lambda j: (0, place))]
        + [pl.BlockSpec((piece.shape[0], bn), lambda j: (0, j)) for piece in pieces]
        + [acc_spec],
        out_specs=out_spec if last else acc_spec,
        compiler_params=pltpu.CompilerParams(vmem_limit_bytes=VMEM_BYTES),
        cost_estimate=pl.CostEstimate(
            flops=2 * rows * inner * steps * bn,
            bytes_accessed=(rows + steps * bn) * inner * 2 + rows * steps * bn * 8,
            transcendentals=0,
        ),
    )(left, *pieces, acc)


def across_row(landed, columns):
    if columns != 4:
        gathered = lax.all_gather(landed, "blk", axis=0)
        return [gathered[j] for j in range(columns)]
    swap_core = [(j, j ^ 1) for j in range(columns)]
    swap_chip = [(j, j ^ 2) for j in range(columns)]
    across = lax.ppermute(landed, "blk", swap_chip)
    near = lax.ppermute(landed, "blk", swap_core)
    return [landed, across, near, lax.ppermute(across, "blk", swap_core)]


def body(a_slots, a_rows, a_cols, a_count, owned_rows, b_matrix):
    groups = lax.axis_size("grid")
    columns = lax.axis_size("blk")
    bs = a_slots.shape[-1]
    cap = a_slots.shape[3]
    rb = owned_rows.shape[-1]
    k_local, n_local = b_matrix.shape
    blocks = k_local // bs
    half = groups // 2

    order = ring_order(groups)
    to_right = [(order[i], order[(i + 1) % groups]) for i in range(groups)]
    to_left = [(order[(i + 1) % groups], order[i]) for i in range(groups)]
    from_left, from_right, early = b_matrix, b_matrix, [b_matrix]
    for s in range(1, half - 1):
        from_left = lax.ppermute(from_left, "grid", to_right)
        from_right = lax.ppermute(from_right, "grid", to_left)
        early += [from_left, from_right]
    split = k_local // 2
    left_low = lax.ppermute(from_left[:split], "grid", to_right)
    right_high = lax.ppermute(from_right[split:], "grid", to_left)
    left_high = lax.ppermute(from_left[split:], "grid", to_right)
    right_low = lax.ppermute(from_right[:split], "grid", to_left)
    low = lax.ppermute(left_low, "grid", to_right)
    high = lax.ppermute(right_high, "grid", to_left)

    live = jnp.arange(cap, dtype=jnp.int32)[None, :] < a_count.reshape(groups, 1)
    row_code = jnp.where(live, a_rows.reshape(groups, cap) + 1, 0)
    meta = jnp.concatenate([row_code, a_cols.reshape(groups, cap)], axis=1)
    meta = jnp.pad(meta.astype(jnp.bfloat16)[:, None, :], ((0, 0), (0, META - 1), (0, bs - 2 * cap)))
    message = jnp.concatenate([a_slots.reshape(groups, cap * bs, bs), meta], axis=1)
    landed = lax.all_to_all(message, "grid", split_axis=0, concat_axis=0, tiled=True)
    parts = across_row(landed, columns)

    metas = jnp.stack([p[:, cap * bs, : 2 * cap] for p in parts]).astype(jnp.int32)
    code, col = metas[..., :cap], metas[..., cap:]
    hit = code[..., None] == owned_rows.reshape(rb) + 1
    row = jnp.sum(jnp.where(hit, jnp.arange(rb, dtype=jnp.int32), 0), axis=-1)
    pos = ring_place(lax.axis_index("grid"), groups)
    ahead = (ring_place(col // blocks, groups) - pos + groups) % groups
    hops = jnp.minimum(ahead, groups - ahead)
    first = jnp.where(hops == 0, 0, 2 * hops - 1) + jnp.where((ahead > 0) & (ahead < half), 1, 0)
    dest = row * (blocks * groups) + first * blocks + col % blocks
    dest = jnp.where(jnp.any(hit, axis=-1), dest, -1)

    acc, late = first_product(dest, parts, early, rb * bs, 3 * k_local, bs, cap, n_local // 4)
    acc = add_product(late, 0, [left_low, left_high, right_low, right_high], acc, False)
    return add_product(late, 2, [low, high], acc, True)


def solution(mesh):
    in_specs = (
        P("grid", "blk", None, None, None, None),
        P("grid", "blk", None, None),
        P("grid", "blk", None, None),
        P("grid", "blk", None),
        P("grid", None),
        P("grid", "blk"),
    )
    out_specs = P("grid", "blk")
    return jax.shard_map(body, mesh=mesh, in_specs=in_specs, out_specs=out_specs, check_vma=False)
```

```python
import functools

import jax
import jax.numpy as jnp
from jax import lax
from jax.experimental import pallas as pl
from jax.experimental.pallas import tpu as pltpu
from jax.sharding import PartitionSpec as P

META = 16
VMEM_BYTES = 62 << 20


def ring_order(n):
    return list(range(0, n, 2)) + list(range(n - 1, 0, -2))


def ring_place(g, n):
    return jnp.where(g % 2 == 0, g // 2, n - 1 - g // 2)


def pack_kernel(slots_hbm, meta_hbm, message_hbm, sems):
    rows = slots_hbm.shape[1]
    copies = [
        pltpu.make_async_copy(slots_hbm, message_hbm.at[:, pl.ds(0, rows)], sems.at[0]),
        pltpu.make_async_copy(meta_hbm, message_hbm.at[:, pl.ds(rows, META)], sems.at[1]),
    ]
    for copy in copies:
        copy.start()
    for copy in copies:
        copy.wait()


def pack(slots, meta):
    groups, rows, width = slots.shape
    anywhere = pl.BlockSpec(memory_space=pl.ANY)
    return pl.pallas_call(
        pack_kernel,
        out_shape=jax.ShapeDtypeStruct((groups, rows + META, width), slots.dtype),
        in_specs=[anywhere] * 2,
        out_specs=anywhere,
        scratch_shapes=[pltpu.SemaphoreType.DMA((2,))],
        compiler_params=pltpu.CompilerParams(vmem_limit_bytes=VMEM_BYTES),
        cost_estimate=pl.CostEstimate(
            flops=0, bytes_accessed=slots.size * 4, transcendentals=0
        ),
    )(slots, meta)


def after_kernel(*refs):
    pass


def after(values, others):
    anywhere = pl.BlockSpec(memory_space=pl.ANY)
    return pl.pallas_call(
        after_kernel,
        out_shape=[jax.ShapeDtypeStruct(v.shape, v.dtype) for v in values],
        in_specs=[anywhere] * (len(values) + len(others)),
        out_specs=[anywhere] * len(values),
        input_output_aliases={i: i for i in range(len(values))},
        compiler_params=pltpu.CompilerParams(vmem_limit_bytes=VMEM_BYTES),
        cost_estimate=pl.CostEstimate(flops=0, bytes_accessed=0, transcendentals=0),
    )(*values, *others)


def first_kernel(dims, dest_ref, *refs):
    n_parts, n_right, per_part, cap, bs, blocks = dims
    parts = refs[:n_parts]
    rights = refs[n_parts : n_parts + n_right]
    acc_hbm, late_hbm, left, right, acc, right_sem, acc_sem, late_sem = refs[n_parts + n_right :]
    depth = blocks * bs
    inner = n_right * depth
    bn = acc.shape[-1]
    fetches = [
        pltpu.make_async_copy(source, right.at[pl.ds(i * depth, depth)], right_sem.at[i])
        for i, source in enumerate(rights)
    ]
    for fetch in fetches:
        fetch.start()
    left[...] = jnp.zeros_like(left)
    k_blocks = left.shape[1] // bs
    for q, part in enumerate(parts):

        def place(i, carry):
            for c in range(cap):
                dest = dest_ref[q, i, c]

                @pl.when(dest >= 0)
                def _():
                    row, col = dest // k_blocks, dest % k_blocks
                    left[
                        pl.ds(pl.multiple_of(row * bs, bs), bs),
                        pl.ds(pl.multiple_of(col * bs, bs), bs),
                    ] = part[i, pl.ds(c * bs, bs), :]

            return carry

        lax.fori_loop(0, per_part, place, 0)
    late = pltpu.make_async_copy(
        left.at[:, pl.ds(inner, late_hbm.shape[1])], late_hbm, late_sem
    )
    late.start()
    for fetch in fetches:
        fetch.wait()
    stores = []
    for j in range(acc.shape[0]):
        acc[j] = jnp.dot(
            left[:, :inner],
            right[:, j * bn : (j + 1) * bn],
            preferred_element_type=jnp.float32,
        )
        store = pltpu.make_async_copy(acc.at[j], acc_hbm.at[j], acc_sem.at[j])
        store.start()
        stores.append(store)
    late.wait()
    for store in stores:
        store.wait()


def first_product(dest, parts, rights, rows, late_width, bs, cap, bn):
    n_parts, n_right = len(parts), len(rights)
    depth, cols = rights[0].shape
    inner = n_right * depth
    anywhere = pl.BlockSpec(memory_space=pl.ANY)
    dims = (n_parts, n_right, parts[0].shape[0], cap, bs, depth // bs)
    return pl.pallas_call(
        functools.partial(first_kernel, dims),
        out_shape=[
            jax.ShapeDtypeStruct((cols // bn, rows, bn), jnp.float32),
            jax.ShapeDtypeStruct((rows, late_width), jnp.bfloat16),
        ],
        in_specs=[pl.BlockSpec(memory_space=pltpu.SMEM)]
        + [pl.BlockSpec(memory_space=pltpu.VMEM)] * n_parts
        + [anywhere] * n_right,
        out_specs=[anywhere] * 2,
        scratch_shapes=[
            pltpu.VMEM((rows, inner + late_width), jnp.bfloat16),
            pltpu.VMEM((inner, cols), jnp.bfloat16),
            pltpu.VMEM((cols // bn, rows, bn), jnp.float32),
            pltpu.SemaphoreType.DMA((n_right,)),
            pltpu.SemaphoreType.DMA((cols // bn,)),
            pltpu.SemaphoreType.DMA,
        ],
        compiler_params=pltpu.CompilerParams(vmem_limit_bytes=VMEM_BYTES),
        cost_estimate=pl.CostEstimate(
            flops=2 * rows * inner * cols,
            bytes_accessed=inner * cols * 2 + rows * cols * 4,
            transcendentals=0,
        ),
    )(dest, *parts, *rights)


def add_kernel(left_ref, *refs):
    right = jnp.concatenate([piece[...] for piece in refs[:-2]], axis=0)
    total = jnp.dot(left_ref[...], right, preferred_element_type=jnp.float32)
    out_ref = refs[-1]
    out_ref[...] = (refs[-2][0] + total).astype(out_ref.dtype).reshape(out_ref.shape)


def add_product(left, place, pieces, acc, last):
    steps, rows, bn = acc.shape
    inner = sum(piece.shape[0] for piece in pieces)
    acc_spec = pl.BlockSpec((1, rows, bn), lambda j: (j, 0, 0))
    out_spec = pl.BlockSpec((rows, bn), lambda j: (0, j))
    out_shape = jax.ShapeDtypeStruct((rows, steps * bn), jnp.bfloat16)
    return pl.pallas_call(
        add_kernel,
        out_shape=out_shape if last else jax.ShapeDtypeStruct(acc.shape, acc.dtype),
        grid=(steps,),
        in_specs=[pl.BlockSpec((rows, inner), lambda j: (0, place))]
        + [pl.BlockSpec((piece.shape[0], bn), lambda j: (0, j)) for piece in pieces]
        + [acc_spec],
        out_specs=out_spec if last else acc_spec,
        compiler_params=pltpu.CompilerParams(vmem_limit_bytes=VMEM_BYTES),
        cost_estimate=pl.CostEstimate(
            flops=2 * rows * inner * steps * bn,
            bytes_accessed=(rows + steps * bn) * inner * 2 + rows * steps * bn * 8,
            transcendentals=0,
        ),
    )(left, *pieces, acc)


def across_row(landed, columns):
    if columns != 4:
        gathered = lax.all_gather(landed, "blk", axis=0)
        return [gathered[j] for j in range(columns)]
    swap_core = [(j, j ^ 1) for j in range(columns)]
    swap_chip = [(j, j ^ 2) for j in range(columns)]
    across = lax.ppermute(landed, "blk", swap_chip)
    near = lax.ppermute(landed, "blk", swap_core)
    return [landed, across, near, lax.ppermute(across, "blk", swap_core)]


def body(a_slots, a_rows, a_cols, a_count, owned_rows, b_matrix):
    groups = lax.axis_size("grid")
    columns = lax.axis_size("blk")
    bs = a_slots.shape[-1]
    cap = a_slots.shape[3]
    rb = owned_rows.shape[-1]
    k_local, n_local = b_matrix.shape
    blocks = k_local // bs
    half = groups // 2

    order = ring_order(groups)
    to_right = [(order[i], order[(i + 1) % groups]) for i in range(groups)]
    to_left = [(order[(i + 1) % groups], order[i]) for i in range(groups)]
    from_left, from_right, early = b_matrix, b_matrix, [b_matrix]
    for s in range(1, half - 1):
        from_left = lax.ppermute(from_left, "grid", to_right)
        from_right = lax.ppermute(from_right, "grid", to_left)
        early += [from_left, from_right]
    split = k_local // 2
    left_low = lax.ppermute(from_left[:split], "grid", to_right)
    right_high = lax.ppermute(from_right[split:], "grid", to_left)
    left_high = lax.ppermute(from_left[split:], "grid", to_right)
    right_low = lax.ppermute(from_right[:split], "grid", to_left)

    live = jnp.arange(cap, dtype=jnp.int32)[None, :] < a_count.reshape(groups, 1)
    row_code = jnp.where(live, a_rows.reshape(groups, cap) + 1, 0)
    meta = jnp.concatenate([row_code, a_cols.reshape(groups, cap)], axis=1)
    meta = jnp.pad(meta.astype(jnp.bfloat16)[:, None, :], ((0, 0), (0, META - 1), (0, bs - 2 * cap)))
    message = pack(a_slots.reshape(groups, cap * bs, bs), meta)
    landed = lax.all_to_all(message, "grid", split_axis=0, concat_axis=0, tiled=True)
    (landed,) = after([landed], early[1:3])
    parts = across_row(landed, columns)

    metas = jnp.stack([p[:, cap * bs, : 2 * cap] for p in parts]).astype(jnp.int32)
    code, col = metas[..., :cap], metas[..., cap:]
    hit = code[..., None] == owned_rows.reshape(rb) + 1
    row = jnp.sum(jnp.where(hit, jnp.arange(rb, dtype=jnp.int32), 0), axis=-1)
    pos = ring_place(lax.axis_index("grid"), groups)
    ahead = (ring_place(col // blocks, groups) - pos + groups) % groups
    hops = jnp.minimum(ahead, groups - ahead)
    first = jnp.where(hops == 0, 0, 2 * hops - 1) + jnp.where((ahead > 0) & (ahead < half), 1, 0)
    dest = row * (blocks * groups) + first * blocks + col % blocks
    dest = jnp.where(jnp.any(hit, axis=-1), dest, -1)

    acc, late = first_product(dest, parts, early, rb * bs, 3 * k_local, bs, cap, n_local // 4)
    left_low, right_high = after([left_low, right_high], [acc])
    low = lax.ppermute(left_low, "grid", to_right)
    high = lax.ppermute(right_high, "grid", to_left)
    acc = add_product(late, 0, [left_low, left_high, right_low, right_high], acc, False)
    return add_product(late, 2, [low, high], acc, True)


def solution(mesh):
    in_specs = (
        P("grid", "blk", None, None, None, None),
        P("grid", "blk", None, None),
        P("grid", "blk", None, None),
        P("grid", "blk", None),
        P("grid", None),
        P("grid", "blk"),
    )
    out_specs = P("grid", "blk")
    return jax.shard_map(body, mesh=mesh, in_specs=in_specs, out_specs=out_specs, check_vma=False)
```

```python
import functools

import jax
import jax.numpy as jnp
from jax import lax
from jax.experimental import pallas as pl
from jax.experimental.pallas import tpu as pltpu
from jax.sharding import PartitionSpec as P

META = 16
VMEM_BYTES = 62 << 20


def ring_order(n):
    return list(range(0, n, 2)) + list(range(n - 1, 0, -2))


def ring_place(g, n):
    return jnp.where(g % 2 == 0, g // 2, n - 1 - g // 2)


def pack_kernel(slots_ref, meta_ref, message_ref):
    rows = slots_ref.shape[1]
    message_ref[:, :rows] = slots_ref[...]
    message_ref[:, rows:] = meta_ref[...]


def pack(slots, meta):
    groups, rows, width = slots.shape
    part = groups // 4
    return pl.pallas_call(
        pack_kernel,
        out_shape=jax.ShapeDtypeStruct((groups, rows + META, width), slots.dtype),
        grid=(groups // part,),
        in_specs=[
            pl.BlockSpec((part, rows, width), lambda i: (i, 0, 0)),
            pl.BlockSpec((part, META, width), lambda i: (i, 0, 0)),
        ],
        out_specs=pl.BlockSpec((part, rows + META, width), lambda i: (i, 0, 0)),
        compiler_params=pltpu.CompilerParams(vmem_limit_bytes=VMEM_BYTES),
        cost_estimate=pl.CostEstimate(
            flops=0, bytes_accessed=slots.size * 4, transcendentals=0
        ),
    )(slots, meta)


def after_kernel(*refs):
    pass


def after(values, others):
    anywhere = pl.BlockSpec(memory_space=pl.ANY)
    return pl.pallas_call(
        after_kernel,
        out_shape=[jax.ShapeDtypeStruct(v.shape, v.dtype) for v in values],
        in_specs=[anywhere] * (len(values) + len(others)),
        out_specs=[anywhere] * len(values),
        input_output_aliases={i: i for i in range(len(values))},
        compiler_params=pltpu.CompilerParams(vmem_limit_bytes=VMEM_BYTES),
        cost_estimate=pl.CostEstimate(flops=0, bytes_accessed=0, transcendentals=0),
    )(*values, *others)


def first_kernel(dims, dest_ref, *refs):
    n_parts, n_right, per_part, cap, bs, blocks = dims
    parts = refs[:n_parts]
    rights = refs[n_parts : n_parts + n_right]
    acc_hbm, late_hbm, left, right, acc, right_sem, acc_sem, late_sem = refs[n_parts + n_right :]
    depth = blocks * bs
    inner = n_right * depth
    bn = acc.shape[-1]
    fetches = [
        pltpu.make_async_copy(source, right.at[pl.ds(i * depth, depth)], right_sem.at[i])
        for i, source in enumerate(rights)
    ]
    for fetch in fetches:
        fetch.start()
    left[...] = jnp.zeros_like(left)
    k_blocks = left.shape[1] // bs
    for q, part in enumerate(parts):

        def place(i, carry):
            for c in range(cap):
                dest = dest_ref[q, i, c]

                @pl.when(dest >= 0)
                def _():
                    row, col = dest // k_blocks, dest % k_blocks
                    left[
                        pl.ds(pl.multiple_of(row * bs, bs), bs),
                        pl.ds(pl.multiple_of(col * bs, bs), bs),
                    ] = part[i, pl.ds(c * bs, bs), :]

            return carry

        lax.fori_loop(0, per_part, place, 0)
    late = pltpu.make_async_copy(
        left.at[:, pl.ds(inner, late_hbm.shape[1])], late_hbm, late_sem
    )
    late.start()
    for fetch in fetches:
        fetch.wait()
    stores = []
    for j in range(acc.shape[0]):
        acc[j] = jnp.dot(
            left[:, :inner],
            right[:, j * bn : (j + 1) * bn],
            preferred_element_type=jnp.float32,
        )
        store = pltpu.make_async_copy(acc.at[j], acc_hbm.at[j], acc_sem.at[j])
        store.start()
        stores.append(store)
    late.wait()
    for store in stores:
        store.wait()


def first_product(dest, parts, rights, rows, late_width, bs, cap, bn):
    n_parts, n_right = len(parts), len(rights)
    depth, cols = rights[0].shape
    inner = n_right * depth
    anywhere = pl.BlockSpec(memory_space=pl.ANY)
    dims = (n_parts, n_right, parts[0].shape[0], cap, bs, depth // bs)
    return pl.pallas_call(
        functools.partial(first_kernel, dims),
        out_shape=[
            jax.ShapeDtypeStruct((cols // bn, rows, bn), jnp.float32),
            jax.ShapeDtypeStruct((rows, late_width), jnp.bfloat16),
        ],
        in_specs=[pl.BlockSpec(memory_space=pltpu.SMEM)]
        + [pl.BlockSpec(memory_space=pltpu.VMEM)] * n_parts
        + [anywhere] * n_right,
        out_specs=[anywhere] * 2,
        scratch_shapes=[
            pltpu.VMEM((rows, inner + late_width), jnp.bfloat16),
            pltpu.VMEM((inner, cols), jnp.bfloat16),
            pltpu.VMEM((cols // bn, rows, bn), jnp.float32),
            pltpu.SemaphoreType.DMA((n_right,)),
            pltpu.SemaphoreType.DMA((cols // bn,)),
            pltpu.SemaphoreType.DMA,
        ],
        compiler_params=pltpu.CompilerParams(vmem_limit_bytes=VMEM_BYTES),
        cost_estimate=pl.CostEstimate(
            flops=2 * rows * inner * cols,
            bytes_accessed=inner * cols * 2 + rows * cols * 4,
            transcendentals=0,
        ),
    )(dest, *parts, *rights)


def add_kernel(depths, left_ref, acc_ref, *refs):
    pieces = refs[: len(depths)]
    out_ref, right, sems = refs[len(depths) :]
    j = pl.program_id(0)
    steps, _, bn = right.shape

    def fetch(chunk):
        at = 0
        copies = []
        for i, (depth, piece) in enumerate(zip(depths, pieces)):
            copies.append(
                pltpu.make_async_copy(
                    piece.at[:, pl.ds(chunk * bn, bn)],
                    right.at[chunk, pl.ds(at, depth)],
                    sems.at[chunk, i],
                )
            )
            at += depth
        return copies

    @pl.when(j == 0)
    def _():
        for chunk in range(steps):
            for copy in fetch(chunk):
                copy.start()

    for chunk in range(steps):

        @pl.when(j == chunk)
        def _():
            for copy in fetch(chunk):
                copy.wait()

    total = jnp.dot(left_ref[...], right[j], preferred_element_type=jnp.float32)
    out_ref[...] = (acc_ref[0] + total).astype(out_ref.dtype).reshape(out_ref.shape)


def add_product(left, place, pieces, acc, last):
    steps, rows, bn = acc.shape
    depths = [piece.shape[0] for piece in pieces]
    inner = sum(depths)
    acc_spec = pl.BlockSpec((1, rows, bn), lambda j: (j, 0, 0))
    out_spec = pl.BlockSpec((rows, bn), lambda j: (0, j))
    out_shape = jax.ShapeDtypeStruct((rows, steps * bn), jnp.bfloat16)
    return pl.pallas_call(
        functools.partial(add_kernel, depths),
        out_shape=out_shape if last else jax.ShapeDtypeStruct(acc.shape, acc.dtype),
        grid=(steps,),
        in_specs=[pl.BlockSpec((rows, inner), lambda j: (0, place)), acc_spec]
        + [pl.BlockSpec(memory_space=pl.ANY)] * len(pieces),
        out_specs=out_spec if last else acc_spec,
        scratch_shapes=[
            pltpu.VMEM((steps, inner, bn), jnp.bfloat16),
            pltpu.SemaphoreType.DMA((steps, len(pieces))),
        ],
        compiler_params=pltpu.CompilerParams(vmem_limit_bytes=VMEM_BYTES),
        cost_estimate=pl.CostEstimate(
            flops=2 * rows * inner * steps * bn,
            bytes_accessed=(rows + steps * bn) * inner * 2 + rows * steps * bn * 8,
            transcendentals=0,
        ),
    )(left, acc, *pieces)


def across_row(landed, columns):
    if columns != 4:
        gathered = lax.all_gather(landed, "blk", axis=0)
        return [gathered[j] for j in range(columns)]
    swap_core = [(j, j ^ 1) for j in range(columns)]
    swap_chip = [(j, j ^ 2) for j in range(columns)]
    across = lax.ppermute(landed, "blk", swap_chip)
    near = lax.ppermute(landed, "blk", swap_core)
    return [landed, across, near, lax.ppermute(across, "blk", swap_core)]


def body(a_slots, a_rows, a_cols, a_count, owned_rows, b_matrix):
    groups = lax.axis_size("grid")
    columns = lax.axis_size("blk")
    bs = a_slots.shape[-1]
    cap = a_slots.shape[3]
    rb = owned_rows.shape[-1]
    k_local, n_local = b_matrix.shape
    blocks = k_local // bs
    half = groups // 2

    order = ring_order(groups)
    to_right = [(order[i], order[(i + 1) % groups]) for i in range(groups)]
    to_left = [(order[(i + 1) % groups], order[i]) for i in range(groups)]
    from_left, from_right, early = b_matrix, b_matrix, [b_matrix]
    for s in range(1, half - 1):
        from_left = lax.ppermute(from_left, "grid", to_right)
        from_right = lax.ppermute(from_right, "grid", to_left)
        early += [from_left, from_right]
    split = k_local // 2
    left_low = lax.ppermute(from_left[:split], "grid", to_right)
    right_high = lax.ppermute(from_right[split:], "grid", to_left)
    left_high = lax.ppermute(from_left[split:], "grid", to_right)
    right_low = lax.ppermute(from_right[:split], "grid", to_left)

    live = jnp.arange(cap, dtype=jnp.int32)[None, :] < a_count.reshape(groups, 1)
    row_code = jnp.where(live, a_rows.reshape(groups, cap) + 1, 0)
    meta = jnp.concatenate([row_code, a_cols.reshape(groups, cap)], axis=1)
    meta = jnp.pad(meta.astype(jnp.bfloat16)[:, None, :], ((0, 0), (0, META - 1), (0, bs - 2 * cap)))
    message = pack(a_slots.reshape(groups, cap * bs, bs), meta)
    landed = lax.all_to_all(message, "grid", split_axis=0, concat_axis=0, tiled=True)
    (landed,) = after([landed], early[1:3])
    parts = across_row(landed, columns)

    metas = jnp.stack([p[:, cap * bs, : 2 * cap] for p in parts]).astype(jnp.int32)
    code, col = metas[..., :cap], metas[..., cap:]
    hit = code[..., None] == owned_rows.reshape(rb) + 1
    row = jnp.sum(jnp.where(hit, jnp.arange(rb, dtype=jnp.int32), 0), axis=-1)
    pos = ring_place(lax.axis_index("grid"), groups)
    ahead = (ring_place(col // blocks, groups) - pos + groups) % groups
    hops = jnp.minimum(ahead, groups - ahead)
    first = jnp.where(hops == 0, 0, 2 * hops - 1) + jnp.where((ahead > 0) & (ahead < half), 1, 0)
    dest = row * (blocks * groups) + first * blocks + col % blocks
    dest = jnp.where(jnp.any(hit, axis=-1), dest, -1)

    acc, late = first_product(dest, parts, early, rb * bs, 3 * k_local, bs, cap, n_local // 4)
    left_low, right_high = after([left_low, right_high], [acc])
    low = lax.ppermute(left_low, "grid", to_right)
    high = lax.ppermute(right_high, "grid", to_left)
    acc = add_product(late, 0, [left_low, left_high, right_low, right_high], acc, False)
    return add_product(late, 2, [low, high], acc, True)


def solution(mesh):
    in_specs = (
        P("grid", "blk", None, None, None, None),
        P("grid", "blk", None, None),
        P("grid", "blk", None, None),
        P("grid", "blk", None),
        P("grid", None),
        P("grid", "blk"),
    )
    out_specs = P("grid", "blk")
    return jax.shard_map(body, mesh=mesh, in_specs=in_specs, out_specs=out_specs, check_vma=False)
```

```python
import functools

import jax
import jax.numpy as jnp
from jax import lax
from jax.experimental import pallas as pl
from jax.experimental.pallas import tpu as pltpu
from jax.sharding import PartitionSpec as P

META = 16
QUARTERS = 4
VMEM_BYTES = 62 << 20


def ring_order(n):
    return list(range(0, n, 2)) + list(range(n - 1, 0, -2))


def ring_place(g, n):
    return jnp.where(g % 2 == 0, g // 2, n - 1 - g // 2)


def pack_kernel(slots_ref, meta_ref, message_ref):
    rows = slots_ref.shape[1]
    message_ref[:, :rows] = slots_ref[...]
    message_ref[:, rows:] = meta_ref[...]


def pack(slots, meta):
    groups, rows, width = slots.shape
    part = groups // 4
    return pl.pallas_call(
        pack_kernel,
        out_shape=jax.ShapeDtypeStruct((groups, rows + META, width), slots.dtype),
        grid=(groups // part,),
        in_specs=[
            pl.BlockSpec((part, rows, width), lambda i: (i, 0, 0)),
            pl.BlockSpec((part, META, width), lambda i: (i, 0, 0)),
        ],
        out_specs=pl.BlockSpec((part, rows + META, width), lambda i: (i, 0, 0)),
        compiler_params=pltpu.CompilerParams(vmem_limit_bytes=VMEM_BYTES),
        cost_estimate=pl.CostEstimate(
            flops=0, bytes_accessed=slots.size * 4, transcendentals=0
        ),
    )(slots, meta)


def after_kernel(*refs):
    pass


def after(values, others):
    anywhere = pl.BlockSpec(memory_space=pl.ANY)
    return pl.pallas_call(
        after_kernel,
        out_shape=[jax.ShapeDtypeStruct(v.shape, v.dtype) for v in values],
        in_specs=[anywhere] * (len(values) + len(others)),
        out_specs=[anywhere] * len(values),
        input_output_aliases={i: i for i in range(len(values))},
        compiler_params=pltpu.CompilerParams(vmem_limit_bytes=VMEM_BYTES),
        cost_estimate=pl.CostEstimate(flops=0, bytes_accessed=0, transcendentals=0),
    )(*values, *others)


def first_kernel(depths, per_part, cap, bs, n_parts, dest_ref, *refs):
    parts = refs[:n_parts]
    rights = refs[n_parts : n_parts + len(depths)]
    refs = refs[n_parts + len(depths) :]
    accs_hbm, late_hbm = refs[:QUARTERS], refs[QUARTERS]
    left, right, acc, right_sem, acc_sem, late_sem = refs[QUARTERS + 1 :]
    inner, bn = right.shape[0], acc.shape[-1]
    at, fetches = 0, []
    for i, (depth, source) in enumerate(zip(depths, rights)):
        fetches.append(
            pltpu.make_async_copy(source, right.at[pl.ds(at, depth)], right_sem.at[i])
        )
        at += depth
    for fetch in fetches:
        fetch.start()
    left[...] = jnp.zeros_like(left)
    k_blocks = left.shape[1] // bs
    for q, part in enumerate(parts):

        def place(i, carry):
            for c in range(cap):
                dest = dest_ref[q, i, c]

                @pl.when(dest >= 0)
                def _():
                    row, col = dest // k_blocks, dest % k_blocks
                    left[
                        pl.ds(pl.multiple_of(row * bs, bs), bs),
                        pl.ds(pl.multiple_of(col * bs, bs), bs),
                    ] = part[i, pl.ds(c * bs, bs), :]

            return carry

        lax.fori_loop(0, per_part, place, 0)
    some = left.shape[0] // QUARTERS
    stores = [
        pltpu.make_async_copy(
            left.at[pl.ds(q * some, some), pl.ds(inner, late_hbm.shape[1])],
            late_hbm.at[pl.ds(q * some, some)],
            late_sem.at[q],
        )
        for q in range(QUARTERS)
    ]
    for store in stores:
        store.start()
    for fetch in fetches:
        fetch.wait()
    for j in range(acc.shape[0]):
        acc[j] = jnp.dot(
            left[:, :inner],
            right[:, j * bn : (j + 1) * bn],
            preferred_element_type=jnp.float32,
        )
        for q in range(QUARTERS):
            store = pltpu.make_async_copy(
                acc.at[j, pl.ds(q * some, some)], accs_hbm[q].at[j], acc_sem.at[j, q]
            )
            store.start()
            stores.append(store)
    for store in stores:
        store.wait()


def first_product(dest, parts, rights, rows, late_width, bs, cap, bn):
    depths = [right.shape[0] for right in rights]
    cols = rights[0].shape[1]
    inner, steps = sum(depths), cols // bn
    anywhere = pl.BlockSpec(memory_space=pl.ANY)
    out = pl.pallas_call(
        functools.partial(first_kernel, depths, parts[0].shape[0], cap, bs, len(parts)),
        out_shape=[jax.ShapeDtypeStruct((steps, rows // QUARTERS, bn), jnp.float32)] * QUARTERS
        + [jax.ShapeDtypeStruct((rows, late_width), jnp.bfloat16)],
        in_specs=[pl.BlockSpec(memory_space=pltpu.SMEM)]
        + [pl.BlockSpec(memory_space=pltpu.VMEM)] * len(parts)
        + [anywhere] * len(rights),
        out_specs=[anywhere] * (QUARTERS + 1),
        scratch_shapes=[
            pltpu.VMEM((rows, inner + late_width), jnp.bfloat16),
            pltpu.VMEM((inner, cols), jnp.bfloat16),
            pltpu.VMEM((steps, rows, bn), jnp.float32),
            pltpu.SemaphoreType.DMA((len(rights),)),
            pltpu.SemaphoreType.DMA((steps, QUARTERS)),
            pltpu.SemaphoreType.DMA((QUARTERS,)),
        ],
        compiler_params=pltpu.CompilerParams(vmem_limit_bytes=VMEM_BYTES),
        cost_estimate=pl.CostEstimate(
            flops=2 * rows * inner * cols,
            bytes_accessed=inner * cols * 2 + rows * cols * 4,
            transcendentals=0,
        ),
    )(dest, *parts, *rights)
    return list(out[:QUARTERS]), out[QUARTERS]


def add_kernel(depths, *refs):
    lefts, accs = refs[:QUARTERS], refs[QUARTERS : 2 * QUARTERS]
    refs = refs[2 * QUARTERS :]
    pieces, outs, (right, sems) = refs[: len(depths)], refs[len(depths) : -2], refs[-2:]
    j = pl.program_id(0)
    steps, _, bn = right.shape

    def fetch(chunk):
        at = 0
        copies = []
        for i, (depth, piece) in enumerate(zip(depths, pieces)):
            copies.append(
                pltpu.make_async_copy(
                    piece.at[:, pl.ds(chunk * bn, bn)],
                    right.at[chunk, pl.ds(at, depth)],
                    sems.at[chunk, i],
                )
            )
            at += depth
        return copies

    @pl.when(j == 0)
    def _():
        for chunk in range(steps):
            for copy in fetch(chunk):
                copy.start()

    for chunk in range(steps):

        @pl.when(j == chunk)
        def _():
            for copy in fetch(chunk):
                copy.wait()

    left = jnp.concatenate([ref[...] for ref in lefts], axis=0)
    total = jnp.dot(left, right[j], preferred_element_type=jnp.float32)
    some = total.shape[0] // QUARTERS
    for q, acc in enumerate(accs):
        part = acc[0] + total[q * some : (q + 1) * some]
        if len(outs) == 1:
            outs[0][q * some : (q + 1) * some] = part.astype(outs[0].dtype)
        else:
            outs[q][0] = part


def add_product(left, place, pieces, accs, last):
    steps, some, bn = accs[0].shape
    rows = some * QUARTERS
    depths = [piece.shape[0] for piece in pieces]
    inner = sum(depths)
    acc_spec = pl.BlockSpec((1, some, bn), lambda j: (j, 0, 0))
    if last:
        out_specs = pl.BlockSpec((rows, bn), lambda j: (0, j))
        out_shape = jax.ShapeDtypeStruct((rows, steps * bn), jnp.bfloat16)
    else:
        out_specs = [acc_spec] * QUARTERS
        out_shape = [jax.ShapeDtypeStruct(accs[0].shape, accs[0].dtype)] * QUARTERS
    return pl.pallas_call(
        functools.partial(add_kernel, depths),
        out_shape=out_shape,
        grid=(steps,),
        in_specs=[
            pl.BlockSpec((some, inner), functools.partial(lambda q, j: (q, place), q))
            for q in range(QUARTERS)
        ]
        + [acc_spec] * QUARTERS
        + [pl.BlockSpec(memory_space=pl.ANY)] * len(pieces),
        out_specs=out_specs,
        scratch_shapes=[
            pltpu.VMEM((steps, inner, bn), jnp.bfloat16),
            pltpu.SemaphoreType.DMA((steps, len(pieces))),
        ],
        compiler_params=pltpu.CompilerParams(vmem_limit_bytes=VMEM_BYTES),
        cost_estimate=pl.CostEstimate(
            flops=2 * rows * inner * steps * bn,
            bytes_accessed=(rows + steps * bn) * inner * 2 + rows * steps * bn * 8,
            transcendentals=0,
        ),
    )(*[left] * QUARTERS, *accs, *pieces)


def across_row(landed, columns):
    if columns != 4:
        gathered = lax.all_gather(landed, "blk", axis=0)
        return [gathered[j] for j in range(columns)]
    swap_core = [(j, j ^ 1) for j in range(columns)]
    swap_chip = [(j, j ^ 2) for j in range(columns)]
    across = lax.ppermute(landed, "blk", swap_chip)
    near = lax.ppermute(landed, "blk", swap_core)
    return [landed, across, near, lax.ppermute(across, "blk", swap_core)]


def body(a_slots, a_rows, a_cols, a_count, owned_rows, b_matrix):
    groups = lax.axis_size("grid")
    columns = lax.axis_size("blk")
    bs = a_slots.shape[-1]
    cap = a_slots.shape[3]
    rb = owned_rows.shape[-1]
    k_local, n_local = b_matrix.shape
    blocks = k_local // bs
    half = groups // 2

    order = ring_order(groups)
    to_right = [(order[i], order[(i + 1) % groups]) for i in range(groups)]
    to_left = [(order[(i + 1) % groups], order[i]) for i in range(groups)]
    split = k_local // 2
    from_left = lax.ppermute(b_matrix, "grid", to_right)
    from_right = lax.ppermute(b_matrix, "grid", to_left)
    steps = [[b_matrix], [from_left, from_right]]
    left_low, left_high = from_left[:split], from_left[split:]
    right_low, right_high = from_right[:split], from_right[split:]
    for s in range(2, half):
        left_low = lax.ppermute(left_low, "grid", to_right)
        right_high = lax.ppermute(right_high, "grid", to_left)
        left_high = lax.ppermute(left_high, "grid", to_right)
        right_low = lax.ppermute(right_low, "grid", to_left)
        steps.append([left_low, left_high, right_low, right_high])
    early = sum(steps[:-1], [])

    live = jnp.arange(cap, dtype=jnp.int32)[None, :] < a_count.reshape(groups, 1)
    row_code = jnp.where(live, a_rows.reshape(groups, cap) + 1, 0)
    meta = jnp.concatenate([row_code, a_cols.reshape(groups, cap)], axis=1)
    meta = jnp.pad(meta.astype(jnp.bfloat16)[:, None, :], ((0, 0), (0, META - 1), (0, bs - 2 * cap)))
    message = pack(a_slots.reshape(groups, cap * bs, bs), meta)
    landed = lax.all_to_all(message, "grid", split_axis=0, concat_axis=0, tiled=True)
    (landed,) = after([landed], [steps[2][0], steps[2][3]])
    parts = across_row(landed, columns)

    metas = jnp.stack([p[:, cap * bs, : 2 * cap] for p in parts]).astype(jnp.int32)
    code, col = metas[..., :cap], metas[..., cap:]
    hit = code[..., None] == owned_rows.reshape(rb) + 1
    row = jnp.sum(jnp.where(hit, jnp.arange(rb, dtype=jnp.int32), 0), axis=-1)
    pos = ring_place(lax.axis_index("grid"), groups)
    ahead = (ring_place(col // blocks, groups) - pos + groups) % groups
    hops = jnp.minimum(ahead, groups - ahead)
    first = jnp.where(hops == 0, 0, 2 * hops - 1) + jnp.where((ahead > 0) & (ahead < half), 1, 0)
    dest = row * (blocks * groups) + first * blocks + col % blocks
    dest = jnp.where(jnp.any(hit, axis=-1), dest, -1)

    accs, late = first_product(dest, parts, early, rb * bs, 3 * k_local, bs, cap, n_local // 4)
    left_low, right_high = after([left_low, right_high], [late])
    low = lax.ppermute(left_low, "grid", to_right)
    high = lax.ppermute(right_high, "grid", to_left)
    accs = add_product(late, 0, [left_low, left_high, right_low, right_high], accs, False)
    return add_product(late, 2, [low, high], accs, True)


def solution(mesh):
    in_specs = (
        P("grid", "blk", None, None, None, None),
        P("grid", "blk", None, None),
        P("grid", "blk", None, None),
        P("grid", "blk", None),
        P("grid", None),
        P("grid", "blk"),
    )
    out_specs = P("grid", "blk")
    return jax.shard_map(body, mesh=mesh, in_specs=in_specs, out_specs=out_specs, check_vma=False)
```

```python
import functools

import jax
import jax.numpy as jnp
from jax import lax
from jax.experimental import pallas as pl
from jax.experimental.pallas import tpu as pltpu
from jax.sharding import PartitionSpec as P

META = 16
PARTS = 4
VMEM_BYTES = 62 << 20


def ring_order(n):
    return list(range(0, n, 2)) + list(range(n - 1, 0, -2))


def ring_place(g, n):
    return jnp.where(g % 2 == 0, g // 2, n - 1 - g // 2)


def pack_kernel(slots_ref, meta_ref, message_ref):
    rows = slots_ref.shape[1]
    message_ref[:, :rows] = slots_ref[...]
    message_ref[:, rows:] = meta_ref[...]


def pack(slots, meta):
    groups, rows, width = slots.shape
    part = groups // 4
    return pl.pallas_call(
        pack_kernel,
        out_shape=jax.ShapeDtypeStruct((groups, rows + META, width), slots.dtype),
        grid=(groups // part,),
        in_specs=[
            pl.BlockSpec((part, rows, width), lambda i: (i, 0, 0)),
            pl.BlockSpec((part, META, width), lambda i: (i, 0, 0)),
        ],
        out_specs=pl.BlockSpec((part, rows + META, width), lambda i: (i, 0, 0)),
        compiler_params=pltpu.CompilerParams(vmem_limit_bytes=VMEM_BYTES),
        cost_estimate=pl.CostEstimate(
            flops=0, bytes_accessed=slots.size * 4, transcendentals=0
        ),
    )(slots, meta)


def after_kernel(*refs):
    pass


def after(values, others):
    anywhere = pl.BlockSpec(memory_space=pl.ANY)
    return pl.pallas_call(
        after_kernel,
        out_shape=[jax.ShapeDtypeStruct(v.shape, v.dtype) for v in values],
        in_specs=[anywhere] * (len(values) + len(others)),
        out_specs=[anywhere] * len(values),
        input_output_aliases={i: i for i in range(len(values))},
        compiler_params=pltpu.CompilerParams(vmem_limit_bytes=VMEM_BYTES),
        cost_estimate=pl.CostEstimate(flops=0, bytes_accessed=0, transcendentals=0),
    )(*values, *others)


def first_kernel(depths, per_part, cap, bs, n_parts, dest_ref, *refs):
    parts = refs[:n_parts]
    rights = refs[n_parts : n_parts + len(depths)]
    refs = refs[n_parts + len(depths) :]
    acc_hbm, late_hbm, left, right, acc, right_sem, acc_sem, late_sem = refs
    inner, bn = right.shape[0], acc.shape[-1]
    at, fetches = 0, []
    for i, (depth, source) in enumerate(zip(depths, rights)):
        fetches.append(
            pltpu.make_async_copy(source, right.at[pl.ds(at, depth)], right_sem.at[i])
        )
        at += depth
    for fetch in fetches:
        fetch.start()
    left[...] = jnp.zeros_like(left)
    k_blocks = left.shape[1] // bs
    for q, part in enumerate(parts):

        def place(i, carry):
            for c in range(cap):
                dest = dest_ref[q, i, c]

                @pl.when(dest >= 0)
                def _():
                    row, col = dest // k_blocks, dest % k_blocks
                    left[
                        pl.ds(pl.multiple_of(row * bs, bs), bs),
                        pl.ds(pl.multiple_of(col * bs, bs), bs),
                    ] = part[i, pl.ds(c * bs, bs), :]

            return carry

        lax.fori_loop(0, per_part, place, 0)
    some = left.shape[0] // PARTS
    stores = [
        pltpu.make_async_copy(
            left.at[pl.ds(q * some, some), pl.ds(inner, late_hbm.shape[1])],
            late_hbm.at[pl.ds(q * some, some)],
            late_sem.at[q],
        )
        for q in range(PARTS)
    ]
    for store in stores:
        store.start()
    for fetch in fetches:
        fetch.wait()
    for j in range(acc.shape[0]):
        acc[j] = jnp.dot(
            left[:, :inner],
            right[:, j * bn : (j + 1) * bn],
            preferred_element_type=jnp.float32,
        )
        store = pltpu.make_async_copy(acc.at[j], acc_hbm.at[j], acc_sem.at[j])
        store.start()
        stores.append(store)
    for store in stores:
        store.wait()


def first_product(dest, parts, rights, rows, late_width, bs, cap, bn):
    depths = [right.shape[0] for right in rights]
    cols = rights[0].shape[1]
    inner, steps = sum(depths), cols // bn
    anywhere = pl.BlockSpec(memory_space=pl.ANY)
    return pl.pallas_call(
        functools.partial(first_kernel, depths, parts[0].shape[0], cap, bs, len(parts)),
        out_shape=[
            jax.ShapeDtypeStruct((steps, rows, bn), jnp.float32),
            jax.ShapeDtypeStruct((rows, late_width), jnp.bfloat16),
        ],
        in_specs=[pl.BlockSpec(memory_space=pltpu.SMEM)]
        + [pl.BlockSpec(memory_space=pltpu.VMEM)] * len(parts)
        + [anywhere] * len(rights),
        out_specs=[anywhere] * 2,
        scratch_shapes=[
            pltpu.VMEM((rows, inner + late_width), jnp.bfloat16),
            pltpu.VMEM((inner, cols), jnp.bfloat16),
            pltpu.VMEM((steps, rows, bn), jnp.float32),
            pltpu.SemaphoreType.DMA((len(rights),)),
            pltpu.SemaphoreType.DMA((steps,)),
            pltpu.SemaphoreType.DMA((PARTS,)),
        ],
        compiler_params=pltpu.CompilerParams(vmem_limit_bytes=VMEM_BYTES),
        cost_estimate=pl.CostEstimate(
            flops=2 * rows * inner * cols,
            bytes_accessed=inner * cols * 2 + rows * cols * 4,
            transcendentals=0,
        ),
    )(dest, *parts, *rights)


def add_kernel(depths, place, late_hbm, acc_hbm, *refs):
    pieces = refs[: len(depths)]
    out_hbm, left, right, acc, out, left_sem, right_sem, acc_sem, out_sem = refs[len(depths) :]
    steps, rows, bn = acc.shape
    inner = left.shape[1]
    some = rows // PARTS
    left_copies = [
        pltpu.make_async_copy(
            late_hbm.at[pl.ds(q * some, some), pl.ds(place, inner)],
            left.at[pl.ds(q * some, some)],
            left_sem.at[q],
        )
        for q in range(PARTS)
    ]
    for copy in left_copies:
        copy.start()
    chunks = []
    for j in range(steps):
        copies, at = [], 0
        for i, (depth, piece) in enumerate(zip(depths, pieces)):
            copies.append(
                pltpu.make_async_copy(
                    piece.at[:, pl.ds(j * bn, bn)],
                    right.at[j, pl.ds(at, depth)],
                    right_sem.at[j, i],
                )
            )
            at += depth
        copies.append(pltpu.make_async_copy(acc_hbm.at[j], acc.at[j], acc_sem.at[j]))
        for copy in copies:
            copy.start()
        chunks.append(copies)
    for copy in left_copies:
        copy.wait()
    stores = []
    for j in range(steps):
        for copy in chunks[j]:
            copy.wait()
        total = jnp.dot(left[...], right[j], preferred_element_type=jnp.float32)
        out[j] = (acc[j] + total).astype(out.dtype)
        if len(out_hbm.shape) == 2:
            target = out_hbm.at[:, pl.ds(j * bn, bn)]
        else:
            target = out_hbm.at[j]
        store = pltpu.make_async_copy(out.at[j], target, out_sem.at[j])
        store.start()
        stores.append(store)
    for store in stores:
        store.wait()


def add_product(late, place, pieces, acc, last):
    steps, rows, bn = acc.shape
    depths = [piece.shape[0] for piece in pieces]
    inner = sum(depths)
    anywhere = pl.BlockSpec(memory_space=pl.ANY)
    if last:
        out_shape = jax.ShapeDtypeStruct((rows, steps * bn), jnp.bfloat16)
    else:
        out_shape = jax.ShapeDtypeStruct(acc.shape, acc.dtype)
    return pl.pallas_call(
        functools.partial(add_kernel, depths, place),
        out_shape=out_shape,
        in_specs=[anywhere] * (2 + len(pieces)),
        out_specs=anywhere,
        scratch_shapes=[
            pltpu.VMEM((rows, inner), jnp.bfloat16),
            pltpu.VMEM((steps, inner, bn), jnp.bfloat16),
            pltpu.VMEM((steps, rows, bn), jnp.float32),
            pltpu.VMEM((steps, rows, bn), out_shape.dtype),
            pltpu.SemaphoreType.DMA((PARTS,)),
            pltpu.SemaphoreType.DMA((steps, len(pieces))),
            pltpu.SemaphoreType.DMA((steps,)),
            pltpu.SemaphoreType.DMA((steps,)),
        ],
        compiler_params=pltpu.CompilerParams(vmem_limit_bytes=VMEM_BYTES),
        cost_estimate=pl.CostEstimate(
            flops=2 * rows * inner * steps * bn,
            bytes_accessed=(rows + steps * bn) * inner * 2 + rows * steps * bn * 8,
            transcendentals=0,
        ),
    )(late, acc, *pieces)


def rest_kernel(start, block_hbm, _, out_hbm, held, in_sem, out_sem):
    some = held.shape[0] // PARTS
    loads, stores = [], []
    for q in range(PARTS):
        rows = pl.ds(q * some, some)
        source = block_hbm.at[pl.ds(start + q * some, some)]
        loads.append(pltpu.make_async_copy(source, held.at[rows], in_sem.at[q]))
        stores.append(pltpu.make_async_copy(held.at[rows], out_hbm.at[rows], out_sem.at[q]))
    for load in loads:
        load.start()
    for load, store in zip(loads, stores):
        load.wait()
        store.start()
    for store in stores:
        store.wait()


def rest(block, start, size, ahead):
    anywhere = pl.BlockSpec(memory_space=pl.ANY)
    shape = (size, block.shape[1])
    return pl.pallas_call(
        functools.partial(rest_kernel, start),
        out_shape=jax.ShapeDtypeStruct(shape, block.dtype),
        in_specs=[anywhere] * 2,
        out_specs=anywhere,
        scratch_shapes=[
            pltpu.VMEM(shape, block.dtype),
            pltpu.SemaphoreType.DMA((PARTS,)),
            pltpu.SemaphoreType.DMA((PARTS,)),
        ],
        compiler_params=pltpu.CompilerParams(vmem_limit_bytes=VMEM_BYTES),
        cost_estimate=pl.CostEstimate(
            flops=0, bytes_accessed=size * block.shape[1] * 4, transcendentals=0
        ),
    )(block, ahead)


def across_row(landed, columns):
    if columns != 4:
        gathered = lax.all_gather(landed, "blk", axis=0)
        return [gathered[j] for j in range(columns)]
    swap_core = [(j, j ^ 1) for j in range(columns)]
    swap_chip = [(j, j ^ 2) for j in range(columns)]
    across = lax.ppermute(landed, "blk", swap_chip)
    near = lax.ppermute(landed, "blk", swap_core)
    return [landed, across, near, lax.ppermute(across, "blk", swap_core)]


def body(a_slots, a_rows, a_cols, a_count, owned_rows, b_matrix):
    groups = lax.axis_size("grid")
    columns = lax.axis_size("blk")
    bs = a_slots.shape[-1]
    cap = a_slots.shape[3]
    rb = owned_rows.shape[-1]
    k_local, n_local = b_matrix.shape
    blocks = k_local // bs
    half = groups // 2

    order = ring_order(groups)
    to_right = [(order[i], order[(i + 1) % groups]) for i in range(groups)]
    to_left = [(order[(i + 1) % groups], order[i]) for i in range(groups)]
    from_left, from_right, early = b_matrix, b_matrix, [b_matrix]
    for s in range(1, half - 1):
        from_left = lax.ppermute(from_left, "grid", to_right)
        from_right = lax.ppermute(from_right, "grid", to_left)
        early += [from_left, from_right]
    split = k_local // 2
    left_low, right_high = from_left[:split], from_right[split:]
    left_high = rest(from_left, split, split, left_low)
    right_low = rest(from_right, 0, split, right_high)
    left_low = lax.ppermute(left_low, "grid", to_right)
    right_high = lax.ppermute(right_high, "grid", to_left)
    left_high = lax.ppermute(left_high, "grid", to_right)
    right_low = lax.ppermute(right_low, "grid", to_left)

    live = jnp.arange(cap, dtype=jnp.int32)[None, :] < a_count.reshape(groups, 1)
    row_code = jnp.where(live, a_rows.reshape(groups, cap) + 1, 0)
    meta = jnp.concatenate([row_code, a_cols.reshape(groups, cap)], axis=1)
    meta = jnp.pad(meta.astype(jnp.bfloat16)[:, None, :], ((0, 0), (0, META - 1), (0, bs - 2 * cap)))
    message = pack(a_slots.reshape(groups, cap * bs, bs), meta)
    landed = lax.all_to_all(message, "grid", split_axis=0, concat_axis=0, tiled=True)
    (landed,) = after([landed], early[1:3])
    parts = across_row(landed, columns)

    metas = jnp.stack([p[:, cap * bs, : 2 * cap] for p in parts]).astype(jnp.int32)
    code, col = metas[..., :cap], metas[..., cap:]
    hit = code[..., None] == owned_rows.reshape(rb) + 1
    row = jnp.sum(jnp.where(hit, jnp.arange(rb, dtype=jnp.int32), 0), axis=-1)
    pos = ring_place(lax.axis_index("grid"), groups)
    ahead = (ring_place(col // blocks, groups) - pos + groups) % groups
    hops = jnp.minimum(ahead, groups - ahead)
    first = jnp.where(hops == 0, 0, 2 * hops - 1) + jnp.where((ahead > 0) & (ahead < half), 1, 0)
    dest = row * (blocks * groups) + first * blocks + col % blocks
    dest = jnp.where(jnp.any(hit, axis=-1), dest, -1)

    acc, late = first_product(dest, parts, early, rb * bs, 3 * k_local, bs, cap, n_local // 4)
    left_low, right_high = after([left_low, right_high], [late])
    low = lax.ppermute(left_low, "grid", to_right)
    high = lax.ppermute(right_high, "grid", to_left)
    acc = add_product(late, 0, [left_low, left_high, right_low, right_high], acc, False)
    return add_product(late, 2 * k_local, [low, high], acc, True)


def solution(mesh):
    in_specs = (
        P("grid", "blk", None, None, None, None),
        P("grid", "blk", None, None),
        P("grid", "blk", None, None),
        P("grid", "blk", None),
        P("grid", None),
        P("grid", "blk"),
    )
    out_specs = P("grid", "blk")
    return jax.shard_map(body, mesh=mesh, in_specs=in_specs, out_specs=out_specs, check_vma=False)
```

```python
import functools

import jax
import jax.numpy as jnp
from jax import lax
from jax.experimental import pallas as pl
from jax.experimental.pallas import tpu as pltpu
from jax.sharding import PartitionSpec as P

META = 16
PARTS = 4
CLEAR = 32
VMEM_BYTES = 62 << 20


def ring_order(n):
    return list(range(0, n, 2)) + list(range(n - 1, 0, -2))


def ring_place(g, n):
    return jnp.where(g % 2 == 0, g // 2, n - 1 - g // 2)


def pack_kernel(slots_ref, meta_ref, message_ref):
    rows = slots_ref.shape[1]
    message_ref[:, :rows] = slots_ref[...]
    message_ref[:, rows:] = meta_ref[...]


def pack(slots, meta):
    groups, rows, width = slots.shape
    part = groups // 4
    return pl.pallas_call(
        pack_kernel,
        out_shape=jax.ShapeDtypeStruct((groups, rows + META, width), slots.dtype),
        grid=(groups // part,),
        in_specs=[
            pl.BlockSpec((part, rows, width), lambda i: (i, 0, 0)),
            pl.BlockSpec((part, META, width), lambda i: (i, 0, 0)),
        ],
        out_specs=pl.BlockSpec((part, rows + META, width), lambda i: (i, 0, 0)),
        compiler_params=pltpu.CompilerParams(vmem_limit_bytes=VMEM_BYTES),
        cost_estimate=pl.CostEstimate(
            flops=0, bytes_accessed=slots.size * 4, transcendentals=0
        ),
    )(slots, meta)


def after_kernel(*refs):
    pass


def after(values, others):
    anywhere = pl.BlockSpec(memory_space=pl.ANY)
    return pl.pallas_call(
        after_kernel,
        out_shape=[jax.ShapeDtypeStruct(v.shape, v.dtype) for v in values],
        in_specs=[anywhere] * (len(values) + len(others)),
        out_specs=[anywhere] * len(values),
        input_output_aliases={i: i for i in range(len(values))},
        compiler_params=pltpu.CompilerParams(vmem_limit_bytes=VMEM_BYTES),
        cost_estimate=pl.CostEstimate(flops=0, bytes_accessed=0, transcendentals=0),
    )(*values, *others)


def first_kernel(depths, per_part, cap, bs, n_parts, dest_ref, *refs):
    parts = refs[:n_parts]
    rights = refs[n_parts : n_parts + len(depths)]
    refs = refs[n_parts + len(depths) :]
    acc_hbm, late_hbm, left, right, acc, right_sem, acc_sem, late_sem = refs
    inner, bn = right.shape[0], acc.shape[-1]
    at, fetches = 0, []
    for i, (depth, source) in enumerate(zip(depths, rights)):
        fetches.append(
            pltpu.make_async_copy(source, right.at[pl.ds(at, depth)], right_sem.at[i])
        )
        at += depth
    for fetch in fetches:
        fetch.start()
    some = left.shape[0] // PARTS

    def clear(i, carry):
        rows = pl.ds(pl.multiple_of(i * CLEAR, CLEAR), CLEAR)
        left[rows] = jnp.zeros((CLEAR, left.shape[1]), left.dtype)
        return carry

    lax.fori_loop(0, left.shape[0] // CLEAR, clear, 0)
    k_blocks = left.shape[1] // bs
    for q, part in enumerate(parts):

        def place(i, carry):
            for c in range(cap):
                dest = dest_ref[q, i, c]

                @pl.when(dest >= 0)
                def _():
                    row, col = dest // k_blocks, dest % k_blocks
                    left[
                        pl.ds(pl.multiple_of(row * bs, bs), bs),
                        pl.ds(pl.multiple_of(col * bs, bs), bs),
                    ] = part[i, pl.ds(c * bs, bs), :]

            return carry

        lax.fori_loop(0, per_part, place, 0)
    stores = [
        pltpu.make_async_copy(
            left.at[pl.ds(q * some, some), pl.ds(inner, late_hbm.shape[1])],
            late_hbm.at[pl.ds(q * some, some)],
            late_sem.at[q],
        )
        for q in range(PARTS)
    ]
    for store in stores:
        store.start()
    for fetch in fetches:
        fetch.wait()

    def multiply(j, carry):
        cols = pl.ds(pl.multiple_of(j * bn, bn), bn)

        def turn(q, inner_carry):
            rows = pl.ds(pl.multiple_of(q * some, some), some)
            acc[j, rows] = jnp.dot(
                left[rows, :inner], right[:, cols], preferred_element_type=jnp.float32
            )
            return inner_carry

        lax.fori_loop(0, PARTS, turn, 0)
        pltpu.make_async_copy(acc.at[j], acc_hbm.at[j], acc_sem.at[j]).start()
        return carry

    lax.fori_loop(0, acc.shape[0], multiply, 0)
    for j in range(acc.shape[0]):
        pltpu.make_async_copy(acc.at[j], acc_hbm.at[j], acc_sem.at[j]).wait()
    for store in stores:
        store.wait()


def first_product(dest, parts, rights, rows, late_width, bs, cap, bn):
    depths = [right.shape[0] for right in rights]
    cols = rights[0].shape[1]
    inner, steps = sum(depths), cols // bn
    anywhere = pl.BlockSpec(memory_space=pl.ANY)
    return pl.pallas_call(
        functools.partial(first_kernel, depths, parts[0].shape[0], cap, bs, len(parts)),
        out_shape=[
            jax.ShapeDtypeStruct((steps, rows, bn), jnp.float32),
            jax.ShapeDtypeStruct((rows, late_width), jnp.bfloat16),
        ],
        in_specs=[pl.BlockSpec(memory_space=pltpu.SMEM)]
        + [pl.BlockSpec(memory_space=pltpu.VMEM)] * len(parts)
        + [anywhere] * len(rights),
        out_specs=[anywhere] * 2,
        scratch_shapes=[
            pltpu.VMEM((rows, inner + late_width), jnp.bfloat16),
            pltpu.VMEM((inner, cols), jnp.bfloat16),
            pltpu.VMEM((steps, rows, bn), jnp.float32),
            pltpu.SemaphoreType.DMA((len(rights),)),
            pltpu.SemaphoreType.DMA((steps,)),
            pltpu.SemaphoreType.DMA((PARTS,)),
        ],
        compiler_params=pltpu.CompilerParams(vmem_limit_bytes=VMEM_BYTES),
        cost_estimate=pl.CostEstimate(
            flops=2 * rows * inner * cols,
            bytes_accessed=inner * cols * 2 + rows * cols * 4,
            transcendentals=0,
        ),
    )(dest, *parts, *rights)


def add_kernel(depths, place, late_hbm, acc_hbm, *refs):
    pieces = refs[: len(depths)]
    out_hbm, left, right, acc, out, left_sem, right_sem, acc_sem, out_sem = refs[len(depths) :]
    steps, rows, bn = acc.shape
    inner = left.shape[1]
    some = rows // PARTS

    def fetch_left(q):
        part = pl.ds(pl.multiple_of(q * some, some), some)
        source = late_hbm.at[part, pl.ds(place, inner)]
        return pltpu.make_async_copy(source, left.at[part], left_sem.at[q])

    def fetch(j):
        cols = pl.ds(pl.multiple_of(j * bn, bn), bn)
        copies, at = [pltpu.make_async_copy(acc_hbm.at[j], acc.at[j], acc_sem.at[j])], 0
        for i, (depth, piece) in enumerate(zip(depths, pieces)):
            target = right.at[j, pl.ds(at, depth)]
            copies.append(pltpu.make_async_copy(piece.at[:, cols], target, right_sem.at[j, i]))
            at += depth
        return copies

    def store(j):
        if len(out_hbm.shape) == 2:
            target = out_hbm.at[:, pl.ds(pl.multiple_of(j * bn, bn), bn)]
        else:
            target = out_hbm.at[j]
        return pltpu.make_async_copy(out.at[j], target, out_sem.at[j])

    def each(count, act):
        def step(i, carry):
            act(i)
            return carry

        lax.fori_loop(0, count, step, 0)

    each(PARTS, lambda q: fetch_left(q).start())
    each(steps, lambda j: [copy.start() for copy in fetch(j)])
    each(PARTS, lambda q: fetch_left(q).wait())

    def multiply(j):
        for copy in fetch(j):
            copy.wait()

        def turn(q):
            part = pl.ds(pl.multiple_of(q * some, some), some)
            total = jnp.dot(left[part], right[j], preferred_element_type=jnp.float32)
            out[j, part] = (acc[j, part] + total).astype(out.dtype)

        each(PARTS, turn)
        store(j).start()

    each(steps, multiply)
    each(steps, lambda j: store(j).wait())


def add_product(late, place, pieces, acc, last):
    steps, rows, bn = acc.shape
    depths = [piece.shape[0] for piece in pieces]
    inner = sum(depths)
    anywhere = pl.BlockSpec(memory_space=pl.ANY)
    if last:
        out_shape = jax.ShapeDtypeStruct((rows, steps * bn), jnp.bfloat16)
    else:
        out_shape = jax.ShapeDtypeStruct(acc.shape, acc.dtype)
    return pl.pallas_call(
        functools.partial(add_kernel, depths, place),
        out_shape=out_shape,
        in_specs=[anywhere] * (2 + len(pieces)),
        out_specs=anywhere,
        scratch_shapes=[
            pltpu.VMEM((rows, inner), jnp.bfloat16),
            pltpu.VMEM((steps, inner, bn), jnp.bfloat16),
            pltpu.VMEM((steps, rows, bn), jnp.float32),
            pltpu.VMEM((steps, rows, bn), out_shape.dtype),
            pltpu.SemaphoreType.DMA((PARTS,)),
            pltpu.SemaphoreType.DMA((steps, len(pieces))),
            pltpu.SemaphoreType.DMA((steps,)),
            pltpu.SemaphoreType.DMA((steps,)),
        ],
        compiler_params=pltpu.CompilerParams(vmem_limit_bytes=VMEM_BYTES),
        cost_estimate=pl.CostEstimate(
            flops=2 * rows * inner * steps * bn,
            bytes_accessed=(rows + steps * bn) * inner * 2 + rows * steps * bn * 8,
            transcendentals=0,
        ),
    )(late, acc, *pieces)


def across_row(landed, columns):
    if columns != 4:
        gathered = lax.all_gather(landed, "blk", axis=0)
        return [gathered[j] for j in range(columns)]
    swap_core = [(j, j ^ 1) for j in range(columns)]
    swap_chip = [(j, j ^ 2) for j in range(columns)]
    across = lax.ppermute(landed, "blk", swap_chip)
    near = lax.ppermute(landed, "blk", swap_core)
    return [landed, across, near, lax.ppermute(across, "blk", swap_core)]


def body(a_slots, a_rows, a_cols, a_count, owned_rows, b_matrix):
    groups = lax.axis_size("grid")
    columns = lax.axis_size("blk")
    bs = a_slots.shape[-1]
    cap = a_slots.shape[3]
    rb = owned_rows.shape[-1]
    k_local, n_local = b_matrix.shape
    blocks = k_local // bs
    half = groups // 2

    order = ring_order(groups)
    to_right = [(order[i], order[(i + 1) % groups]) for i in range(groups)]
    to_left = [(order[(i + 1) % groups], order[i]) for i in range(groups)]
    from_left, from_right, early = b_matrix, b_matrix, [b_matrix]
    for s in range(1, half - 1):
        from_left = lax.ppermute(from_left, "grid", to_right)
        from_right = lax.ppermute(from_right, "grid", to_left)
        early += [from_left, from_right]
    split = k_local // 2
    left_low, right_high = from_left[:split], from_right[split:]
    left_high, right_low = from_left[split:], from_right[:split]
    left_low = lax.ppermute(left_low, "grid", to_right)
    right_high = lax.ppermute(right_high, "grid", to_left)
    left_high = lax.ppermute(left_high, "grid", to_right)
    right_low = lax.ppermute(right_low, "grid", to_left)

    live = jnp.arange(cap, dtype=jnp.int32)[None, :] < a_count.reshape(groups, 1)
    row_code = jnp.where(live, a_rows.reshape(groups, cap) + 1, 0)
    meta = jnp.concatenate([row_code, a_cols.reshape(groups, cap)], axis=1)
    meta = jnp.pad(meta.astype(jnp.bfloat16)[:, None, :], ((0, 0), (0, META - 1), (0, bs - 2 * cap)))
    message = pack(a_slots.reshape(groups, cap * bs, bs), meta)
    landed = lax.all_to_all(message, "grid", split_axis=0, concat_axis=0, tiled=True)
    (landed,) = after([landed], early[1:3])
    parts = across_row(landed, columns)

    metas = jnp.stack([p[:, cap * bs, : 2 * cap] for p in parts]).astype(jnp.int32)
    code, col = metas[..., :cap], metas[..., cap:]
    hit = code[..., None] == owned_rows.reshape(rb) + 1
    row = jnp.sum(jnp.where(hit, jnp.arange(rb, dtype=jnp.int32), 0), axis=-1)
    pos = ring_place(lax.axis_index("grid"), groups)
    ahead = (ring_place(col // blocks, groups) - pos + groups) % groups
    hops = jnp.minimum(ahead, groups - ahead)
    first = jnp.where(hops == 0, 0, 2 * hops - 1) + jnp.where((ahead > 0) & (ahead < half), 1, 0)
    dest = row * (blocks * groups) + first * blocks + col % blocks
    dest = jnp.where(jnp.any(hit, axis=-1), dest, -1)

    acc, late = first_product(dest, parts, early, rb * bs, 3 * k_local, bs, cap, n_local // 4)
    left_low, right_high = after([left_low, right_high], [late])
    low = lax.ppermute(left_low, "grid", to_right)
    high = lax.ppermute(right_high, "grid", to_left)
    acc = add_product(late, 0, [left_low, left_high, right_low, right_high], acc, False)
    return add_product(late, 2 * k_local, [low, high], acc, True)


def solution(mesh):
    in_specs = (
        P("grid", "blk", None, None, None, None),
        P("grid", "blk", None, None),
        P("grid", "blk", None, None),
        P("grid", "blk", None),
        P("grid", None),
        P("grid", "blk"),
    )
    out_specs = P("grid", "blk")
    return jax.shard_map(body, mesh=mesh, in_specs=in_specs, out_specs=out_specs, check_vma=False)
```

```python
import functools

import jax
import jax.numpy as jnp
from jax import lax
from jax.experimental import pallas as pl
from jax.experimental.pallas import tpu as pltpu
from jax.sharding import PartitionSpec as P

META = 16
PARTS = 4
CLEAR = 32
VMEM_BYTES = 62 << 20
SPARE_BYTES = 4 << 20


def ring_order(n):
    return list(range(0, n, 2)) + list(range(n - 1, 0, -2))


def ring_place(g, n):
    return jnp.where(g % 2 == 0, g // 2, n - 1 - g // 2)


def pack_kernel(slots_ref, meta_ref, message_ref):
    rows = slots_ref.shape[1]
    message_ref[:, :rows] = slots_ref[...]
    message_ref[:, rows:] = meta_ref[...]


def pack(slots, meta):
    groups, rows, width = slots.shape
    part = groups // 4
    return pl.pallas_call(
        pack_kernel,
        out_shape=jax.ShapeDtypeStruct((groups, rows + META, width), slots.dtype),
        grid=(groups // part,),
        in_specs=[
            pl.BlockSpec((part, rows, width), lambda i: (i, 0, 0)),
            pl.BlockSpec((part, META, width), lambda i: (i, 0, 0)),
        ],
        out_specs=pl.BlockSpec((part, rows + META, width), lambda i: (i, 0, 0)),
        compiler_params=pltpu.CompilerParams(vmem_limit_bytes=VMEM_BYTES),
        cost_estimate=pl.CostEstimate(
            flops=0, bytes_accessed=slots.size * 4, transcendentals=0
        ),
    )(slots, meta)


def after_kernel(*refs):
    pass


def after(values, others, claim):
    anywhere = pl.BlockSpec(memory_space=pl.ANY)
    return pl.pallas_call(
        after_kernel,
        out_shape=[jax.ShapeDtypeStruct(v.shape, v.dtype) for v in values],
        in_specs=[anywhere] * (len(values) + len(others)),
        out_specs=[anywhere] * len(values),
        input_output_aliases={i: i for i in range(len(values))},
        compiler_params=pltpu.CompilerParams(vmem_limit_bytes=claim),
        cost_estimate=pl.CostEstimate(flops=0, bytes_accessed=0, transcendentals=0),
    )(*values, *others)


def first_kernel(depths, per_part, cap, bs, n_parts, dest_ref, *refs):
    parts = refs[:n_parts]
    rights = refs[n_parts : n_parts + len(depths)]
    refs = refs[n_parts + len(depths) :]
    acc_hbm, late_hbm, left, right, acc, right_sem, acc_sem, late_sem = refs
    inner, bn = right.shape[0], acc.shape[-1]
    at, fetches = 0, []
    for i, (depth, source) in enumerate(zip(depths, rights)):
        fetches.append(
            pltpu.make_async_copy(source, right.at[pl.ds(at, depth)], right_sem.at[i])
        )
        at += depth
    for fetch in fetches:
        fetch.start()
    some = left.shape[0] // PARTS

    def clear(i, carry):
        rows = pl.ds(pl.multiple_of(i * CLEAR, CLEAR), CLEAR)
        left[rows] = jnp.zeros((CLEAR, left.shape[1]), left.dtype)
        return carry

    lax.fori_loop(0, left.shape[0] // CLEAR, clear, 0)
    k_blocks = left.shape[1] // bs
    for q, part in enumerate(parts):

        def place(i, carry):
            for c in range(cap):
                dest = dest_ref[q, i, c]

                @pl.when(dest >= 0)
                def _():
                    row, col = dest // k_blocks, dest % k_blocks
                    left[
                        pl.ds(pl.multiple_of(row * bs, bs), bs),
                        pl.ds(pl.multiple_of(col * bs, bs), bs),
                    ] = part[i, pl.ds(c * bs, bs), :]

            return carry

        lax.fori_loop(0, per_part, place, 0)
    stores = [
        pltpu.make_async_copy(
            left.at[pl.ds(q * some, some), pl.ds(inner, late_hbm.shape[1])],
            late_hbm.at[pl.ds(q * some, some)],
            late_sem.at[q],
        )
        for q in range(PARTS)
    ]
    for store in stores:
        store.start()
    for fetch in fetches:
        fetch.wait()

    def multiply(j, carry):
        cols = pl.ds(pl.multiple_of(j * bn, bn), bn)
        acc[j] = jnp.dot(left[:, :inner], right[:, cols], preferred_element_type=jnp.float32)
        pltpu.make_async_copy(acc.at[j], acc_hbm.at[j], acc_sem.at[j]).start()
        return carry

    lax.fori_loop(0, acc.shape[0], multiply, 0)
    for j in range(acc.shape[0]):
        pltpu.make_async_copy(acc.at[j], acc_hbm.at[j], acc_sem.at[j]).wait()
    for store in stores:
        store.wait()


def first_product(dest, parts, rights, rows, late_width, bs, cap, bn):
    depths = [right.shape[0] for right in rights]
    cols = rights[0].shape[1]
    inner, steps = sum(depths), cols // bn
    anywhere = pl.BlockSpec(memory_space=pl.ANY)
    return pl.pallas_call(
        functools.partial(first_kernel, depths, parts[0].shape[0], cap, bs, len(parts)),
        out_shape=[
            jax.ShapeDtypeStruct((steps, rows, bn), jnp.float32),
            jax.ShapeDtypeStruct((rows, late_width), jnp.bfloat16),
        ],
        in_specs=[pl.BlockSpec(memory_space=pltpu.SMEM)]
        + [pl.BlockSpec(memory_space=pltpu.VMEM)] * len(parts)
        + [anywhere] * len(rights),
        out_specs=[anywhere] * 2,
        scratch_shapes=[
            pltpu.VMEM((rows, inner + late_width), jnp.bfloat16),
            pltpu.VMEM((inner, cols), jnp.bfloat16),
            pltpu.VMEM((steps, rows, bn), jnp.float32),
            pltpu.SemaphoreType.DMA((len(rights),)),
            pltpu.SemaphoreType.DMA((steps,)),
            pltpu.SemaphoreType.DMA((PARTS,)),
        ],
        compiler_params=pltpu.CompilerParams(
            vmem_limit_bytes=SPARE_BYTES
            + 2 * (rows * (inner + late_width) + inner * cols + 2 * rows * cols)
            + 2 * sum(part.size for part in parts)
        ),
        cost_estimate=pl.CostEstimate(
            flops=2 * rows * inner * cols,
            bytes_accessed=inner * cols * 2 + rows * cols * 4,
            transcendentals=0,
        ),
    )(dest, *parts, *rights)


def add_kernel(depths, place, late_hbm, acc_hbm, *refs):
    pieces = refs[: len(depths)]
    out_hbm, left, right, acc, out, left_sem, right_sem, acc_sem, out_sem = refs[len(depths) :]
    steps, rows, bn = acc.shape
    inner = left.shape[1]
    some = rows // PARTS

    def fetch_left(q):
        part = pl.ds(pl.multiple_of(q * some, some), some)
        source = late_hbm.at[part, pl.ds(place, inner)]
        return pltpu.make_async_copy(source, left.at[part], left_sem.at[q])

    def fetch(j):
        cols = pl.ds(pl.multiple_of(j * bn, bn), bn)
        copies, at = [pltpu.make_async_copy(acc_hbm.at[j], acc.at[j], acc_sem.at[j])], 0
        for i, (depth, piece) in enumerate(zip(depths, pieces)):
            target = right.at[j, pl.ds(at, depth)]
            copies.append(pltpu.make_async_copy(piece.at[:, cols], target, right_sem.at[j, i]))
            at += depth
        return copies

    def store(j):
        if len(out_hbm.shape) == 2:
            target = out_hbm.at[:, pl.ds(pl.multiple_of(j * bn, bn), bn)]
        else:
            target = out_hbm.at[j]
        return pltpu.make_async_copy(out.at[j], target, out_sem.at[j])

    def each(count, act):
        def step(i, carry):
            act(i)
            return carry

        lax.fori_loop(0, count, step, 0)

    each(PARTS, lambda q: fetch_left(q).start())
    each(steps, lambda j: [copy.start() for copy in fetch(j)])
    each(PARTS, lambda q: fetch_left(q).wait())

    def multiply(j):
        for copy in fetch(j):
            copy.wait()

        def turn(q):
            part = pl.ds(pl.multiple_of(q * some, some), some)
            total = jnp.dot(left[part], right[j], preferred_element_type=jnp.float32)
            out[j, part] = (acc[j, part] + total).astype(out.dtype)

        each(PARTS, turn)
        store(j).start()

    each(steps, multiply)
    each(steps, lambda j: store(j).wait())


def add_product(late, place, pieces, acc, last):
    steps, rows, bn = acc.shape
    depths = [piece.shape[0] for piece in pieces]
    inner = sum(depths)
    anywhere = pl.BlockSpec(memory_space=pl.ANY)
    if last:
        out_shape = jax.ShapeDtypeStruct((rows, steps * bn), jnp.bfloat16)
    else:
        out_shape = jax.ShapeDtypeStruct(acc.shape, acc.dtype)
    return pl.pallas_call(
        functools.partial(add_kernel, depths, place),
        out_shape=out_shape,
        in_specs=[anywhere] * (2 + len(pieces)),
        out_specs=anywhere,
        scratch_shapes=[
            pltpu.VMEM((rows, inner), jnp.bfloat16),
            pltpu.VMEM((steps, inner, bn), jnp.bfloat16),
            pltpu.VMEM((steps, rows, bn), jnp.float32),
            pltpu.VMEM((steps, rows, bn), out_shape.dtype),
            pltpu.SemaphoreType.DMA((PARTS,)),
            pltpu.SemaphoreType.DMA((steps, len(pieces))),
            pltpu.SemaphoreType.DMA((steps,)),
            pltpu.SemaphoreType.DMA((steps,)),
        ],
        compiler_params=pltpu.CompilerParams(
            vmem_limit_bytes=SPARE_BYTES + 2 * inner * (rows + steps * bn) + 8 * rows * steps * bn
        ),
        cost_estimate=pl.CostEstimate(
            flops=2 * rows * inner * steps * bn,
            bytes_accessed=(rows + steps * bn) * inner * 2 + rows * steps * bn * 8,
            transcendentals=0,
        ),
    )(late, acc, *pieces)


def halve_kernel(block_hbm, _, low_hbm, high_hbm, held, in_sem, out_sem):
    some = held.shape[0] // PARTS
    loads, stores = [], []
    for q in range(PARTS):
        rows = pl.ds(q * some, some)
        out_hbm = low_hbm if q < PARTS // 2 else high_hbm
        target = out_hbm.at[pl.ds(q % (PARTS // 2) * some, some)]
        loads.append(pltpu.make_async_copy(block_hbm.at[rows], held.at[rows], in_sem.at[q]))
        stores.append(pltpu.make_async_copy(held.at[rows], target, out_sem.at[q]))
    for load in loads:
        load.start()
    for load, store in zip(loads, stores):
        load.wait()
        store.start()
    for store in stores:
        store.wait()


def halve(block, ahead):
    anywhere = pl.BlockSpec(memory_space=pl.ANY)
    rows, cols = block.shape
    return pl.pallas_call(
        halve_kernel,
        out_shape=[jax.ShapeDtypeStruct((rows // 2, cols), block.dtype)] * 2,
        in_specs=[anywhere] * 2,
        out_specs=[anywhere] * 2,
        scratch_shapes=[
            pltpu.VMEM(block.shape, block.dtype),
            pltpu.SemaphoreType.DMA((PARTS,)),
            pltpu.SemaphoreType.DMA((PARTS,)),
        ],
        cost_estimate=pl.CostEstimate(flops=0, bytes_accessed=rows * cols * 4, transcendentals=0),
    )(block, ahead)


def across_row(landed, columns):
    if columns != 4:
        gathered = lax.all_gather(landed, "blk", axis=0)
        return [gathered[j] for j in range(columns)]
    swap_core = [(j, j ^ 1) for j in range(columns)]
    swap_chip = [(j, j ^ 2) for j in range(columns)]
    across = lax.ppermute(landed, "blk", swap_chip)
    near = lax.ppermute(landed, "blk", swap_core)
    return [landed, across, near, lax.ppermute(across, "blk", swap_core)]


def body(a_slots, a_rows, a_cols, a_count, owned_rows, b_matrix):
    groups = lax.axis_size("grid")
    columns = lax.axis_size("blk")
    bs = a_slots.shape[-1]
    cap = a_slots.shape[3]
    rb = owned_rows.shape[-1]
    k_local, n_local = b_matrix.shape
    blocks = k_local // bs
    half = groups // 2

    order = ring_order(groups)
    to_right = [(order[i], order[(i + 1) % groups]) for i in range(groups)]
    to_left = [(order[(i + 1) % groups], order[i]) for i in range(groups)]
    from_left, from_right, early = b_matrix, b_matrix, [b_matrix]
    for s in range(1, half - 1):
        from_left = lax.ppermute(from_left, "grid", to_right)
        from_right = lax.ppermute(from_right, "grid", to_left)
        early += [from_left, from_right]

    live = jnp.arange(cap, dtype=jnp.int32)[None, :] < a_count.reshape(groups, 1)
    row_code = jnp.where(live, a_rows.reshape(groups, cap) + 1, 0)
    meta = jnp.concatenate([row_code, a_cols.reshape(groups, cap)], axis=1)
    meta = jnp.pad(meta.astype(jnp.bfloat16)[:, None, :], ((0, 0), (0, META - 1), (0, bs - 2 * cap)))
    message = pack(a_slots.reshape(groups, cap * bs, bs), meta)
    landed = lax.all_to_all(message, "grid", split_axis=0, concat_axis=0, tiled=True)
    (landed,) = after([landed], early[1:3], VMEM_BYTES)
    parts = across_row(landed, columns)

    metas = jnp.stack([p[:, cap * bs, : 2 * cap] for p in parts]).astype(jnp.int32)
    code, col = metas[..., :cap], metas[..., cap:]
    hit = code[..., None] == owned_rows.reshape(rb) + 1
    row = jnp.sum(jnp.where(hit, jnp.arange(rb, dtype=jnp.int32), 0), axis=-1)
    pos = ring_place(lax.axis_index("grid"), groups)
    ahead = (ring_place(col // blocks, groups) - pos + groups) % groups
    hops = jnp.minimum(ahead, groups - ahead)
    first = jnp.where(hops == 0, 0, 2 * hops - 1) + jnp.where((ahead > 0) & (ahead < half), 1, 0)
    dest = row * (blocks * groups) + first * blocks + col % blocks
    dest = jnp.where(jnp.any(hit, axis=-1), dest, -1)

    left_low, left_high = halve(from_left, dest)
    right_low, right_high = halve(from_right, dest)
    left_low = lax.ppermute(left_low, "grid", to_right)
    right_high = lax.ppermute(right_high, "grid", to_left)
    left_high = lax.ppermute(left_high, "grid", to_right)
    right_low = lax.ppermute(right_low, "grid", to_left)

    acc, late = first_product(dest, parts, early, rb * bs, 3 * k_local, bs, cap, n_local // 4)
    left_low, right_high = after([left_low, right_high], [late], SPARE_BYTES)
    low = lax.ppermute(left_low, "grid", to_right)
    high = lax.ppermute(right_high, "grid", to_left)
    acc = add_product(late, 0, [left_low, left_high, right_low, right_high], acc, False)
    return add_product(late, 2 * k_local, [low, high], acc, True)


def solution(mesh):
    in_specs = (
        P("grid", "blk", None, None, None, None),
        P("grid", "blk", None, None),
        P("grid", "blk", None, None),
        P("grid", "blk", None),
        P("grid", None),
        P("grid", "blk"),
    )
    out_specs = P("grid", "blk")
    return jax.shard_map(body, mesh=mesh, in_specs=in_specs, out_specs=out_specs, check_vma=False)
```

```python
import functools

import jax
import jax.numpy as jnp
from jax import lax
from jax.experimental import pallas as pl
from jax.experimental.pallas import tpu as pltpu
from jax.sharding import PartitionSpec as P

META = 16
PARTS = 4
CLEAR = 32
VMEM_BYTES = 62 << 20
FIRST_BYTES = 255 << 18
SPARE_BYTES = 4 << 20


def ring_order(n):
    return list(range(0, n, 2)) + list(range(n - 1, 0, -2))


def ring_place(g, n):
    return jnp.where(g % 2 == 0, g // 2, n - 1 - g // 2)


def pack_kernel(slots_ref, meta_ref, message_ref):
    rows = slots_ref.shape[1]
    message_ref[:, :rows] = slots_ref[...]
    message_ref[:, rows:] = meta_ref[...]


def pack(slots, meta):
    groups, rows, width = slots.shape
    part = groups // 4
    return pl.pallas_call(
        pack_kernel,
        out_shape=jax.ShapeDtypeStruct((groups, rows + META, width), slots.dtype),
        grid=(groups // part,),
        in_specs=[
            pl.BlockSpec((part, rows, width), lambda i: (i, 0, 0)),
            pl.BlockSpec((part, META, width), lambda i: (i, 0, 0)),
        ],
        out_specs=pl.BlockSpec((part, rows + META, width), lambda i: (i, 0, 0)),
        compiler_params=pltpu.CompilerParams(vmem_limit_bytes=VMEM_BYTES),
        cost_estimate=pl.CostEstimate(
            flops=0, bytes_accessed=slots.size * 4, transcendentals=0
        ),
    )(slots, meta)


def after_kernel(*refs):
    pass


def after(values, others):
    anywhere = pl.BlockSpec(memory_space=pl.ANY)
    return pl.pallas_call(
        after_kernel,
        out_shape=[jax.ShapeDtypeStruct(v.shape, v.dtype) for v in values],
        in_specs=[anywhere] * (len(values) + len(others)),
        out_specs=[anywhere] * len(values),
        input_output_aliases={i: i for i in range(len(values))},
        compiler_params=pltpu.CompilerParams(vmem_limit_bytes=SPARE_BYTES),
        cost_estimate=pl.CostEstimate(flops=0, bytes_accessed=0, transcendentals=0),
    )(*values, *others)


def first_kernel(depths, per_part, cap, bs, n_parts, dest_ref, *refs):
    parts = refs[:n_parts]
    rights = refs[n_parts : n_parts + len(depths)]
    refs = refs[n_parts + len(depths) :]
    acc_hbm, late_hbm, mark, left, right, acc, right_sem, acc_sem, late_sem = refs
    mark[...] = jnp.zeros_like(mark)
    inner, bn = right.shape[0], acc.shape[-1]
    at, fetches = 0, []
    for i, (depth, source) in enumerate(zip(depths, rights)):
        fetches.append(
            pltpu.make_async_copy(source, right.at[pl.ds(at, depth)], right_sem.at[i])
        )
        at += depth
    for fetch in fetches:
        fetch.start()
    some = left.shape[0] // PARTS

    def clear(i, carry):
        rows = pl.ds(pl.multiple_of(i * CLEAR, CLEAR), CLEAR)
        left[rows] = jnp.zeros((CLEAR, left.shape[1]), left.dtype)
        return carry

    lax.fori_loop(0, left.shape[0] // CLEAR, clear, 0)
    k_blocks = left.shape[1] // bs
    for q, part in enumerate(parts):

        def place(i, carry):
            for c in range(cap):
                dest = dest_ref[q, i, c]

                @pl.when(dest >= 0)
                def _():
                    row, col = dest // k_blocks, dest % k_blocks
                    left[
                        pl.ds(pl.multiple_of(row * bs, bs), bs),
                        pl.ds(pl.multiple_of(col * bs, bs), bs),
                    ] = part[i, pl.ds(c * bs, bs), :]

            return carry

        lax.fori_loop(0, per_part, place, 0)
    stores = [
        pltpu.make_async_copy(
            left.at[pl.ds(q * some, some), pl.ds(inner, late_hbm.shape[1])],
            late_hbm.at[pl.ds(q * some, some)],
            late_sem.at[q],
        )
        for q in range(PARTS)
    ]
    for store in stores:
        store.start()
    for fetch in fetches:
        fetch.wait()

    def multiply(j, carry):
        cols = pl.ds(pl.multiple_of(j * bn, bn), bn)
        acc[j] = jnp.dot(left[:, :inner], right[:, cols], preferred_element_type=jnp.float32)
        pltpu.make_async_copy(acc.at[j], acc_hbm.at[j], acc_sem.at[j]).start()
        return carry

    lax.fori_loop(0, acc.shape[0], multiply, 0)
    for j in range(acc.shape[0]):
        pltpu.make_async_copy(acc.at[j], acc_hbm.at[j], acc_sem.at[j]).wait()
    for store in stores:
        store.wait()


def first_product(dest, parts, rights, rows, late_width, bs, cap, bn):
    depths = [right.shape[0] for right in rights]
    cols = rights[0].shape[1]
    inner, steps = sum(depths), cols // bn
    anywhere = pl.BlockSpec(memory_space=pl.ANY)
    return pl.pallas_call(
        functools.partial(first_kernel, depths, parts[0].shape[0], cap, bs, len(parts)),
        out_shape=[
            jax.ShapeDtypeStruct((steps, rows, bn), jnp.float32),
            jax.ShapeDtypeStruct((rows, late_width), jnp.bfloat16),
            jax.ShapeDtypeStruct((8, bs), jnp.float32),
        ],
        in_specs=[pl.BlockSpec(memory_space=pltpu.SMEM)]
        + [pl.BlockSpec(memory_space=pltpu.VMEM)] * len(parts)
        + [anywhere] * len(rights),
        out_specs=[anywhere] * 2 + [pl.BlockSpec(memory_space=pltpu.VMEM)],
        scratch_shapes=[
            pltpu.VMEM((rows, inner + late_width), jnp.bfloat16),
            pltpu.VMEM((inner, cols), jnp.bfloat16),
            pltpu.VMEM((steps, rows, bn), jnp.float32),
            pltpu.SemaphoreType.DMA((len(rights),)),
            pltpu.SemaphoreType.DMA((steps,)),
            pltpu.SemaphoreType.DMA((PARTS,)),
        ],
        compiler_params=pltpu.CompilerParams(vmem_limit_bytes=FIRST_BYTES),
        cost_estimate=pl.CostEstimate(
            flops=2 * rows * inner * cols,
            bytes_accessed=inner * cols * 2 + rows * cols * 4,
            transcendentals=0,
        ),
    )(dest, *parts, *rights)


def add_kernel(depths, place, late_hbm, acc_hbm, *refs):
    pieces = refs[: len(depths)]
    out_hbm, left, right, acc, out, left_sem, right_sem, acc_sem, out_sem = refs[len(depths) :]
    steps, rows, bn = acc.shape
    inner = left.shape[1]
    some = rows // PARTS

    def fetch_left(q):
        part = pl.ds(pl.multiple_of(q * some, some), some)
        source = late_hbm.at[part, pl.ds(place, inner)]
        return pltpu.make_async_copy(source, left.at[part], left_sem.at[q])

    def fetch(j):
        cols = pl.ds(pl.multiple_of(j * bn, bn), bn)
        copies, at = [pltpu.make_async_copy(acc_hbm.at[j], acc.at[j], acc_sem.at[j])], 0
        for i, (depth, piece) in enumerate(zip(depths, pieces)):
            target = right.at[j, pl.ds(at, depth)]
            copies.append(pltpu.make_async_copy(piece.at[:, cols], target, right_sem.at[j, i]))
            at += depth
        return copies

    def store(j):
        if len(out_hbm.shape) == 2:
            target = out_hbm.at[:, pl.ds(pl.multiple_of(j * bn, bn), bn)]
        else:
            target = out_hbm.at[j]
        return pltpu.make_async_copy(out.at[j], target, out_sem.at[j])

    def each(count, act):
        def step(i, carry):
            act(i)
            return carry

        lax.fori_loop(0, count, step, 0)

    each(PARTS, lambda q: fetch_left(q).start())
    each(steps, lambda j: [copy.start() for copy in fetch(j)])
    each(PARTS, lambda q: fetch_left(q).wait())

    def multiply(j):
        for copy in fetch(j):
            copy.wait()

        def turn(q):
            part = pl.ds(pl.multiple_of(q * some, some), some)
            total = jnp.dot(left[part], right[j], preferred_element_type=jnp.float32)
            out[j, part] = (acc[j, part] + total).astype(out.dtype)

        each(PARTS, turn)
        store(j).start()

    each(steps, multiply)
    each(steps, lambda j: store(j).wait())


def add_product(late, place, pieces, acc, last):
    steps, rows, bn = acc.shape
    depths = [piece.shape[0] for piece in pieces]
    inner = sum(depths)
    anywhere = pl.BlockSpec(memory_space=pl.ANY)
    if last:
        out_shape = jax.ShapeDtypeStruct((rows, steps * bn), jnp.bfloat16)
    else:
        out_shape = jax.ShapeDtypeStruct(acc.shape, acc.dtype)
    return pl.pallas_call(
        functools.partial(add_kernel, depths, place),
        out_shape=out_shape,
        in_specs=[anywhere] * (2 + len(pieces)),
        out_specs=anywhere,
        scratch_shapes=[
            pltpu.VMEM((rows, inner), jnp.bfloat16),
            pltpu.VMEM((steps, inner, bn), jnp.bfloat16),
            pltpu.VMEM((steps, rows, bn), jnp.float32),
            pltpu.VMEM((steps, rows, bn), out_shape.dtype),
            pltpu.SemaphoreType.DMA((PARTS,)),
            pltpu.SemaphoreType.DMA((steps, len(pieces))),
            pltpu.SemaphoreType.DMA((steps,)),
            pltpu.SemaphoreType.DMA((steps,)),
        ],
        compiler_params=pltpu.CompilerParams(
            vmem_limit_bytes=SPARE_BYTES + 2 * inner * (rows + steps * bn) + 8 * rows * steps * bn
        ),
        cost_estimate=pl.CostEstimate(
            flops=2 * rows * inner * steps * bn,
            bytes_accessed=(rows + steps * bn) * inner * 2 + rows * steps * bn * 8,
            transcendentals=0,
        ),
    )(late, acc, *pieces)


def across_row(landed, columns):
    if columns != 4:
        gathered = lax.all_gather(landed, "blk", axis=0)
        return [gathered[j] for j in range(columns)]
    swap_core = [(j, j ^ 1) for j in range(columns)]
    swap_chip = [(j, j ^ 2) for j in range(columns)]
    across = lax.ppermute(landed, "blk", swap_chip)
    near = lax.ppermute(landed, "blk", swap_core)
    return [landed, across, near, lax.ppermute(across, "blk", swap_core)]


def body(a_slots, a_rows, a_cols, a_count, owned_rows, b_matrix):
    groups = lax.axis_size("grid")
    columns = lax.axis_size("blk")
    bs = a_slots.shape[-1]
    cap = a_slots.shape[3]
    rb = owned_rows.shape[-1]
    k_local, n_local = b_matrix.shape
    blocks = k_local // bs
    half = groups // 2

    order = ring_order(groups)
    to_right = [(order[i], order[(i + 1) % groups]) for i in range(groups)]
    to_left = [(order[(i + 1) % groups], order[i]) for i in range(groups)]
    from_left, from_right, early = b_matrix, b_matrix, [b_matrix]
    for s in range(1, half - 1):
        from_left = lax.ppermute(from_left, "grid", to_right)
        from_right = lax.ppermute(from_right, "grid", to_left)
        early += [from_left, from_right]
    split = k_local // 2
    left_low, right_high = from_left[:split], from_right[split:]
    left_high, right_low = from_left[split:], from_right[:split]
    left_low = lax.ppermute(left_low, "grid", to_right)
    right_high = lax.ppermute(right_high, "grid", to_left)
    left_high = lax.ppermute(left_high, "grid", to_right)
    right_low = lax.ppermute(right_low, "grid", to_left)

    live = jnp.arange(cap, dtype=jnp.int32)[None, :] < a_count.reshape(groups, 1)
    row_code = jnp.where(live, a_rows.reshape(groups, cap) + 1, 0)
    meta = jnp.concatenate([row_code, a_cols.reshape(groups, cap)], axis=1)
    meta = jnp.pad(meta.astype(jnp.bfloat16)[:, None, :], ((0, 0), (0, META - 1), (0, bs - 2 * cap)))
    message = pack(a_slots.reshape(groups, cap * bs, bs), meta)
    landed = lax.all_to_all(message, "grid", split_axis=0, concat_axis=0, tiled=True)
    (landed,) = after([landed], early[1:3])
    parts = across_row(landed, columns)

    metas = jnp.stack([p[:, cap * bs, : 2 * cap] for p in parts]).astype(jnp.int32)
    code, col = metas[..., :cap], metas[..., cap:]
    hit = code[..., None] == owned_rows.reshape(rb) + 1
    row = jnp.sum(jnp.where(hit, jnp.arange(rb, dtype=jnp.int32), 0), axis=-1)
    pos = ring_place(lax.axis_index("grid"), groups)
    ahead = (ring_place(col // blocks, groups) - pos + groups) % groups
    hops = jnp.minimum(ahead, groups - ahead)
    first = jnp.where(hops == 0, 0, 2 * hops - 1) + jnp.where((ahead > 0) & (ahead < half), 1, 0)
    dest = row * (blocks * groups) + first * blocks + col % blocks
    dest = jnp.where(jnp.any(hit, axis=-1), dest, -1)

    acc, late, mark = first_product(dest, parts, early, rb * bs, 3 * k_local, bs, cap, n_local // 4)
    left_low, right_high = after([left_low, right_high], [mark])
    low = lax.ppermute(left_low, "grid", to_right)
    high = lax.ppermute(right_high, "grid", to_left)
    acc = add_product(late, 0, [left_low, left_high, right_low, right_high], acc, False)
    return add_product(late, 2 * k_local, [low, high], acc, True)


def solution(mesh):
    in_specs = (
        P("grid", "blk", None, None, None, None),
        P("grid", "blk", None, None),
        P("grid", "blk", None, None),
        P("grid", "blk", None),
        P("grid", None),
        P("grid", "blk"),
    )
    out_specs = P("grid", "blk")
    return jax.shard_map(body, mesh=mesh, in_specs=in_specs, out_specs=out_specs, check_vma=False)
```

```python
import functools

import jax
import jax.numpy as jnp
from jax import lax
from jax.experimental import pallas as pl
from jax.experimental.pallas import tpu as pltpu
from jax.sharding import PartitionSpec as P

META = 16
PARTS = 4
CLEAR = 32
VMEM_BYTES = 62 << 20
FIRST_BYTES = 26 << 20
ADD_BYTES = 18 << 20
LARGE = 4 << 20
SPARE_BYTES = 4 << 20


def ring_order(n):
    return list(range(0, n, 2)) + list(range(n - 1, 0, -2))


def ring_place(g, n):
    return jnp.where(g % 2 == 0, g // 2, n - 1 - g // 2)


def pack_kernel(slots_ref, meta_ref, message_ref):
    rows = slots_ref.shape[1]
    message_ref[:, :rows] = slots_ref[...]
    message_ref[:, rows:] = meta_ref[...]


def pack(slots, meta):
    groups, rows, width = slots.shape
    part = groups // 4
    return pl.pallas_call(
        pack_kernel,
        out_shape=jax.ShapeDtypeStruct((groups, rows + META, width), slots.dtype),
        grid=(groups // part,),
        in_specs=[
            pl.BlockSpec((part, rows, width), lambda i: (i, 0, 0)),
            pl.BlockSpec((part, META, width), lambda i: (i, 0, 0)),
        ],
        out_specs=pl.BlockSpec((part, rows + META, width), lambda i: (i, 0, 0)),
        compiler_params=pltpu.CompilerParams(vmem_limit_bytes=VMEM_BYTES),
        cost_estimate=pl.CostEstimate(
            flops=0, bytes_accessed=slots.size * 4, transcendentals=0
        ),
    )(slots, meta)


def after_kernel(*refs):
    pass


def after(values, others):
    anywhere = pl.BlockSpec(memory_space=pl.ANY)
    return pl.pallas_call(
        after_kernel,
        out_shape=[jax.ShapeDtypeStruct(v.shape, v.dtype) for v in values],
        in_specs=[anywhere] * (len(values) + len(others)),
        out_specs=[anywhere] * len(values),
        input_output_aliases={i: i for i in range(len(values))},
        compiler_params=pltpu.CompilerParams(vmem_limit_bytes=SPARE_BYTES),
        cost_estimate=pl.CostEstimate(flops=0, bytes_accessed=0, transcendentals=0),
    )(*values, *others)


def first_kernel(depths, per_part, cap, bs, n_parts, dest_ref, *refs):
    parts = refs[:n_parts]
    rights = refs[n_parts : n_parts + len(depths)]
    refs = refs[n_parts + len(depths) :]
    acc_hbm, late_hbm, mark, left, right, acc, held, right_sem, acc_sem, late_sem, part_sem = refs
    mark[...] = jnp.zeros_like(mark)
    inner, bn = right.shape[0], acc.shape[-1]
    part_copies = [
        pltpu.make_async_copy(part, held.at[q], part_sem.at[q]) for q, part in enumerate(parts)
    ]
    for copy in part_copies:
        copy.start()
    at, fetches = 0, []
    for i, (depth, source) in enumerate(zip(depths, rights)):
        fetches.append(
            pltpu.make_async_copy(source, right.at[pl.ds(at, depth)], right_sem.at[i])
        )
        at += depth
    for fetch in fetches:
        fetch.start()
    some = left.shape[0] // PARTS

    def clear(i, carry):
        rows = pl.ds(pl.multiple_of(i * CLEAR, CLEAR), CLEAR)
        left[rows] = jnp.zeros((CLEAR, left.shape[1]), left.dtype)
        return carry

    lax.fori_loop(0, left.shape[0] // CLEAR, clear, 0)
    k_blocks = left.shape[1] // bs
    for q in range(n_parts):
        part_copies[q].wait()

        def place(i, carry):
            for c in range(cap):
                dest = dest_ref[q, i, c]

                @pl.when(dest >= 0)
                def _():
                    row, col = dest // k_blocks, dest % k_blocks
                    left[
                        pl.ds(pl.multiple_of(row * bs, bs), bs),
                        pl.ds(pl.multiple_of(col * bs, bs), bs),
                    ] = held[q, i, pl.ds(c * bs, bs), :]

            return carry

        lax.fori_loop(0, per_part, place, 0)
    stores = [
        pltpu.make_async_copy(
            left.at[pl.ds(q * some, some), pl.ds(inner, late_hbm.shape[1])],
            late_hbm.at[pl.ds(q * some, some)],
            late_sem.at[q],
        )
        for q in range(PARTS)
    ]
    for store in stores:
        store.start()
    for fetch in fetches:
        fetch.wait()

    def multiply(j, carry):
        cols = pl.ds(pl.multiple_of(j * bn, bn), bn)
        acc[j] = jnp.dot(left[:, :inner], right[:, cols], preferred_element_type=jnp.float32)
        pltpu.make_async_copy(acc.at[j], acc_hbm.at[j], acc_sem.at[j]).start()
        return carry

    lax.fori_loop(0, acc.shape[0], multiply, 0)
    for j in range(acc.shape[0]):
        pltpu.make_async_copy(acc.at[j], acc_hbm.at[j], acc_sem.at[j]).wait()
    for store in stores:
        store.wait()


def first_product(dest, parts, rights, rows, late_width, bs, cap, bn):
    depths = [right.shape[0] for right in rights]
    cols = rights[0].shape[1]
    inner, steps = sum(depths), cols // bn
    anywhere = pl.BlockSpec(memory_space=pl.ANY)
    return pl.pallas_call(
        functools.partial(first_kernel, depths, parts[0].shape[0], cap, bs, len(parts)),
        out_shape=[
            jax.ShapeDtypeStruct((steps, rows, bn), jnp.float32),
            jax.ShapeDtypeStruct((rows, late_width), jnp.bfloat16),
            jax.ShapeDtypeStruct((8, bs), jnp.float32),
        ],
        in_specs=[pl.BlockSpec(memory_space=pltpu.SMEM)]
        + [pl.BlockSpec(memory_space=pltpu.HBM)] * (len(parts) + len(rights)),
        out_specs=[anywhere] * 2 + [pl.BlockSpec(memory_space=pltpu.VMEM)],
        scratch_shapes=[
            pltpu.VMEM((rows, inner + late_width), jnp.bfloat16),
            pltpu.VMEM((inner, cols), jnp.bfloat16),
            pltpu.VMEM((steps, rows, bn), jnp.float32),
            pltpu.VMEM((len(parts),) + parts[0].shape, parts[0].dtype),
            pltpu.SemaphoreType.DMA((len(rights),)),
            pltpu.SemaphoreType.DMA((steps,)),
            pltpu.SemaphoreType.DMA((PARTS,)),
            pltpu.SemaphoreType.DMA((len(parts),)),
        ],
        compiler_params=pltpu.CompilerParams(vmem_limit_bytes=FIRST_BYTES if cols * inner < LARGE else VMEM_BYTES),
        cost_estimate=pl.CostEstimate(
            flops=2 * rows * inner * cols,
            bytes_accessed=inner * cols * 2 + rows * cols * 4,
            transcendentals=0,
        ),
    )(dest, *parts, *rights)


def add_kernel(depths, place, late_hbm, acc_hbm, *refs):
    pieces = refs[: len(depths)]
    out_hbm, left, right, acc, out, left_sem, right_sem, acc_sem, out_sem = refs[len(depths) :]
    steps, rows, bn = acc.shape
    inner = left.shape[1]
    some = rows // PARTS

    def fetch_left(q):
        part = pl.ds(pl.multiple_of(q * some, some), some)
        source = late_hbm.at[part, pl.ds(place, inner)]
        return pltpu.make_async_copy(source, left.at[part], left_sem.at[q])

    def fetch(j):
        cols = pl.ds(pl.multiple_of(j * bn, bn), bn)
        copies, at = [pltpu.make_async_copy(acc_hbm.at[j], acc.at[j], acc_sem.at[j])], 0
        for i, (depth, piece) in enumerate(zip(depths, pieces)):
            target = right.at[j, pl.ds(at, depth)]
            copies.append(pltpu.make_async_copy(piece.at[:, cols], target, right_sem.at[j, i]))
            at += depth
        return copies

    def store(j):
        if len(out_hbm.shape) == 2:
            target = out_hbm.at[:, pl.ds(pl.multiple_of(j * bn, bn), bn)]
        else:
            target = out_hbm.at[j]
        return pltpu.make_async_copy(out.at[j], target, out_sem.at[j])

    def each(count, act):
        def step(i, carry):
            act(i)
            return carry

        lax.fori_loop(0, count, step, 0)

    each(PARTS, lambda q: fetch_left(q).start())
    each(steps, lambda j: [copy.start() for copy in fetch(j)])
    each(PARTS, lambda q: fetch_left(q).wait())

    def multiply(j):
        for copy in fetch(j):
            copy.wait()

        def turn(q):
            part = pl.ds(pl.multiple_of(q * some, some), some)
            total = jnp.dot(left[part], right[j], preferred_element_type=jnp.float32)
            out[j, part] = (acc[j, part] + total).astype(out.dtype)

        each(PARTS, turn)
        store(j).start()

    each(steps, multiply)
    each(steps, lambda j: store(j).wait())


def add_product(late, place, pieces, acc, last):
    steps, rows, bn = acc.shape
    depths = [piece.shape[0] for piece in pieces]
    inner = sum(depths)
    anywhere = pl.BlockSpec(memory_space=pl.ANY)
    if last:
        out_shape = jax.ShapeDtypeStruct((rows, steps * bn), jnp.bfloat16)
    else:
        out_shape = jax.ShapeDtypeStruct(acc.shape, acc.dtype)
    return pl.pallas_call(
        functools.partial(add_kernel, depths, place),
        out_shape=out_shape,
        in_specs=[anywhere] * (2 + len(pieces)),
        out_specs=anywhere,
        scratch_shapes=[
            pltpu.VMEM((rows, inner), jnp.bfloat16),
            pltpu.VMEM((steps, inner, bn), jnp.bfloat16),
            pltpu.VMEM((steps, rows, bn), jnp.float32),
            pltpu.VMEM((steps, rows, bn), out_shape.dtype),
            pltpu.SemaphoreType.DMA((PARTS,)),
            pltpu.SemaphoreType.DMA((steps, len(pieces))),
            pltpu.SemaphoreType.DMA((steps,)),
            pltpu.SemaphoreType.DMA((steps,)),
        ],
        compiler_params=pltpu.CompilerParams(
            vmem_limit_bytes=ADD_BYTES
        ),
        cost_estimate=pl.CostEstimate(
            flops=2 * rows * inner * steps * bn,
            bytes_accessed=(rows + steps * bn) * inner * 2 + rows * steps * bn * 8,
            transcendentals=0,
        ),
    )(late, acc, *pieces)


def across_row(landed, columns):
    if columns != 4:
        gathered = lax.all_gather(landed, "blk", axis=0)
        return [gathered[j] for j in range(columns)]
    swap_core = [(j, j ^ 1) for j in range(columns)]
    swap_chip = [(j, j ^ 2) for j in range(columns)]
    across = lax.ppermute(landed, "blk", swap_chip)
    near = lax.ppermute(landed, "blk", swap_core)
    return [landed, across, near, lax.ppermute(across, "blk", swap_core)]


def body(a_slots, a_rows, a_cols, a_count, owned_rows, b_matrix):
    groups = lax.axis_size("grid")
    columns = lax.axis_size("blk")
    bs = a_slots.shape[-1]
    cap = a_slots.shape[3]
    rb = owned_rows.shape[-1]
    k_local, n_local = b_matrix.shape
    blocks = k_local // bs
    half = groups // 2

    order = ring_order(groups)
    to_right = [(order[i], order[(i + 1) % groups]) for i in range(groups)]
    to_left = [(order[(i + 1) % groups], order[i]) for i in range(groups)]
    from_left, from_right, early = b_matrix, b_matrix, [b_matrix]
    for s in range(1, half - 1):
        from_left = lax.ppermute(from_left, "grid", to_right)
        from_right = lax.ppermute(from_right, "grid", to_left)
        early += [from_left, from_right]
    split = k_local // 2
    left_low, right_high = from_left[:split], from_right[split:]
    left_high, right_low = from_left[split:], from_right[:split]
    left_low = lax.ppermute(left_low, "grid", to_right)
    right_high = lax.ppermute(right_high, "grid", to_left)
    left_high = lax.ppermute(left_high, "grid", to_right)
    right_low = lax.ppermute(right_low, "grid", to_left)

    live = jnp.arange(cap, dtype=jnp.int32)[None, :] < a_count.reshape(groups, 1)
    row_code = jnp.where(live, a_rows.reshape(groups, cap) + 1, 0)
    meta = jnp.concatenate([row_code, a_cols.reshape(groups, cap)], axis=1)
    meta = jnp.pad(meta.astype(jnp.bfloat16)[:, None, :], ((0, 0), (0, META - 1), (0, bs - 2 * cap)))
    message = pack(a_slots.reshape(groups, cap * bs, bs), meta)
    landed = lax.all_to_all(message, "grid", split_axis=0, concat_axis=0, tiled=True)
    (landed,) = after([landed], early[1:3])
    parts = across_row(landed, columns)

    metas = jnp.stack([p[:, cap * bs, : 2 * cap] for p in parts]).astype(jnp.int32)
    code, col = metas[..., :cap], metas[..., cap:]
    hit = code[..., None] == owned_rows.reshape(rb) + 1
    row = jnp.sum(jnp.where(hit, jnp.arange(rb, dtype=jnp.int32), 0), axis=-1)
    pos = ring_place(lax.axis_index("grid"), groups)
    ahead = (ring_place(col // blocks, groups) - pos + groups) % groups
    hops = jnp.minimum(ahead, groups - ahead)
    first = jnp.where(hops == 0, 0, 2 * hops - 1) + jnp.where((ahead > 0) & (ahead < half), 1, 0)
    dest = row * (blocks * groups) + first * blocks + col % blocks
    dest = jnp.where(jnp.any(hit, axis=-1), dest, -1)

    acc, late, mark = first_product(dest, parts, early, rb * bs, 3 * k_local, bs, cap, n_local // 4)
    left_low, right_high = after([left_low, right_high], [mark])
    low = lax.ppermute(left_low, "grid", to_right)
    high = lax.ppermute(right_high, "grid", to_left)
    acc = add_product(late, 0, [left_low, left_high, right_low, right_high], acc, False)
    return add_product(late, 2 * k_local, [low, high], acc, True)


def solution(mesh):
    in_specs = (
        P("grid", "blk", None, None, None, None),
        P("grid", "blk", None, None),
        P("grid", "blk", None, None),
        P("grid", "blk", None),
        P("grid", None),
        P("grid", "blk"),
    )
    out_specs = P("grid", "blk")
    return jax.shard_map(body, mesh=mesh, in_specs=in_specs, out_specs=out_specs, check_vma=False)
```

```python
import functools

import jax
import jax.numpy as jnp
from jax import lax
from jax.experimental import pallas as pl
from jax.experimental.pallas import tpu as pltpu
from jax.sharding import PartitionSpec as P

META = 16
PARTS = 4
CLEAR = 32
VMEM_BYTES = 62 << 20
FIRST_BYTES = 26 << 20
ADD_BYTES = 18 << 20
LARGE = 4 << 20
SPARE_BYTES = 4 << 20


def ring_order(n):
    return list(range(0, n, 2)) + list(range(n - 1, 0, -2))


def ring_place(g, n):
    return jnp.where(g % 2 == 0, g // 2, n - 1 - g // 2)


def pack_kernel(slots_ref, meta_ref, message_ref):
    rows = slots_ref.shape[1]
    message_ref[:, :rows] = slots_ref[...]
    message_ref[:, rows:] = meta_ref[...]


def pack(slots, meta):
    groups, rows, width = slots.shape
    part = groups // 4
    return pl.pallas_call(
        pack_kernel,
        out_shape=jax.ShapeDtypeStruct((groups, rows + META, width), slots.dtype),
        grid=(groups // part,),
        in_specs=[
            pl.BlockSpec((part, rows, width), lambda i: (i, 0, 0)),
            pl.BlockSpec((part, META, width), lambda i: (i, 0, 0)),
        ],
        out_specs=pl.BlockSpec((part, rows + META, width), lambda i: (i, 0, 0)),
        compiler_params=pltpu.CompilerParams(vmem_limit_bytes=VMEM_BYTES),
        cost_estimate=pl.CostEstimate(
            flops=0, bytes_accessed=slots.size * 4, transcendentals=0
        ),
    )(slots, meta)


def after_kernel(*refs):
    pass


def after(values, others, claim):
    anywhere = pl.BlockSpec(memory_space=pl.ANY)
    return pl.pallas_call(
        after_kernel,
        out_shape=[jax.ShapeDtypeStruct(v.shape, v.dtype) for v in values],
        in_specs=[anywhere] * (len(values) + len(others)),
        out_specs=[anywhere] * len(values),
        input_output_aliases={i: i for i in range(len(values))},
        compiler_params=pltpu.CompilerParams(vmem_limit_bytes=claim),
        cost_estimate=pl.CostEstimate(flops=0, bytes_accessed=0, transcendentals=0),
    )(*values, *others)


def first_kernel(depths, per_part, cap, bs, n_parts, dest_ref, *refs):
    parts = refs[:n_parts]
    rights = refs[n_parts : n_parts + len(depths)]
    refs = refs[n_parts + len(depths) :]
    acc_hbm, late_hbm, mark, left, right, acc, held, right_sem, acc_sem, late_sem, part_sem = refs
    mark[...] = jnp.zeros_like(mark)
    inner, bn = right.shape[0], acc.shape[-1]
    part_copies = [
        pltpu.make_async_copy(part, held.at[q], part_sem.at[q]) for q, part in enumerate(parts)
    ]
    for copy in part_copies:
        copy.start()
    at, fetches = 0, []
    for i, (depth, source) in enumerate(zip(depths, rights)):
        fetches.append(
            pltpu.make_async_copy(source, right.at[pl.ds(at, depth)], right_sem.at[i])
        )
        at += depth
    for fetch in fetches:
        fetch.start()
    some = left.shape[0] // PARTS

    def clear(i, carry):
        rows = pl.ds(pl.multiple_of(i * CLEAR, CLEAR), CLEAR)
        left[rows] = jnp.zeros((CLEAR, left.shape[1]), left.dtype)
        return carry

    lax.fori_loop(0, left.shape[0] // CLEAR, clear, 0)
    k_blocks = left.shape[1] // bs
    for q in range(n_parts):
        part_copies[q].wait()

        def place(i, carry):
            for c in range(cap):
                dest = dest_ref[q, i, c]

                @pl.when(dest >= 0)
                def _():
                    row, col = dest // k_blocks, dest % k_blocks
                    left[
                        pl.ds(pl.multiple_of(row * bs, bs), bs),
                        pl.ds(pl.multiple_of(col * bs, bs), bs),
                    ] = held[q, i, pl.ds(c * bs, bs), :]

            return carry

        lax.fori_loop(0, per_part, place, 0)
    stores = [
        pltpu.make_async_copy(
            left.at[pl.ds(q * some, some), pl.ds(inner, late_hbm.shape[1])],
            late_hbm.at[pl.ds(q * some, some)],
            late_sem.at[q],
        )
        for q in range(PARTS)
    ]
    for store in stores:
        store.start()
    for fetch in fetches:
        fetch.wait()

    def multiply(j, carry):
        cols = pl.ds(pl.multiple_of(j * bn, bn), bn)
        acc[j] = jnp.dot(left[:, :inner], right[:, cols], preferred_element_type=jnp.float32)
        pltpu.make_async_copy(acc.at[j], acc_hbm.at[j], acc_sem.at[j]).start()
        return carry

    lax.fori_loop(0, acc.shape[0], multiply, 0)
    for j in range(acc.shape[0]):
        pltpu.make_async_copy(acc.at[j], acc_hbm.at[j], acc_sem.at[j]).wait()
    for store in stores:
        store.wait()


def first_product(dest, parts, rights, rows, late_width, bs, cap, bn):
    depths = [right.shape[0] for right in rights]
    cols = rights[0].shape[1]
    inner, steps = sum(depths), cols // bn
    anywhere = pl.BlockSpec(memory_space=pl.ANY)
    return pl.pallas_call(
        functools.partial(first_kernel, depths, parts[0].shape[0], cap, bs, len(parts)),
        out_shape=[
            jax.ShapeDtypeStruct((steps, rows, bn), jnp.float32),
            jax.ShapeDtypeStruct((rows, late_width), jnp.bfloat16),
            jax.ShapeDtypeStruct((8, bs), jnp.float32),
        ],
        in_specs=[pl.BlockSpec(memory_space=pltpu.SMEM)]
        + [pl.BlockSpec(memory_space=pltpu.HBM)] * (len(parts) + len(rights)),
        out_specs=[anywhere] * 2 + [pl.BlockSpec(memory_space=pltpu.VMEM)],
        scratch_shapes=[
            pltpu.VMEM((rows, inner + late_width), jnp.bfloat16),
            pltpu.VMEM((inner, cols), jnp.bfloat16),
            pltpu.VMEM((steps, rows, bn), jnp.float32),
            pltpu.VMEM((len(parts),) + parts[0].shape, parts[0].dtype),
            pltpu.SemaphoreType.DMA((len(rights),)),
            pltpu.SemaphoreType.DMA((steps,)),
            pltpu.SemaphoreType.DMA((PARTS,)),
            pltpu.SemaphoreType.DMA((len(parts),)),
        ],
        compiler_params=pltpu.CompilerParams(vmem_limit_bytes=FIRST_BYTES if cols * inner < LARGE else VMEM_BYTES),
        cost_estimate=pl.CostEstimate(
            flops=2 * rows * inner * cols,
            bytes_accessed=inner * cols * 2 + rows * cols * 4,
            transcendentals=0,
        ),
    )(dest, *parts, *rights)


def add_kernel(depths, place, late_hbm, acc_hbm, *refs):
    pieces = refs[: len(depths)]
    out_hbm, left, right, acc, out, left_sem, right_sem, acc_sem, out_sem = refs[len(depths) :]
    steps, rows, bn = acc.shape
    inner = left.shape[1]
    some = rows // PARTS

    def fetch_left(q):
        part = pl.ds(pl.multiple_of(q * some, some), some)
        source = late_hbm.at[part, pl.ds(place, inner)]
        return pltpu.make_async_copy(source, left.at[part], left_sem.at[q])

    def fetch(j):
        cols = pl.ds(pl.multiple_of(j * bn, bn), bn)
        copies, at = [pltpu.make_async_copy(acc_hbm.at[j], acc.at[j], acc_sem.at[j])], 0
        for i, (depth, piece) in enumerate(zip(depths, pieces)):
            target = right.at[j, pl.ds(at, depth)]
            copies.append(pltpu.make_async_copy(piece.at[:, cols], target, right_sem.at[j, i]))
            at += depth
        return copies

    def store(j):
        if len(out_hbm.shape) == 2:
            target = out_hbm.at[:, pl.ds(pl.multiple_of(j * bn, bn), bn)]
        else:
            target = out_hbm.at[j]
        return pltpu.make_async_copy(out.at[j], target, out_sem.at[j])

    def each(count, act):
        def step(i, carry):
            act(i)
            return carry

        lax.fori_loop(0, count, step, 0)

    each(PARTS, lambda q: fetch_left(q).start())
    each(steps, lambda j: [copy.start() for copy in fetch(j)])
    each(PARTS, lambda q: fetch_left(q).wait())

    def multiply(j):
        for copy in fetch(j):
            copy.wait()

        total = jnp.dot(left[...], right[j], preferred_element_type=jnp.float32)
        out[j] = (acc[j] + total).astype(out.dtype)
        store(j).start()

    each(steps, multiply)
    each(steps, lambda j: store(j).wait())


def add_product(late, place, pieces, acc, last):
    steps, rows, bn = acc.shape
    depths = [piece.shape[0] for piece in pieces]
    inner = sum(depths)
    anywhere = pl.BlockSpec(memory_space=pl.ANY)
    if last:
        out_shape = jax.ShapeDtypeStruct((rows, steps * bn), jnp.bfloat16)
    else:
        out_shape = jax.ShapeDtypeStruct(acc.shape, acc.dtype)
    return pl.pallas_call(
        functools.partial(add_kernel, depths, place),
        out_shape=out_shape,
        in_specs=[anywhere] * (2 + len(pieces)),
        out_specs=anywhere,
        scratch_shapes=[
            pltpu.VMEM((rows, inner), jnp.bfloat16),
            pltpu.VMEM((steps, inner, bn), jnp.bfloat16),
            pltpu.VMEM((steps, rows, bn), jnp.float32),
            pltpu.VMEM((steps, rows, bn), out_shape.dtype),
            pltpu.SemaphoreType.DMA((PARTS,)),
            pltpu.SemaphoreType.DMA((steps, len(pieces))),
            pltpu.SemaphoreType.DMA((steps,)),
            pltpu.SemaphoreType.DMA((steps,)),
        ],
        compiler_params=pltpu.CompilerParams(
            vmem_limit_bytes=ADD_BYTES
        ),
        cost_estimate=pl.CostEstimate(
            flops=2 * rows * inner * steps * bn,
            bytes_accessed=(rows + steps * bn) * inner * 2 + rows * steps * bn * 8,
            transcendentals=0,
        ),
    )(late, acc, *pieces)


def across_row(landed, columns):
    if columns != 4:
        gathered = lax.all_gather(landed, "blk", axis=0)
        return [gathered[j] for j in range(columns)]
    swap_core = [(j, j ^ 1) for j in range(columns)]
    swap_chip = [(j, j ^ 2) for j in range(columns)]
    across = lax.ppermute(landed, "blk", swap_chip)
    near = lax.ppermute(landed, "blk", swap_core)
    return [landed, across, near, lax.ppermute(across, "blk", swap_core)]


def body(a_slots, a_rows, a_cols, a_count, owned_rows, b_matrix):
    groups = lax.axis_size("grid")
    columns = lax.axis_size("blk")
    bs = a_slots.shape[-1]
    cap = a_slots.shape[3]
    rb = owned_rows.shape[-1]
    k_local, n_local = b_matrix.shape
    blocks = k_local // bs
    half = groups // 2

    order = ring_order(groups)
    to_right = [(order[i], order[(i + 1) % groups]) for i in range(groups)]
    to_left = [(order[(i + 1) % groups], order[i]) for i in range(groups)]
    from_left, from_right, early = b_matrix, b_matrix, [b_matrix]
    for s in range(1, half - 1):
        from_left = lax.ppermute(from_left, "grid", to_right)
        from_right = lax.ppermute(from_right, "grid", to_left)
        early += [from_left, from_right]
    split = k_local // 2
    left_low, right_high = from_left[:split], from_right[split:]
    left_high, right_low = from_left[split:], from_right[:split]
    left_low = lax.ppermute(left_low, "grid", to_right)
    right_high = lax.ppermute(right_high, "grid", to_left)
    left_high = lax.ppermute(left_high, "grid", to_right)
    right_low = lax.ppermute(right_low, "grid", to_left)

    live = jnp.arange(cap, dtype=jnp.int32)[None, :] < a_count.reshape(groups, 1)
    row_code = jnp.where(live, a_rows.reshape(groups, cap) + 1, 0)
    meta = jnp.concatenate([row_code, a_cols.reshape(groups, cap)], axis=1)
    meta = jnp.pad(meta.astype(jnp.bfloat16)[:, None, :], ((0, 0), (0, META - 1), (0, bs - 2 * cap)))
    message = pack(a_slots.reshape(groups, cap * bs, bs), meta)
    landed = lax.all_to_all(message, "grid", split_axis=0, concat_axis=0, tiled=True)
    (landed,) = after([landed], early[1:3], VMEM_BYTES)
    parts = across_row(landed, columns)

    metas = jnp.stack([p[:, cap * bs, : 2 * cap] for p in parts]).astype(jnp.int32)
    code, col = metas[..., :cap], metas[..., cap:]
    hit = code[..., None] == owned_rows.reshape(rb) + 1
    row = jnp.sum(jnp.where(hit, jnp.arange(rb, dtype=jnp.int32), 0), axis=-1)
    pos = ring_place(lax.axis_index("grid"), groups)
    ahead = (ring_place(col // blocks, groups) - pos + groups) % groups
    hops = jnp.minimum(ahead, groups - ahead)
    first = jnp.where(hops == 0, 0, 2 * hops - 1) + jnp.where((ahead > 0) & (ahead < half), 1, 0)
    dest = row * (blocks * groups) + first * blocks + col % blocks
    dest = jnp.where(jnp.any(hit, axis=-1), dest, -1)

    acc, late, mark = first_product(dest, parts, early, rb * bs, 3 * k_local, bs, cap, n_local // 4)
    left_low, right_high = after([left_low, right_high], [mark], SPARE_BYTES)
    low = lax.ppermute(left_low, "grid", to_right)
    high = lax.ppermute(right_high, "grid", to_left)
    acc = add_product(late, 0, [left_low, left_high, right_low, right_high], acc, False)
    return add_product(late, 2 * k_local, [low, high], acc, True)


def solution(mesh):
    in_specs = (
        P("grid", "blk", None, None, None, None),
        P("grid", "blk", None, None),
        P("grid", "blk", None, None),
        P("grid", "blk", None),
        P("grid", None),
        P("grid", "blk"),
    )
    out_specs = P("grid", "blk")
    return jax.shard_map(body, mesh=mesh, in_specs=in_specs, out_specs=out_specs, check_vma=False)
```

```python
import functools

import jax
import jax.numpy as jnp
from jax import lax
from jax.experimental import pallas as pl
from jax.experimental.pallas import tpu as pltpu
from jax.sharding import PartitionSpec as P

META = 16
PARTS = 4
CLEAR = 32
VMEM_BYTES = 62 << 20
FIRST_BYTES = 26 << 20
ADD_BYTES = 18 << 20
LARGE = 4 << 20
SPARE_BYTES = 4 << 20


def ring_order(n):
    return list(range(0, n, 2)) + list(range(n - 1, 0, -2))


def ring_place(g, n):
    return jnp.where(g % 2 == 0, g // 2, n - 1 - g // 2)


def pack_kernel(slots_ref, meta_ref, message_ref):
    rows = slots_ref.shape[1]
    message_ref[:, :rows] = slots_ref[...]
    message_ref[:, rows:] = meta_ref[...]


def pack(slots, meta):
    groups, rows, width = slots.shape
    part = groups // 4
    return pl.pallas_call(
        pack_kernel,
        out_shape=jax.ShapeDtypeStruct((groups, rows + META, width), slots.dtype),
        grid=(groups // part,),
        in_specs=[
            pl.BlockSpec((part, rows, width), lambda i: (i, 0, 0)),
            pl.BlockSpec((part, META, width), lambda i: (i, 0, 0)),
        ],
        out_specs=pl.BlockSpec((part, rows + META, width), lambda i: (i, 0, 0)),
        compiler_params=pltpu.CompilerParams(vmem_limit_bytes=VMEM_BYTES),
        cost_estimate=pl.CostEstimate(
            flops=0, bytes_accessed=slots.size * 4, transcendentals=0
        ),
    )(slots, meta)


def after_kernel(*refs):
    pass


def after(values, others, claim):
    anywhere = pl.BlockSpec(memory_space=pl.ANY)
    return pl.pallas_call(
        after_kernel,
        out_shape=[jax.ShapeDtypeStruct(v.shape, v.dtype) for v in values],
        in_specs=[anywhere] * (len(values) + len(others)),
        out_specs=[anywhere] * len(values),
        input_output_aliases={i: i for i in range(len(values))},
        compiler_params=pltpu.CompilerParams(vmem_limit_bytes=claim),
        cost_estimate=pl.CostEstimate(flops=0, bytes_accessed=0, transcendentals=0),
    )(*values, *others)


def first_kernel(depths, per_part, cap, bs, n_parts, dest_ref, *refs):
    parts = refs[:n_parts]
    rights = refs[n_parts : n_parts + len(depths)]
    refs = refs[n_parts + len(depths) :]
    acc_hbm, late_hbm, mark, left, right, acc, held, right_sem, acc_sem, late_sem, part_sem = refs
    mark[...] = jnp.zeros_like(mark)
    inner, bn = right.shape[0], acc.shape[-1]
    part_copies = [
        pltpu.make_async_copy(part, held.at[q], part_sem.at[q]) for q, part in enumerate(parts)
    ]
    for copy in part_copies:
        copy.start()
    at, fetches = 0, []
    for i, (depth, source) in enumerate(zip(depths, rights)):
        fetches.append(
            pltpu.make_async_copy(source, right.at[pl.ds(at, depth)], right_sem.at[i])
        )
        at += depth
    for fetch in fetches:
        fetch.start()
    some = left.shape[0] // PARTS

    def clear(i, carry):
        rows = pl.ds(pl.multiple_of(i * CLEAR, CLEAR), CLEAR)
        left[rows] = jnp.zeros((CLEAR, left.shape[1]), left.dtype)
        return carry

    lax.fori_loop(0, left.shape[0] // CLEAR, clear, 0)
    k_blocks = left.shape[1] // bs
    for q in range(n_parts):
        part_copies[q].wait()

        def place(i, carry):
            for c in range(cap):
                dest = dest_ref[q, i, c]

                @pl.when(dest >= 0)
                def _():
                    row, col = dest // k_blocks, dest % k_blocks
                    left[
                        pl.ds(pl.multiple_of(row * bs, bs), bs),
                        pl.ds(pl.multiple_of(col * bs, bs), bs),
                    ] = held[q, i, pl.ds(c * bs, bs), :]

            return carry

        lax.fori_loop(0, per_part, place, 0)
    stores = [
        pltpu.make_async_copy(
            left.at[pl.ds(q * some, some), pl.ds(inner, late_hbm.shape[1])],
            late_hbm.at[pl.ds(q * some, some)],
            late_sem.at[q],
        )
        for q in range(PARTS)
    ]
    for store in stores:
        store.start()
    for fetch in fetches:
        fetch.wait()

    def multiply(j, carry):
        cols = pl.ds(pl.multiple_of(j * bn, bn), bn)
        acc[j] = jnp.dot(left[:, :inner], right[:, cols], preferred_element_type=jnp.float32)
        pltpu.make_async_copy(acc.at[j], acc_hbm.at[j], acc_sem.at[j]).start()
        return carry

    lax.fori_loop(0, acc.shape[0], multiply, 0)
    for j in range(acc.shape[0]):
        pltpu.make_async_copy(acc.at[j], acc_hbm.at[j], acc_sem.at[j]).wait()
    for store in stores:
        store.wait()


def first_product(dest, parts, rights, rows, late_width, bs, cap, bn):
    depths = [right.shape[0] for right in rights]
    cols = rights[0].shape[1]
    inner, steps = sum(depths), cols // bn
    anywhere = pl.BlockSpec(memory_space=pl.ANY)
    return pl.pallas_call(
        functools.partial(first_kernel, depths, parts[0].shape[0], cap, bs, len(parts)),
        out_shape=[
            jax.ShapeDtypeStruct((steps, rows, bn), jnp.float32),
            jax.ShapeDtypeStruct((rows, late_width), jnp.bfloat16),
            jax.ShapeDtypeStruct((8, bs), jnp.float32),
        ],
        in_specs=[pl.BlockSpec(memory_space=pltpu.SMEM)]
        + [pl.BlockSpec(memory_space=pltpu.HBM)] * (len(parts) + len(rights)),
        out_specs=[anywhere] * 2 + [pl.BlockSpec(memory_space=pltpu.VMEM)],
        scratch_shapes=[
            pltpu.VMEM((rows, inner + late_width), jnp.bfloat16),
            pltpu.VMEM((inner, cols), jnp.bfloat16),
            pltpu.VMEM((steps, rows, bn), jnp.float32),
            pltpu.VMEM((len(parts),) + parts[0].shape, parts[0].dtype),
            pltpu.SemaphoreType.DMA((len(rights),)),
            pltpu.SemaphoreType.DMA((steps,)),
            pltpu.SemaphoreType.DMA((PARTS,)),
            pltpu.SemaphoreType.DMA((len(parts),)),
        ],
        compiler_params=pltpu.CompilerParams(vmem_limit_bytes=FIRST_BYTES if cols * inner < LARGE else VMEM_BYTES),
        cost_estimate=pl.CostEstimate(
            flops=2 * rows * inner * cols,
            bytes_accessed=inner * cols * 2 + rows * cols * 4,
            transcendentals=0,
        ),
    )(dest, *parts, *rights)


def add_kernel(depths, place, late_hbm, acc_hbm, *refs):
    pieces = refs[: len(depths)]
    out_hbm, left, right, acc, out, left_sem, right_sem, acc_sem, out_sem = refs[len(depths) :]
    steps, rows, bn = acc.shape
    inner = left.shape[1]
    some = rows // PARTS

    def fetch_left(q):
        part = pl.ds(pl.multiple_of(q * some, some), some)
        source = late_hbm.at[part, pl.ds(place, inner)]
        return pltpu.make_async_copy(source, left.at[part], left_sem.at[q])

    def fetch(j):
        cols = pl.ds(pl.multiple_of(j * bn, bn), bn)
        copies, at = [pltpu.make_async_copy(acc_hbm.at[j], acc.at[j], acc_sem.at[j])], 0
        for i, (depth, piece) in enumerate(zip(depths, pieces)):
            target = right.at[j, pl.ds(at, depth)]
            copies.append(pltpu.make_async_copy(piece.at[:, cols], target, right_sem.at[j, i]))
            at += depth
        return copies

    def store(j):
        if len(out_hbm.shape) == 2:
            target = out_hbm.at[:, pl.ds(pl.multiple_of(j * bn, bn), bn)]
        else:
            target = out_hbm.at[j]
        return pltpu.make_async_copy(out.at[j], target, out_sem.at[j])

    def each(count, act):
        def step(i, carry):
            act(i)
            return carry

        lax.fori_loop(0, count, step, 0)

    each(PARTS, lambda q: fetch_left(q).start())
    each(steps, lambda j: [copy.start() for copy in fetch(j)])
    each(PARTS, lambda q: fetch_left(q).wait())

    def multiply(j):
        for copy in fetch(j):
            copy.wait()

        total = jnp.dot(left[...], right[j], preferred_element_type=jnp.float32)
        out[j] = (acc[j] + total).astype(out.dtype)
        store(j).start()

    each(steps, multiply)
    each(steps, lambda j: store(j).wait())


def add_product(late, place, pieces, acc, last):
    steps, rows, bn = acc.shape
    depths = [piece.shape[0] for piece in pieces]
    inner = sum(depths)
    anywhere = pl.BlockSpec(memory_space=pl.ANY)
    if last:
        out_shape = jax.ShapeDtypeStruct((rows, steps * bn), jnp.bfloat16)
    else:
        out_shape = jax.ShapeDtypeStruct(acc.shape, acc.dtype)
    return pl.pallas_call(
        functools.partial(add_kernel, depths, place),
        out_shape=out_shape,
        in_specs=[anywhere] * (2 + len(pieces)),
        out_specs=anywhere,
        scratch_shapes=[
            pltpu.VMEM((rows, inner), jnp.bfloat16),
            pltpu.VMEM((steps, inner, bn), jnp.bfloat16),
            pltpu.VMEM((steps, rows, bn), jnp.float32),
            pltpu.VMEM((steps, rows, bn), out_shape.dtype),
            pltpu.SemaphoreType.DMA((PARTS,)),
            pltpu.SemaphoreType.DMA((steps, len(pieces))),
            pltpu.SemaphoreType.DMA((steps,)),
            pltpu.SemaphoreType.DMA((steps,)),
        ],
        compiler_params=pltpu.CompilerParams(
            vmem_limit_bytes=ADD_BYTES
        ),
        cost_estimate=pl.CostEstimate(
            flops=2 * rows * inner * steps * bn,
            bytes_accessed=(rows + steps * bn) * inner * 2 + rows * steps * bn * 8,
            transcendentals=0,
        ),
    )(late, acc, *pieces)


def across_row(landed, columns):
    if columns != 4:
        gathered = lax.all_gather(landed, "blk", axis=0)
        return [gathered[j] for j in range(columns)]
    swap_core = [(j, j ^ 1) for j in range(columns)]
    swap_chip = [(j, j ^ 2) for j in range(columns)]
    across = lax.ppermute(landed, "blk", swap_chip)
    near = lax.ppermute(landed, "blk", swap_core)
    return [landed, across, near, lax.ppermute(across, "blk", swap_core)]


def body(a_slots, a_rows, a_cols, a_count, owned_rows, b_matrix):
    groups = lax.axis_size("grid")
    columns = lax.axis_size("blk")
    bs = a_slots.shape[-1]
    cap = a_slots.shape[3]
    rb = owned_rows.shape[-1]
    k_local, n_local = b_matrix.shape
    blocks = k_local // bs
    half = groups // 2

    order = ring_order(groups)
    to_right = [(order[i], order[(i + 1) % groups]) for i in range(groups)]
    to_left = [(order[(i + 1) % groups], order[i]) for i in range(groups)]
    from_left, from_right, early = b_matrix, b_matrix, [b_matrix]
    for s in range(1, half - 1):
        from_left = lax.ppermute(from_left, "grid", to_right)
        from_right = lax.ppermute(from_right, "grid", to_left)
        early += [from_left, from_right]
    split = k_local // 16 * 9
    left_low, right_high = from_left[:split], from_right[split:]
    left_high, right_low = from_left[split:], from_right[:split]
    left_low = lax.ppermute(left_low, "grid", to_right)
    right_high = lax.ppermute(right_high, "grid", to_left)
    left_high = lax.ppermute(left_high, "grid", to_right)
    right_low = lax.ppermute(right_low, "grid", to_left)

    live = jnp.arange(cap, dtype=jnp.int32)[None, :] < a_count.reshape(groups, 1)
    row_code = jnp.where(live, a_rows.reshape(groups, cap) + 1, 0)
    meta = jnp.concatenate([row_code, a_cols.reshape(groups, cap)], axis=1)
    meta = jnp.pad(meta.astype(jnp.bfloat16)[:, None, :], ((0, 0), (0, META - 1), (0, bs - 2 * cap)))
    message = pack(a_slots.reshape(groups, cap * bs, bs), meta)
    landed = lax.all_to_all(message, "grid", split_axis=0, concat_axis=0, tiled=True)
    (landed,) = after([landed], early[1:3], VMEM_BYTES)
    parts = across_row(landed, columns)

    metas = jnp.stack([p[:, cap * bs, : 2 * cap] for p in parts]).astype(jnp.int32)
    code, col = metas[..., :cap], metas[..., cap:]
    hit = code[..., None] == owned_rows.reshape(rb) + 1
    row = jnp.sum(jnp.where(hit, jnp.arange(rb, dtype=jnp.int32), 0), axis=-1)
    pos = ring_place(lax.axis_index("grid"), groups)
    ahead = (ring_place(col // blocks, groups) - pos + groups) % groups
    hops = jnp.minimum(ahead, groups - ahead)
    first = jnp.where(hops == 0, 0, 2 * hops - 1) + jnp.where((ahead > 0) & (ahead < half), 1, 0)
    dest = row * (blocks * groups) + first * blocks + col % blocks
    dest = jnp.where(jnp.any(hit, axis=-1), dest, -1)

    acc, late, mark = first_product(dest, parts, early, rb * bs, 3 * k_local, bs, cap, n_local // 4)
    left_low, right_high = after([left_low, right_high], [mark], SPARE_BYTES)
    low = lax.ppermute(left_low, "grid", to_right)
    high = lax.ppermute(right_high, "grid", to_left)
    acc = add_product(late, 0, [left_low, left_high, right_low, right_high], acc, False)
    return add_product(late, 2 * k_local, [low, high], acc, True)


def solution(mesh):
    in_specs = (
        P("grid", "blk", None, None, None, None),
        P("grid", "blk", None, None),
        P("grid", "blk", None, None),
        P("grid", "blk", None),
        P("grid", None),
        P("grid", "blk"),
    )
    out_specs = P("grid", "blk")
    return jax.shard_map(body, mesh=mesh, in_specs=in_specs, out_specs=out_specs, check_vma=False)
```

```python
import functools

import jax
import jax.numpy as jnp
from jax import lax
from jax.experimental import pallas as pl
from jax.experimental.pallas import tpu as pltpu
from jax.sharding import PartitionSpec as P

META = 16
PARTS = 4
CLEAR = 32
VMEM_BYTES = 62 << 20
FIRST_BYTES = 26 << 20
ADD_BYTES = 18 << 20
LARGE = 4 << 20
SPARE_BYTES = 4 << 20


def ring_order(n):
    return list(range(0, n, 2)) + list(range(n - 1, 0, -2))


def ring_place(g, n):
    return jnp.where(g % 2 == 0, g // 2, n - 1 - g // 2)


def pack_kernel(slots_ref, meta_ref, message_ref):
    rows = slots_ref.shape[1]
    message_ref[:, :rows] = slots_ref[...]
    message_ref[:, rows:] = meta_ref[...]


def pack(slots, meta):
    groups, rows, width = slots.shape
    part = groups // 4
    return pl.pallas_call(
        pack_kernel,
        out_shape=jax.ShapeDtypeStruct((groups, rows + META, width), slots.dtype),
        grid=(groups // part,),
        in_specs=[
            pl.BlockSpec((part, rows, width), lambda i: (i, 0, 0)),
            pl.BlockSpec((part, META, width), lambda i: (i, 0, 0)),
        ],
        out_specs=pl.BlockSpec((part, rows + META, width), lambda i: (i, 0, 0)),
        compiler_params=pltpu.CompilerParams(vmem_limit_bytes=VMEM_BYTES),
        cost_estimate=pl.CostEstimate(
            flops=0, bytes_accessed=slots.size * 4, transcendentals=0
        ),
    )(slots, meta)


def after_kernel(*refs):
    pass


def after(values, others, claim):
    anywhere = pl.BlockSpec(memory_space=pl.ANY)
    return pl.pallas_call(
        after_kernel,
        out_shape=[jax.ShapeDtypeStruct(v.shape, v.dtype) for v in values],
        in_specs=[anywhere] * (len(values) + len(others)),
        out_specs=[anywhere] * len(values),
        input_output_aliases={i: i for i in range(len(values))},
        compiler_params=pltpu.CompilerParams(vmem_limit_bytes=claim),
        cost_estimate=pl.CostEstimate(flops=0, bytes_accessed=0, transcendentals=0),
    )(*values, *others)


def first_kernel(depths, per_part, cap, bs, n_parts, dest_ref, *refs):
    parts = refs[:n_parts]
    rights = refs[n_parts : n_parts + len(depths)]
    refs = refs[n_parts + len(depths) :]
    acc_hbm, late_hbm, mark, left, right, acc, held, right_sem, acc_sem, late_sem, part_sem = refs
    mark[...] = jnp.zeros_like(mark)
    inner, bn = right.shape[0], acc.shape[-1]
    part_copies = [
        pltpu.make_async_copy(part, held.at[q], part_sem.at[q]) for q, part in enumerate(parts)
    ]
    for copy in part_copies:
        copy.start()
    at, fetches = 0, []
    for i, (depth, source) in enumerate(zip(depths, rights)):
        fetches.append(
            pltpu.make_async_copy(source, right.at[pl.ds(at, depth)], right_sem.at[i])
        )
        at += depth
    for fetch in fetches:
        fetch.start()
    some = left.shape[0] // PARTS

    def clear(i, carry):
        rows = pl.ds(pl.multiple_of(i * CLEAR, CLEAR), CLEAR)
        left[rows] = jnp.zeros((CLEAR, left.shape[1]), left.dtype)
        return carry

    lax.fori_loop(0, left.shape[0] // CLEAR, clear, 0)
    k_blocks = left.shape[1] // bs
    for q in range(n_parts):
        part_copies[q].wait()

        def place(i, carry):
            for c in range(cap):
                dest = dest_ref[q, i, c]

                @pl.when(dest >= 0)
                def _():
                    row, col = dest // k_blocks, dest % k_blocks
                    left[
                        pl.ds(pl.multiple_of(row * bs, bs), bs),
                        pl.ds(pl.multiple_of(col * bs, bs), bs),
                    ] = held[q, i, pl.ds(c * bs, bs), :]

            return carry

        lax.fori_loop(0, per_part, place, 0)
    stores = [
        pltpu.make_async_copy(
            left.at[pl.ds(q * some, some), pl.ds(inner, late_hbm.shape[1])],
            late_hbm.at[pl.ds(q * some, some)],
            late_sem.at[q],
        )
        for q in range(PARTS)
    ]
    for store in stores:
        store.start()
    for fetch in fetches:
        fetch.wait()

    def multiply(j, carry):
        cols = pl.ds(pl.multiple_of(j * bn, bn), bn)
        acc[j] = jnp.dot(left[:, :inner], right[:, cols], preferred_element_type=jnp.float32)
        pltpu.make_async_copy(acc.at[j], acc_hbm.at[j], acc_sem.at[j]).start()
        return carry

    lax.fori_loop(0, acc.shape[0], multiply, 0)
    for j in range(acc.shape[0]):
        pltpu.make_async_copy(acc.at[j], acc_hbm.at[j], acc_sem.at[j]).wait()
    for store in stores:
        store.wait()


def first_product(dest, parts, rights, rows, late_width, bs, cap, bn):
    depths = [right.shape[0] for right in rights]
    cols = rights[0].shape[1]
    inner, steps = sum(depths), cols // bn
    anywhere = pl.BlockSpec(memory_space=pl.ANY)
    return pl.pallas_call(
        functools.partial(first_kernel, depths, parts[0].shape[0], cap, bs, len(parts)),
        out_shape=[
            jax.ShapeDtypeStruct((steps, rows, bn), jnp.float32),
            jax.ShapeDtypeStruct((rows, late_width), jnp.bfloat16),
            jax.ShapeDtypeStruct((8, bs), jnp.float32),
        ],
        in_specs=[pl.BlockSpec(memory_space=pltpu.SMEM)]
        + [pl.BlockSpec(memory_space=pltpu.HBM)] * (len(parts) + len(rights)),
        out_specs=[anywhere] * 2 + [pl.BlockSpec(memory_space=pltpu.VMEM)],
        scratch_shapes=[
            pltpu.VMEM((rows, inner + late_width), jnp.bfloat16),
            pltpu.VMEM((inner, cols), jnp.bfloat16),
            pltpu.VMEM((steps, rows, bn), jnp.float32),
            pltpu.VMEM((len(parts),) + parts[0].shape, parts[0].dtype),
            pltpu.SemaphoreType.DMA((len(rights),)),
            pltpu.SemaphoreType.DMA((steps,)),
            pltpu.SemaphoreType.DMA((PARTS,)),
            pltpu.SemaphoreType.DMA((len(parts),)),
        ],
        compiler_params=pltpu.CompilerParams(vmem_limit_bytes=FIRST_BYTES if cols * inner < LARGE else VMEM_BYTES),
        cost_estimate=pl.CostEstimate(
            flops=2 * rows * inner * cols,
            bytes_accessed=inner * cols * 2 + rows * cols * 4,
            transcendentals=0,
        ),
    )(dest, *parts, *rights)


def add_kernel(depths, place, late_hbm, acc_hbm, *refs):
    pieces = refs[: len(depths)]
    out_hbm, left, right, acc, out, left_sem, right_sem, acc_sem, out_sem = refs[len(depths) :]
    steps, rows, bn = acc.shape
    inner = left.shape[1]
    some = rows // PARTS

    def fetch_left(q):
        part = pl.ds(pl.multiple_of(q * some, some), some)
        source = late_hbm.at[part, pl.ds(place, inner)]
        return pltpu.make_async_copy(source, left.at[part], left_sem.at[q])

    def fetch(j):
        cols = pl.ds(pl.multiple_of(j * bn, bn), bn)
        copies, at = [pltpu.make_async_copy(acc_hbm.at[j], acc.at[j], acc_sem.at[j])], 0
        for i, (depth, piece) in enumerate(zip(depths, pieces)):
            target = right.at[j, pl.ds(at, depth)]
            copies.append(pltpu.make_async_copy(piece.at[:, cols], target, right_sem.at[j, i]))
            at += depth
        return copies

    def store(j):
        if len(out_hbm.shape) == 2:
            target = out_hbm.at[:, pl.ds(pl.multiple_of(j * bn, bn), bn)]
        else:
            target = out_hbm.at[j]
        return pltpu.make_async_copy(out.at[j], target, out_sem.at[j])

    def each(count, act):
        def step(i, carry):
            act(i)
            return carry

        lax.fori_loop(0, count, step, 0)

    each(PARTS, lambda q: fetch_left(q).start())
    each(steps, lambda j: [copy.start() for copy in fetch(j)])
    each(PARTS, lambda q: fetch_left(q).wait())

    def multiply(j):
        for copy in fetch(j):
            copy.wait()

        total = jnp.dot(left[...], right[j], preferred_element_type=jnp.float32)
        out[j] = (acc[j] + total).astype(out.dtype)
        store(j).start()

    each(steps, multiply)
    each(steps, lambda j: store(j).wait())


def add_product(late, place, pieces, acc, last):
    steps, rows, bn = acc.shape
    depths = [piece.shape[0] for piece in pieces]
    inner = sum(depths)
    anywhere = pl.BlockSpec(memory_space=pl.ANY)
    if last:
        out_shape = jax.ShapeDtypeStruct((rows, steps * bn), jnp.bfloat16)
    else:
        out_shape = jax.ShapeDtypeStruct(acc.shape, acc.dtype)
    return pl.pallas_call(
        functools.partial(add_kernel, depths, place),
        out_shape=out_shape,
        in_specs=[anywhere] * (2 + len(pieces)),
        out_specs=anywhere,
        scratch_shapes=[
            pltpu.VMEM((rows, inner), jnp.bfloat16),
            pltpu.VMEM((steps, inner, bn), jnp.bfloat16),
            pltpu.VMEM((steps, rows, bn), jnp.float32),
            pltpu.VMEM((steps, rows, bn), out_shape.dtype),
            pltpu.SemaphoreType.DMA((PARTS,)),
            pltpu.SemaphoreType.DMA((steps, len(pieces))),
            pltpu.SemaphoreType.DMA((steps,)),
            pltpu.SemaphoreType.DMA((steps,)),
        ],
        compiler_params=pltpu.CompilerParams(
            vmem_limit_bytes=ADD_BYTES
        ),
        cost_estimate=pl.CostEstimate(
            flops=2 * rows * inner * steps * bn,
            bytes_accessed=(rows + steps * bn) * inner * 2 + rows * steps * bn * 8,
            transcendentals=0,
        ),
    )(late, acc, *pieces)


def across_row(landed, columns):
    if columns != 4:
        gathered = lax.all_gather(landed, "blk", axis=0)
        return [gathered[j] for j in range(columns)]
    swap_core = [(j, j ^ 1) for j in range(columns)]
    swap_chip = [(j, j ^ 2) for j in range(columns)]
    across = lax.ppermute(landed, "blk", swap_chip)
    near = lax.ppermute(landed, "blk", swap_core)
    return [landed, across, near, lax.ppermute(across, "blk", swap_core)]


def body(a_slots, a_rows, a_cols, a_count, owned_rows, b_matrix):
    groups = lax.axis_size("grid")
    columns = lax.axis_size("blk")
    bs = a_slots.shape[-1]
    cap = a_slots.shape[3]
    rb = owned_rows.shape[-1]
    k_local, n_local = b_matrix.shape
    blocks = k_local // bs
    half = groups // 2

    order = ring_order(groups)
    to_right = [(order[i], order[(i + 1) % groups]) for i in range(groups)]
    to_left = [(order[(i + 1) % groups], order[i]) for i in range(groups)]
    from_left, from_right, early = b_matrix, b_matrix, []
    for s in range(1, half - 1):
        from_left = lax.ppermute(from_left, "grid", to_right)
        from_right = lax.ppermute(from_right, "grid", to_left)
        early += [from_left, from_right]
    split = k_local // 2
    left_low, right_high = from_left[:split], from_right[split:]
    left_high, right_low = from_left[split:], from_right[:split]
    left_low = lax.ppermute(left_low, "grid", to_right)
    right_high = lax.ppermute(right_high, "grid", to_left)
    left_high = lax.ppermute(left_high, "grid", to_right)
    right_low = lax.ppermute(right_low, "grid", to_left)

    live = jnp.arange(cap, dtype=jnp.int32)[None, :] < a_count.reshape(groups, 1)
    row_code = jnp.where(live, a_rows.reshape(groups, cap) + 1, 0)
    meta = jnp.concatenate([row_code, a_cols.reshape(groups, cap)], axis=1)
    meta = jnp.pad(meta.astype(jnp.bfloat16)[:, None, :], ((0, 0), (0, META - 1), (0, bs - 2 * cap)))
    message = pack(a_slots.reshape(groups, cap * bs, bs), meta)
    landed = lax.all_to_all(message, "grid", split_axis=0, concat_axis=0, tiled=True)
    (landed,) = after([landed], early[:2], VMEM_BYTES)
    parts = across_row(landed, columns)

    metas = jnp.stack([p[:, cap * bs, : 2 * cap] for p in parts]).astype(jnp.int32)
    code, col = metas[..., :cap], metas[..., cap:]
    hit = code[..., None] == owned_rows.reshape(rb) + 1
    row = jnp.sum(jnp.where(hit, jnp.arange(rb, dtype=jnp.int32), 0), axis=-1)
    pos = ring_place(lax.axis_index("grid"), groups)
    ahead = (ring_place(col // blocks, groups) - pos + groups) % groups
    hops = jnp.minimum(ahead, groups - ahead)
    first = jnp.where(hops == 0, groups - 2, 2 * hops - 2 + jnp.where(ahead < half, 1, 0))
    first = jnp.where(hops == half, groups - 1, first)
    dest = row * (blocks * groups) + first * blocks + col % blocks
    dest = jnp.where(jnp.any(hit, axis=-1), dest, -1)

    acc, late, mark = first_product(dest, parts, early, rb * bs, 4 * k_local, bs, cap, n_local // 4)
    left_low, right_high = after([left_low, right_high], [mark], SPARE_BYTES)
    low = lax.ppermute(left_low, "grid", to_right)
    high = lax.ppermute(right_high, "grid", to_left)
    pieces = [left_low, left_high, right_low, right_high, b_matrix]
    acc = add_product(late, 0, pieces, acc, False)
    return add_product(late, 3 * k_local, [low, high], acc, True)


def solution(mesh):
    in_specs = (
        P("grid", "blk", None, None, None, None),
        P("grid", "blk", None, None),
        P("grid", "blk", None, None),
        P("grid", "blk", None),
        P("grid", None),
        P("grid", "blk"),
    )
    out_specs = P("grid", "blk")
    return jax.shard_map(body, mesh=mesh, in_specs=in_specs, out_specs=out_specs, check_vma=False)
```
